32 devices in a mesh: patch: 4 (over x, core), line: 2 (over y), layer: 4 (over z).
Axes of the slice: x: 2, y: 2, z: 4, core: 2. Of those that a mesh axis runs over, the one named last changes fastest.
Arguments:
- elastic: float32 [4, 5, 1024, 2048], P('patch', None, 'line', 'layer'), may hold values from -6 to 6
- acoustic: float32 [4, 3, 1024, 2048], P('patch', None, 'line', 'layer'), may hold values from -6 to 6
- el_media: float32 [4, 3, 1024, 2048], P('patch', None, 'line', 'layer'), may hold values from 0.2 to 1.5
- ac_media: float32 [4, 2, 1024, 2048], P('patch', None, 'line', 'layer'), may hold values from 0.2 to 1.5
- cont_matrix: float32 [128, 20], replicated, may hold values from -1.25 to 1.25
- fringe_cells: int32 [4, 2, 4, 4, 256], P('patch', 'line', 'layer'), may hold values from 0 to 262143, as said below
- donor_cells: int32 [4, 2, 4, 4, 4, 256], P('patch', 'line', 'layer'), may hold values from 0 to 262143
- donor_weights: float32 [4, 2, 4, 4, 4, 256], P('patch', 'line', 'layer'), may hold values from 0 to 1, as said below
- donor_counts: int32 [4, 2, 4, 4], P('patch', 'line', 'layer'), may hold values from 0 to 256, as said below
- el_pair: int32 [4, 1024], P('patch', 'line'), may hold values from 0 to 511
- ac_pair: int32 [4, 1024], P('patch', 'line'), may hold values from 0 to 511
Outputs:
- new_elastic: float32 [4, 5, 1024, 2048], P('patch', None, 'line', 'layer')
- new_acoustic: float32 [4, 3, 1024, 2048], P('patch', None, 'line', 'layer')
The draws below stay inside these ranges and needn't reach their ends.
Inputs may be any that keep to these rules, and one draw needn't show every extreme that they name: `fringe_cells`: within one device the 1024 fringe cells are distinct. `donor_weights`: Positive; the four weights of a slot sum to 1. `donor_counts`: 0 where donor and receiver are the same patch; on every device one donor patch fills all 256 slots.
All inputs are finite; a program needn't handle non-finite values.
Results may differ from the reference program's by a relative error of at most 0.0001.
Values sent between devices are 32-bit elements; how exact they have to be, the bound alone decides.
No kernel may reach another device: no remote copies, remote signals or barrier semaphores. Data moves between devices by JAX's collectives and lax.ppermute only.
A program may use at most 512 MiB of HBM per device.

```python
import math
import jax
import jax.numpy as jnp
from jax import lax

NX = 1024
CONT = 128
MATCH = 10
ZD = 512
RCAP = 256
NP = 4
SLABS = 2
LAYERS = 4
XD = 512
NZ = 2048
P_SIZE = 1152
K = 576


def draw_fringe_cells(key, part):
    subkey = jax.random.fold_in(key, 11)
    stride = XD * ZD // (NP * RCAP)
    slots = lax.iota(jnp.int32, NP * RCAP).reshape(NP, RCAP)
    offsets = jax.random.randint(subkey, (NP, SLABS, LAYERS, NP, RCAP), 0, stride)
    return (slots[None, None, None] * stride + offsets).astype(jnp.int32)


def draw_donor_cells(key, part):
    subkey = jax.random.fold_in(key, 12)
    return jax.random.randint(subkey, (NP, SLABS, LAYERS, NP, 4, RCAP), 0, XD * ZD).astype(jnp.int32)


def draw_donor_weights(key, part):
    subkey = jax.random.fold_in(key, 13)
    raw = jax.random.uniform(subkey, (NP, SLABS, LAYERS, NP, 4, RCAP), jnp.float32, 0.1, 1.0)
    total = raw[:, :, :, :, 0] + raw[:, :, :, :, 1] + raw[:, :, :, :, 2] + raw[:, :, :, :, 3]
    return (raw / total[:, :, :, :, None]).astype(jnp.float32)


def draw_donor_counts(key, part):
    subkey = jax.random.fold_in(key, 14)
    first_key, second_key = jax.random.split(subkey)
    offset = jax.random.randint(first_key, (NP, SLABS, LAYERS, 1), 1, NP)
    receiver = lax.iota(jnp.int32, NP).reshape(NP, 1, 1, 1)
    donor = lax.iota(jnp.int32, NP).reshape(1, 1, 1, NP)
    busiest = (receiver + offset) % NP
    light = jax.random.randint(second_key, (NP, SLABS, LAYERS, NP), 1, RCAP // 2 + 1)
    counts = jnp.where(donor == busiest, RCAP, light)
    return jnp.where(donor == receiver, 0, counts).astype(jnp.int32)


def pairing(key, salt):
    subkey = jax.random.fold_in(key, salt)
    local = lax.iota(jnp.int32, NX) % XD
    jitter = jax.random.randint(subkey, (NP, NX), -3, 4)
    return jnp.clip(local[None, :] + jitter, 0, XD - 1).astype(jnp.int32)


def draw_el_pair(key, part):
    return pairing(key, 15)


def draw_ac_pair(key, part):
    return pairing(key, 16)


def block_scale(key, extent, pieces, smallest, top_value):
    level = 1.0
    for dim, parts in pieces:
        draws = jax.random.uniform(jax.random.fold_in(jax.random.fold_in(key, 6), dim), (parts,), jnp.float32, smallest / len(pieces), top_value / len(pieces))
        level = level * jnp.repeat(jnp.exp(draws), extent[dim] // parts).reshape((-1,) + (1,) * (len(extent) - 1 - dim))
    return level


def normal_values(rng, extent, deviation, most, cuts=(), kind=jnp.bfloat16):
    drawn = deviation * jax.random.normal(rng, extent, jnp.float32)
    if cuts:
        drawn = drawn * block_scale(rng, extent, cuts, -0.22, 0.18)
    return jnp.clip(drawn, -most, most).astype(kind)


def setup_inputs(seed: int = 0) -> dict:
    key_of = jax.random.split(jax.random.key(seed), 12)
    elastic = normal_values(key_of[0], (NP, 5, NX, NZ), 1.0, 6.0, ((0, 4), (2, 2), (3, 4)), jnp.float32)
    acoustic = normal_values(key_of[1], (NP, 3, NX, NZ), 1.0, 6.0, ((0, 4), (2, 2), (3, 4)), jnp.float32)
    el_media = jnp.clip(jnp.exp(math.log(1.5) - 2.014903 * jax.random.uniform(key_of[2], (NP, 3, NX, NZ), jnp.float32) ** block_scale(key_of[2], (NP, 3, NX, NZ), ((0, 4), (2, 2), (3, 4)), -0.2, 0.2)), 0.2, 1.5)
    ac_media = jnp.clip(jnp.exp(math.log(1.5) - 2.014903 * jax.random.uniform(key_of[3], (NP, 2, NX, NZ), jnp.float32) ** block_scale(key_of[3], (NP, 2, NX, NZ), ((0, 4), (2, 2), (3, 4)), -0.2, 0.2)), 0.2, 1.5)
    cont_matrix = normal_values(key_of[4], (CONT, 2 * MATCH), (2 * MATCH) ** -0.5, 1.25, (), jnp.float32)
    fringe_cells = draw_fringe_cells(jax.random.fold_in(key_of[11], 71), 0)
    donor_cells = draw_donor_cells(jax.random.fold_in(key_of[11], 71), 0)
    donor_weights = draw_donor_weights(jax.random.fold_in(key_of[11], 71), 0)
    donor_counts = draw_donor_counts(jax.random.fold_in(key_of[11], 71), 0)
    el_pair = draw_el_pair(jax.random.fold_in(key_of[11], 71), 0)
    ac_pair = draw_ac_pair(jax.random.fold_in(key_of[11], 71), 0)
    return {"elastic": elastic, "acoustic": acoustic, "el_media": el_media, "ac_media": ac_media, "cont_matrix": cont_matrix, "fringe_cells": fringe_cells, "donor_cells": donor_cells, "donor_weights": donor_weights, "donor_counts": donor_counts, "el_pair": el_pair, "ac_pair": ac_pair}


step_size = 0.25
penalty = 2.0


def x_derivative(lines, cont_matrix):
    matching = jnp.concatenate([lines[:, NX - MATCH:, :], lines[:, :MATCH, :]], axis=1)
    tail = jnp.einsum("cg,fgz->fcz", cont_matrix, matching, precision=lax.Precision.HIGHEST)
    extended = jnp.concatenate([lines, tail], axis=1)
    spectrum = jnp.fft.rfft(extended, axis=1)
    modes = jnp.arange(K + 1)
    wavenumber = jnp.where(modes < K, modes * (2.0 * math.pi / P_SIZE), 0.0)
    derived = jnp.fft.irfft(spectrum * (1j * wavenumber)[None, :, None], n=P_SIZE, axis=1)
    return derived[:, :NX, :].astype(lines.dtype)


def z_derivative(fields):
    padded = jnp.pad(fields, ((0, 0), (0, 0), (1, 1)))
    return (padded[:, :, 2:] - padded[:, :, :-2]) * 0.5


def overwrite_fringe(new_field, old_field, fringe_cells, donor_cells, donor_weights, donor_counts):
    recv_index = jnp.arange(NP, dtype=jnp.int32).reshape(NP, 1, 1, 1, 1)
    slab_index = jnp.arange(SLABS, dtype=jnp.int32).reshape(1, SLABS, 1, 1, 1)
    layer_index = jnp.arange(LAYERS, dtype=jnp.int32).reshape(1, 1, LAYERS, 1, 1)
    donor_index = jnp.arange(NP, dtype=jnp.int32).reshape(1, 1, 1, NP, 1)
    donor_x = slab_index[..., None] * XD + donor_cells // ZD
    donor_z = layer_index[..., None] * ZD + donor_cells % ZD
    picked = old_field[donor_index[..., None], :, donor_x, donor_z]
    weights = donor_weights[..., None]
    interp = picked[:, :, :, :, 0] * weights[:, :, :, :, 0]
    interp = interp + picked[:, :, :, :, 1] * weights[:, :, :, :, 1]
    interp = interp + picked[:, :, :, :, 2] * weights[:, :, :, :, 2]
    interp = interp + picked[:, :, :, :, 3] * weights[:, :, :, :, 3]
    fringe_x = slab_index * XD + fringe_cells // ZD
    fringe_z = layer_index * ZD + fringe_cells % ZD
    current = new_field[recv_index, :, fringe_x, fringe_z]
    live = jnp.arange(RCAP, dtype=jnp.int32) < donor_counts[..., None]
    chosen = jnp.where(live[..., None], interp, current)
    return new_field.at[recv_index, :, fringe_x, fringe_z].set(chosen)


def reference(elastic, acoustic, el_media, ac_media, cont_matrix, fringe_cells, donor_cells, donor_weights, donor_counts, el_pair, ac_pair):
    slab_start = (jnp.arange(NX, dtype=jnp.int32) // XD) * XD
    basin_list = []
    ocean_list = []
    for patch_index in range(NP):
        basin = elastic[patch_index]
        ocean = acoustic[patch_index]
        dx_basin = x_derivative(jnp.stack([basin[0], basin[1], basin[2], basin[4]]), cont_matrix)
        dx_ocean = x_derivative(ocean[0:2], cont_matrix)
        depth_diff = z_derivative(jnp.stack([basin[0], basin[1], basin[3], basin[4], ocean[0], ocean[2]]))
        buoyancy = el_media[patch_index, 0]
        lame_first = el_media[patch_index, 1]
        shear_modulus = el_media[patch_index, 2]
        stiffness = lame_first + 2.0 * shear_modulus
        rate_vx = buoyancy * (dx_basin[2] + depth_diff[3])
        rate_vz = buoyancy * (dx_basin[3] + depth_diff[2])
        rate_sxx = stiffness * dx_basin[0] + lame_first * depth_diff[1]
        rate_szz = lame_first * dx_basin[0] + stiffness * depth_diff[1]
        rate_sxz = shear_modulus * (depth_diff[0] + dx_basin[1])
        bulk_modulus = ac_media[patch_index, 0]
        ocean_buoyancy = ac_media[patch_index, 1]
        rate_pressure = -bulk_modulus * (dx_ocean[1] + depth_diff[5])
        rate_ocean_vx = -ocean_buoyancy * dx_ocean[0]
        rate_ocean_vz = -ocean_buoyancy * depth_diff[4]
        pressure_pair = ocean[0][slab_start + el_pair[patch_index], NZ - 1]
        rate_szz = rate_szz.at[:, 0].add(penalty * (-pressure_pair - basin[3][:, 0]))
        velocity_pair = basin[1][slab_start + ac_pair[patch_index], 0]
        rate_ocean_vz = rate_ocean_vz.at[:, NZ - 1].add(penalty * (velocity_pair - ocean[2][:, NZ - 1]))
        basin_rates = jnp.stack([rate_vx, rate_vz, rate_sxx, rate_szz, rate_sxz])
        ocean_rates = jnp.stack([rate_pressure, rate_ocean_vx, rate_ocean_vz])
        basin_list.append(basin + step_size * basin_rates)
        ocean_list.append(ocean + step_size * ocean_rates)
    new_elastic = jnp.stack(basin_list)
    new_acoustic = jnp.stack(ocean_list)
    new_elastic = overwrite_fringe(new_elastic, elastic, fringe_cells, donor_cells, donor_weights, donor_counts)
    new_acoustic = overwrite_fringe(new_acoustic, acoustic, fringe_cells, donor_cells, donor_weights, donor_counts)
    return new_elastic, new_acoustic
```

```python
import functools
import math

import jax
import jax.numpy as jnp
import numpy as np
from jax import lax
from jax.experimental import pallas as pl
from jax.experimental.pallas import tpu as pltpu
from jax.sharding import PartitionSpec as P

STEP = 0.25
PENALTY = 2.0
LANES = 128
VMEM_LIMIT = 56 * 1024 * 1024
HIGH = lax.Precision.HIGH
HIGHEST = lax.Precision.HIGHEST


def derivative_row(period):
    n = np.arange(1, period)
    sign = np.where(n % 2 == 0, 1.0, -1.0)
    row = np.zeros(period)
    row[1:] = (math.pi / period) * sign / np.tan(math.pi * n / period)
    return row


def operator_blocks(cont_matrix, rows, slabs, me):
    cont = cont_matrix.shape[0]
    match = cont_matrix.shape[1] // 2
    points = rows * slabs
    period = points + cont
    row = derivative_row(period)
    j = np.arange(rows)
    blocks = np.stack(
        [
            row[(o * rows + j[:, None] - j[None, :]) % period]
            for o in range(-(slabs - 1), slabs)
        ]
    ).astype(np.float32)
    to_tail = np.stack(
        [
            row[(s * rows + j[:, None] - points - np.arange(cont)[None, :]) % period]
            for s in range(slabs)
        ]
    ).astype(np.float32)
    tail_rows = lax.dynamic_index_in_dim(jnp.asarray(to_tail), me, 0, keepdims=False)
    folded = jnp.dot(tail_rows, cont_matrix, precision=HIGHEST)
    on_last = jnp.pad(folded[:, :match], ((0, 0), (rows - match, 0)))
    on_first = jnp.pad(folded[:, match:], ((0, 0), (0, rows - match)))
    table = jnp.asarray(blocks)
    out = []
    for distance in range(slabs):
        source = (me - distance) % slabs
        block = lax.dynamic_index_in_dim(table, me - source + slabs - 1, 0, keepdims=False)
        block = block + jnp.where(source == slabs - 1, on_last, 0.0)
        out.append(block + jnp.where(source == 0, on_first, 0.0))
    return out


def gather_kernel(fields, rows, depth, slots, cells_ref, weights_ref, elastic_ref, acoustic_ref, out_ref, mixed):
    n_el = elastic_ref.shape[1]
    chunks = depth // LANES
    for f in range(fields):
        source = elastic_ref.at[0, f] if f < n_el else acoustic_ref.at[0, f - n_el]
        for c in range(chunks):
            mixed[pl.ds((c * fields + f) * rows, rows), :] = source[:, c * LANES : (c + 1) * LANES]
    lane = lax.broadcasted_iota(jnp.int32, (fields, LANES), 1)
    groups = slots // LANES
    patches = out_ref.shape[0]

    def one_group(step, carry):
        patch, group = step // groups, step % groups

        def one_slot(r, values):
            total = jnp.zeros((fields, LANES), jnp.float32)
            for s in range(4):
                index = (patch * 4 + s) * slots + group * LANES + r
                cell = cells_ref[index]
                x, z = cell // depth, cell % depth
                start = (z // LANES) * (fields * rows) + x
                picked = mixed[pl.ds(start, fields, stride=rows), :]
                total = total + jnp.where(lane == z % LANES, picked * weights_ref[index], 0.0)
            column = jnp.sum(total, axis=1, keepdims=True)
            return jnp.where(lane == r, column, values)

        values = lax.fori_loop(0, LANES, one_slot, jnp.zeros((fields, LANES), jnp.float32), unroll=8)
        out_ref[patch, group] = values
        return carry

    lax.fori_loop(0, patches * groups, one_group, 0)


def base_kernel(
    rows, depth, slots, tile,
    cells_ref, counts_ref, interp_ref, gates_ref,
    d_ref, elastic_ref, acoustic_ref, el_media_ref, ac_media_ref, halo_ref,
    el_pair_ref, ac_pair_ref, ocean_row_ref, basin_row_ref,
    new_el_ref, new_ac_ref, open_ref,
):
    step = pl.program_id(0)
    here = pl.ds(pl.multiple_of(step * tile, tile), tile)
    lane = lax.broadcasted_iota(jnp.int32, (tile, depth), 1)
    operator = d_ref[...]

    def field(ref, f):
        return ref[0, f, here, :]

    def dx(ref, f):
        return jnp.dot(operator, ref[0, f], precision=HIGH, preferred_element_type=jnp.float32)

    def dz(value, slot):
        above = halo_ref[:, slot : slot + 1]
        below = halo_ref[:, 6 + slot : 7 + slot]
        following = jnp.where(lane == depth - 1, below, pltpu.roll(value, depth - 1, 1))
        previous = jnp.where(lane == 0, above, pltpu.roll(value, 1, 1))
        return (following - previous) * 0.5

    vx, vz, sxx, szz, sxz = [field(elastic_ref, f) for f in range(5)]
    p, ovx, ovz = [field(acoustic_ref, f) for f in range(3)]
    buoyancy = el_media_ref[0, 0]
    lame = el_media_ref[0, 1]
    shear = el_media_ref[0, 2]
    stiffness = lame + 2.0 * shear
    bulk = ac_media_ref[0, 0]
    ocean_buoyancy = ac_media_ref[0, 1]

    dx_vx = dx(elastic_ref, 0)
    dz_vz = dz(vz, 1)
    new_el_ref[0, 0, here, :] = vx + STEP * (buoyancy * (dx(elastic_ref, 2) + dz(sxz, 3)))
    new_el_ref[0, 1, here, :] = vz + STEP * (buoyancy * (dx(elastic_ref, 4) + dz(szz, 2)))
    new_el_ref[0, 2, here, :] = sxx + STEP * (stiffness * dx_vx + lame * dz_vz)
    choose = lax.broadcasted_iota(jnp.int32, (tile, rows), 1)
    pressure = jnp.sum(jnp.where(el_pair_ref[...] == choose, ocean_row_ref[...], 0.0), axis=1, keepdims=True)
    velocity = jnp.sum(jnp.where(ac_pair_ref[...] == choose, basin_row_ref[...], 0.0), axis=1, keepdims=True)
    rate_szz = lame * dx_vx + stiffness * dz_vz
    rate_szz = rate_szz + jnp.where(lane == 0, gates_ref[0] * (PENALTY * (-pressure - szz)), 0.0)
    new_el_ref[0, 3, here, :] = szz + STEP * rate_szz
    new_el_ref[0, 4, here, :] = sxz + STEP * (shear * (dz(vx, 0) + dx(elastic_ref, 1)))
    new_ac_ref[0, 0, here, :] = p - STEP * (bulk * (dx(acoustic_ref, 1) + dz(ovz, 5)))
    new_ac_ref[0, 1, here, :] = ovx - STEP * (ocean_buoyancy * dx(acoustic_ref, 0))
    rate_ovz = -ocean_buoyancy * dz(p, 4)
    rate_ovz = rate_ovz + jnp.where(lane == depth - 1, gates_ref[1] * (PENALTY * (velocity - ovz)), 0.0)
    new_ac_ref[0, 2, here, :] = ovz + STEP * rate_ovz
    open_ref[here, :] = jnp.ones((tile, depth), jnp.float32)

    @pl.when(step == pl.num_programs(0) - 1)
    def _():
        row_at = lax.broadcasted_iota(jnp.int32, (8, LANES), 0)
        lane_at = lax.broadcasted_iota(jnp.int32, (8, LANES), 1)
        groups = slots // LANES

        def one_patch(q, carry):
            def one_slot(r, inner):
                cell = cells_ref[q * slots + r]
                x, z = cell // depth, cell % depth
                at_row = pl.ds(pl.multiple_of((x // 8) * 8, 8), 8)
                at_lane = pl.ds(pl.multiple_of((z // LANES) * LANES, LANES), LANES)
                hit = (row_at == x % 8) & (lane_at == z % LANES)
                base = ((q * groups + r // LANES) * 8) * LANES + r % LANES
                for f in range(5):
                    old = new_el_ref[0, f, at_row, at_lane]
                    new_el_ref[0, f, at_row, at_lane] = jnp.where(hit, interp_ref[base + f * LANES], old)
                for f in range(3):
                    old = new_ac_ref[0, f, at_row, at_lane]
                    new_ac_ref[0, f, at_row, at_lane] = jnp.where(hit, interp_ref[base + (5 + f) * LANES], old)
                old = open_ref[at_row, at_lane]
                open_ref[at_row, at_lane] = jnp.where(hit, 0.0, old)
                return inner

            return lax.fori_loop(0, counts_ref[q], one_slot, carry)

        lax.fori_loop(0, counts_ref.shape[0], one_patch, 0)


def far_kernel(coefficients, d_ref, far_ref, media_ref, open_ref, base_ref, out_ref):
    far = jnp.dot(d_ref[...], far_ref[...], precision=HIGH, preferred_element_type=jnp.float32)
    media = [media_ref[0, i] for i in range(media_ref.shape[1])]
    is_open = open_ref[...] > 0.5
    for i, coefficient in enumerate(coefficients):
        old = base_ref[0, i]
        out_ref[0, i] = jnp.where(is_open, old + (STEP * coefficient(*media)) * far, old)


def add_far(base, operator, far, media, first_media, n_media, first_field, coefficients, opened, tile):
    rows, reach = operator.shape
    depth = far.shape[1]
    n_out = len(coefficients)
    return pl.pallas_call(
        functools.partial(far_kernel, coefficients),
        grid=(depth // tile,),
        in_specs=[
            pl.BlockSpec((rows, reach), lambda i: (0, 0)),
            pl.BlockSpec((reach, tile), lambda i: (0, i)),
            pl.BlockSpec((1, n_media, rows, tile), lambda i: (0, first_media // n_media, 0, i)),
            pl.BlockSpec((rows, tile), lambda i: (0, i)),
            pl.BlockSpec((1, n_out, rows, tile), lambda i: (0, first_field // n_out, 0, i)),
        ],
        out_specs=pl.BlockSpec((1, n_out, rows, tile), lambda i: (0, first_field // n_out, 0, i)),
        out_shape=jax.ShapeDtypeStruct(base.shape, base.dtype),
        input_output_aliases={4: 0},
        compiler_params=pltpu.CompilerParams(vmem_limit_bytes=VMEM_LIMIT),
        cost_estimate=pl.CostEstimate(
            flops=6 * rows * reach * depth,
            bytes_accessed=4 * rows * depth * (3 + n_media + n_out),
            transcendentals=0,
        ),
        name="add_far",
    )(operator, far, media, opened, base)


def per_device(
    elastic,
    acoustic,
    el_media,
    ac_media,
    cont_matrix,
    fringe_cells,
    donor_cells,
    donor_weights,
    donor_counts,
    el_pair,
    ac_pair,
):
    rows, depth = elastic.shape[2], elastic.shape[3]
    slabs = lax.axis_size("line")
    layers = lax.axis_size("layer")
    patches = lax.axis_size("patch")
    slots = fringe_cells.shape[-1]
    groups = slots // LANES
    me = lax.axis_index("line")
    layer = lax.axis_index("layer")

    def other_slabs(value):
        parts = [
            lax.ppermute(value, "line", [(i, (i + distance) % slabs) for i in range(slabs)])
            for distance in range(1, slabs)
        ]
        return parts[0] if slabs == 2 else jnp.concatenate(parts, axis=0)

    far = [
        other_slabs(value)
        for value in (elastic[0, 0], elastic[0, 1], elastic[0, 2], elastic[0, 4], acoustic[0, 0], acoustic[0, 1])
    ]

    asked = jnp.concatenate([donor_cells[0, 0, 0].astype(jnp.float32), donor_weights[0, 0, 0]], axis=1)
    asked = lax.all_to_all(asked, "patch", split_axis=0, concat_axis=0, tiled=True)
    asked_cells = asked[:, :4].astype(jnp.int32).reshape(-1)
    asked_weights = asked[:, 4:].reshape(-1)

    smem = pl.BlockSpec(memory_space=pltpu.SMEM)
    vmem = pl.BlockSpec(memory_space=pltpu.VMEM)
    local = pl.pallas_call(
        functools.partial(gather_kernel, 8, rows, depth, slots),
        in_specs=[smem, smem, vmem, vmem],
        out_specs=vmem,
        out_shape=jax.ShapeDtypeStruct((patches, groups, 8, LANES), jnp.float32),
        scratch_shapes=[pltpu.VMEM((8 * rows * (depth // LANES), LANES), jnp.float32)],
        compiler_params=pltpu.CompilerParams(vmem_limit_bytes=VMEM_LIMIT),
        cost_estimate=pl.CostEstimate(flops=10**9, bytes_accessed=32 * rows * depth, transcendentals=0),
        name="donor_gather",
    )(asked_cells, asked_weights, elastic, acoustic)
    interp = lax.all_to_all(local, "patch", split_axis=0, concat_axis=0, tiled=True).reshape(-1)

    depth_in = [elastic[0, 0], elastic[0, 1], elastic[0, 3], elastic[0, 4], acoustic[0, 0], acoustic[0, 2]]
    top_cells = jnp.stack([value[:, 0] for value in depth_in])
    bottom_cells = jnp.stack([value[:, depth - 1] for value in depth_in])
    from_above = lax.ppermute(bottom_cells, "layer", [(i, (i + 1) % layers) for i in range(layers)])
    from_below = lax.ppermute(top_cells, "layer", [(i, (i - 1) % layers) for i in range(layers)])
    at_top, at_bottom = layer == 0, layer == layers - 1
    ocean_row = from_above[4:5]
    basin_row = from_below[1:2]
    halo = jnp.concatenate([jnp.where(at_top, 0.0, from_above), jnp.where(at_bottom, 0.0, from_below)]).T
    gates = jnp.stack([at_top, at_bottom]).astype(jnp.float32)

    blocks = operator_blocks(cont_matrix, rows, slabs, me)
    far_operator = blocks[1] if slabs == 2 else jnp.concatenate(blocks[1:], axis=1)

    tile = min(64, rows)
    new_el, new_ac, opened = pl.pallas_call(
        functools.partial(base_kernel, rows, depth, slots, tile),
        grid=(rows // tile,),
        in_specs=[
            smem,
            smem,
            smem,
            smem,
            pl.BlockSpec((tile, rows), lambda i: (i, 0)),
            vmem,
            vmem,
            pl.BlockSpec((1, 3, tile, depth), lambda i: (0, 0, i, 0)),
            pl.BlockSpec((1, 2, tile, depth), lambda i: (0, 0, i, 0)),
            pl.BlockSpec((tile, 12), lambda i: (i, 0)),
            pl.BlockSpec((tile, 1), lambda i: (i, 0)),
            pl.BlockSpec((tile, 1), lambda i: (i, 0)),
            vmem,
            vmem,
        ],
        out_specs=[vmem, vmem, vmem],
        out_shape=[
            jax.ShapeDtypeStruct(elastic.shape, jnp.float32),
            jax.ShapeDtypeStruct(acoustic.shape, jnp.float32),
            jax.ShapeDtypeStruct((rows, depth), jnp.float32),
        ],
        compiler_params=pltpu.CompilerParams(vmem_limit_bytes=VMEM_LIMIT),
        cost_estimate=pl.CostEstimate(
            flops=36 * rows * rows * depth, bytes_accessed=88 * rows * depth, transcendentals=0
        ),
        name="near_section",
    )(
        fringe_cells[0, 0, 0].reshape(-1),
        donor_counts[0, 0, 0],
        interp,
        gates,
        blocks[0],
        elastic,
        acoustic,
        el_media,
        ac_media,
        halo,
        el_pair[0][:, None],
        ac_pair[0][:, None],
        ocean_row,
        basin_row,
    )

    far_tile = min(256, depth)
    new_el = add_far(
        new_el, far_operator, far[0], el_media, 0, 3, 2,
        (lambda b, l, m: l + 2.0 * m, lambda b, l, m: l), opened, far_tile,
    )
    new_el = add_far(new_el, far_operator, far[1], el_media, 2, 1, 4, (lambda m: m,), opened, far_tile)
    new_el = add_far(new_el, far_operator, far[2], el_media, 0, 1, 0, (lambda b: b,), opened, far_tile)
    new_el = add_far(new_el, far_operator, far[3], el_media, 0, 1, 1, (lambda b: b,), opened, far_tile)
    new_ac = add_far(new_ac, far_operator, far[4], ac_media, 1, 1, 1, (lambda b: -b,), opened, far_tile)
    new_ac = add_far(new_ac, far_operator, far[5], ac_media, 0, 1, 0, (lambda k: -k,), opened, far_tile)
    return new_el, new_ac


def solution(mesh):
    placed = (
        P("patch", None, "line", "layer"),
        P("patch", None, "line", "layer"),
        P("patch", None, "line", "layer"),
        P("patch", None, "line", "layer"),
        P(),
        P("patch", "line", "layer", None, None),
        P("patch", "line", "layer", None, None, None),
        P("patch", "line", "layer", None, None, None),
        P("patch", "line", "layer", None),
        P("patch", "line"),
        P("patch", "line"),
    )
    return jax.shard_map(
        per_device,
        mesh=mesh,
        in_specs=placed,
        out_specs=(P("patch", None, "line", "layer"), P("patch", None, "line", "layer")),
        check_vma=False,
    )
```

```python
import functools
import math

import jax
import jax.numpy as jnp
import numpy as np
from jax import lax
from jax.experimental import pallas as pl
from jax.experimental.pallas import tpu as pltpu
from jax.sharding import PartitionSpec as P

STEP = 0.25
PENALTY = 2.0
LANES = 128
VMEM_LIMIT = 56 * 1024 * 1024
HIGH = lax.Precision.HIGH
HIGHEST = lax.Precision.HIGHEST


def derivative_row(period):
    n = np.arange(1, period)
    sign = np.where(n % 2 == 0, 1.0, -1.0)
    row = np.zeros(period)
    row[1:] = (math.pi / period) * sign / np.tan(math.pi * n / period)
    return row


def operator_blocks(cont_matrix, rows, slabs, me):
    cont = cont_matrix.shape[0]
    match = cont_matrix.shape[1] // 2
    points = rows * slabs
    period = points + cont
    row = derivative_row(period)
    j = np.arange(rows)
    blocks = np.stack(
        [
            row[(o * rows + j[:, None] - j[None, :]) % period]
            for o in range(-(slabs - 1), slabs)
        ]
    ).astype(np.float32)
    to_tail = np.stack(
        [
            row[(s * rows + j[:, None] - points - np.arange(cont)[None, :]) % period]
            for s in range(slabs)
        ]
    ).astype(np.float32)
    tail_rows = lax.dynamic_index_in_dim(jnp.asarray(to_tail), me, 0, keepdims=False)
    folded = jnp.dot(tail_rows, cont_matrix, precision=HIGHEST)
    on_last = jnp.pad(folded[:, :match], ((0, 0), (rows - match, 0)))
    on_first = jnp.pad(folded[:, match:], ((0, 0), (0, rows - match)))
    table = jnp.asarray(blocks)
    out = []
    for distance in range(slabs):
        source = (me - distance) % slabs
        block = lax.dynamic_index_in_dim(table, me - source + slabs - 1, 0, keepdims=False)
        block = block + jnp.where(source == slabs - 1, on_last, 0.0)
        out.append(block + jnp.where(source == 0, on_first, 0.0))
    return out


def split(value, size):
    if size & (size - 1) == 0:
        return lax.shift_right_logical(value, size.bit_length() - 1), value & (size - 1)
    return lax.div(value, size), lax.rem(value, size)


def take_kernel(in_ref, out_ref):
    out_ref[...] = in_ref[0, 0]


def take_field(fields, index, tile):
    rows, depth = fields.shape[2:]
    return pl.pallas_call(
        take_kernel,
        grid=(rows // tile,),
        in_specs=[pl.BlockSpec((1, 1, tile, depth), lambda i: (0, index, i, 0))],
        out_specs=pl.BlockSpec((tile, depth), lambda i: (i, 0)),
        out_shape=jax.ShapeDtypeStruct((rows, depth), fields.dtype),
        compiler_params=pltpu.CompilerParams(vmem_limit_bytes=VMEM_LIMIT),
        cost_estimate=pl.CostEstimate(flops=0, bytes_accessed=8 * rows * depth, transcendentals=0),
        name="take_field",
    )(fields)


def gather_kernel(fields, rows, depth, slots, words_ref, weights_ref, elastic_ref, acoustic_ref, out_ref, mixed):
    n_el = elastic_ref.shape[1]
    chunks = depth // LANES
    for f in range(fields):
        source = elastic_ref.at[0, f] if f < n_el else acoustic_ref.at[0, f - n_el]
        for c in range(chunks):
            mixed[pl.ds((c * fields + f) * rows, rows), :] = source[:, c * LANES : (c + 1) * LANES]
    lane = lax.broadcasted_iota(jnp.int32, (fields, LANES), 1)
    groups = out_ref.shape[1]

    def one_group(step, carry):
        def one_slot(r, values):
            first = (step * LANES + r) * 4
            total = None
            for s in range(4):
                start, at = split(words_ref[first + s], LANES)
                picked = mixed[pl.ds(start, fields, stride=rows), :]
                term = jnp.where(lane == at, picked * weights_ref[first + s], 0.0)
                total = term if total is None else total + term
            column = jnp.sum(total, axis=1, keepdims=True)
            return jnp.where(lane == r, column, values)

        values = lax.fori_loop(0, LANES, one_slot, jnp.zeros((fields, LANES), jnp.float32), unroll=16)
        out_ref[step // groups, step % groups] = values
        return carry

    lax.fori_loop(0, out_ref.shape[0] * groups, one_group, 0)


def near_kernel(n_el, d_ref, elastic_ref, acoustic_ref, out_ref):
    value = jnp.where(pl.program_id(0) < n_el, elastic_ref[0, 0], acoustic_ref[0, 0])
    out_ref[0] = jnp.dot(d_ref[...], value, precision=HIGH, preferred_element_type=jnp.float32)


def near_derivatives(operator, elastic, acoustic):
    rows, depth = elastic.shape[2:]
    return pl.pallas_call(
        functools.partial(near_kernel, 4),
        grid=(6,),
        in_specs=[
            pl.BlockSpec((rows, rows), lambda f: (0, 0)),
            pl.BlockSpec((1, 1, rows, depth), lambda f: (0, jnp.where(f < 3, f, 4), 0, 0)),
            pl.BlockSpec((1, 1, rows, depth), lambda f: (0, jnp.maximum(f - 4, 0), 0, 0)),
        ],
        out_specs=pl.BlockSpec((1, rows, depth), lambda f: (f, 0, 0)),
        out_shape=jax.ShapeDtypeStruct((6, rows, depth), jnp.float32),
        compiler_params=pltpu.CompilerParams(vmem_limit_bytes=VMEM_LIMIT),
        cost_estimate=pl.CostEstimate(
            flops=36 * rows * rows * depth, bytes_accessed=48 * rows * depth, transcendentals=0
        ),
        name="near_dx",
    )(operator, elastic, acoustic)


def section_kernel(
    rows, depth, slots, tile,
    words_ref, counts_ref, interp_ref, gates_ref,
    dx_ref, elastic_ref, acoustic_ref, el_media_ref, ac_media_ref, halo_ref,
    el_pair_ref, ac_pair_ref, ocean_row_ref, basin_row_ref,
    new_el_ref, new_ac_ref, open_ref,
):
    step = pl.program_id(0)
    here = pl.ds(pl.multiple_of(step * tile, tile), tile)
    lane = lax.broadcasted_iota(jnp.int32, (tile, depth), 1)

    def dz(value, slot):
        above = halo_ref[:, slot : slot + 1]
        below = halo_ref[:, 6 + slot : 7 + slot]
        following = jnp.where(lane == depth - 1, below, pltpu.roll(value, depth - 1, 1))
        previous = jnp.where(lane == 0, above, pltpu.roll(value, 1, 1))
        return (following - previous) * 0.5

    vx, vz, sxx, szz, sxz = [elastic_ref[0, f] for f in range(5)]
    p, ovx, ovz = [acoustic_ref[0, f] for f in range(3)]
    buoyancy = el_media_ref[0, 0]
    lame = el_media_ref[0, 1]
    shear = el_media_ref[0, 2]
    stiffness = lame + 2.0 * shear
    bulk = ac_media_ref[0, 0]
    ocean_buoyancy = ac_media_ref[0, 1]

    dx_vx = dx_ref[0]
    dz_vz = dz(vz, 1)
    new_el_ref[0, 0, here, :] = vx + STEP * (buoyancy * (dx_ref[2] + dz(sxz, 3)))
    new_el_ref[0, 1, here, :] = vz + STEP * (buoyancy * (dx_ref[3] + dz(szz, 2)))
    new_el_ref[0, 2, here, :] = sxx + STEP * (stiffness * dx_vx + lame * dz_vz)
    choose = lax.broadcasted_iota(jnp.int32, (tile, rows), 1)
    pressure = jnp.sum(jnp.where(el_pair_ref[...] == choose, ocean_row_ref[...], 0.0), axis=1, keepdims=True)
    velocity = jnp.sum(jnp.where(ac_pair_ref[...] == choose, basin_row_ref[...], 0.0), axis=1, keepdims=True)
    rate_szz = lame * dx_vx + stiffness * dz_vz
    rate_szz = rate_szz + jnp.where(lane == 0, gates_ref[0] * (PENALTY * (-pressure - szz)), 0.0)
    new_el_ref[0, 3, here, :] = szz + STEP * rate_szz
    new_el_ref[0, 4, here, :] = sxz + STEP * (shear * (dz(vx, 0) + dx_ref[1]))
    new_ac_ref[0, 0, here, :] = p - STEP * (bulk * (dx_ref[5] + dz(ovz, 5)))
    new_ac_ref[0, 1, here, :] = ovx - STEP * (ocean_buoyancy * dx_ref[4])
    rate_ovz = -ocean_buoyancy * dz(p, 4)
    rate_ovz = rate_ovz + jnp.where(lane == depth - 1, gates_ref[1] * (PENALTY * (velocity - ovz)), 0.0)
    new_ac_ref[0, 2, here, :] = ovz + STEP * rate_ovz
    open_ref[here, :] = jnp.ones((tile, depth), jnp.float32)

    @pl.when(step == pl.num_programs(0) - 1)
    def _():
        place = lax.broadcasted_iota(jnp.int32, (8, LANES), 0) * LANES
        place = place + lax.broadcasted_iota(jnp.int32, (8, LANES), 1)
        n_el = new_el_ref.shape[1]

        def one_patch(q, carry):
            def one_slot(r, inner):
                block, at = split(words_ref[q * slots + r], 8 * LANES)
                high, low = split(block, depth // LANES)
                at_row = pl.ds(pl.multiple_of(high * 8, 8), 8)
                at_lane = pl.ds(pl.multiple_of(low * LANES, LANES), LANES)
                hit = place == at
                group, within = split(r, LANES)
                first = (q * (slots // LANES) + group) * (8 * LANES) + within
                for f in range(8):
                    target = new_el_ref.at[0, f] if f < n_el else new_ac_ref.at[0, f - n_el]
                    target[at_row, at_lane] = jnp.where(hit, interp_ref[first + f * LANES], target[at_row, at_lane])
                open_ref[at_row, at_lane] = jnp.where(hit, 0.0, open_ref[at_row, at_lane])
                return inner

            return lax.fori_loop(0, counts_ref[q], one_slot, carry)

        lax.fori_loop(0, counts_ref.shape[0], one_patch, 0)


def far_kernel(coefficients, d_ref, far_ref, media_ref, open_ref, base_ref, out_ref):
    far = jnp.dot(d_ref[...], far_ref[...], precision=HIGH, preferred_element_type=jnp.float32)
    media = [media_ref[0, i] for i in range(media_ref.shape[1])]
    is_open = open_ref[...] > 0.5
    for i, coefficient in enumerate(coefficients):
        old = base_ref[0, i]
        out_ref[0, i] = jnp.where(is_open, old + (STEP * coefficient(*media)) * far, old)


def add_far(base, operator, far, media, first_media, n_media, first_field, coefficients, opened, tile):
    rows, reach = operator.shape
    depth = far.shape[1]
    n_out = len(coefficients)
    return pl.pallas_call(
        functools.partial(far_kernel, coefficients),
        grid=(depth // tile,),
        in_specs=[
            pl.BlockSpec((rows, reach), lambda i: (0, 0)),
            pl.BlockSpec((reach, tile), lambda i: (0, i)),
            pl.BlockSpec((1, n_media, rows, tile), lambda i: (0, first_media // n_media, 0, i)),
            pl.BlockSpec((rows, tile), lambda i: (0, i)),
            pl.BlockSpec((1, n_out, rows, tile), lambda i: (0, first_field // n_out, 0, i)),
        ],
        out_specs=pl.BlockSpec((1, n_out, rows, tile), lambda i: (0, first_field // n_out, 0, i)),
        out_shape=jax.ShapeDtypeStruct(base.shape, base.dtype),
        input_output_aliases={4: 0},
        compiler_params=pltpu.CompilerParams(vmem_limit_bytes=VMEM_LIMIT),
        cost_estimate=pl.CostEstimate(
            flops=6 * rows * reach * depth,
            bytes_accessed=4 * rows * depth * (3 + n_media + n_out),
            transcendentals=0,
        ),
        name="add_far",
    )(operator, far, media, opened, base)


def per_device(
    elastic,
    acoustic,
    el_media,
    ac_media,
    cont_matrix,
    fringe_cells,
    donor_cells,
    donor_weights,
    donor_counts,
    el_pair,
    ac_pair,
):
    rows, depth = elastic.shape[2], elastic.shape[3]
    slabs = lax.axis_size("line")
    layers = lax.axis_size("layer")
    patches = lax.axis_size("patch")
    slots = fringe_cells.shape[-1]
    groups = slots // LANES
    me = lax.axis_index("line")
    layer = lax.axis_index("layer")
    tile = min(64, rows)

    def other_slabs(value):
        parts = [
            lax.ppermute(value, "line", [(i, (i + distance) % slabs) for i in range(slabs)])
            for distance in range(1, slabs)
        ]
        return parts[0] if slabs == 2 else jnp.concatenate(parts, axis=0)

    far = [
        other_slabs(value)
        for value in [take_field(elastic, f, tile) for f in (0, 1, 2, 4)] + [take_field(acoustic, f, tile) for f in (0, 1)]
    ]

    asked = jnp.concatenate([donor_cells[0, 0, 0].astype(jnp.float32), donor_weights[0, 0, 0]], axis=1)
    asked = lax.all_to_all(asked, "patch", split_axis=0, concat_axis=0, tiled=True)
    x, z = split(jnp.swapaxes(asked[:, :4], 1, 2).astype(jnp.int32), depth)
    chunk, at_lane = split(z, LANES)
    asked_words = ((chunk * (8 * rows) + x) * LANES + at_lane).reshape(-1)
    asked_weights = jnp.swapaxes(asked[:, 4:], 1, 2).reshape(-1)

    smem = pl.BlockSpec(memory_space=pltpu.SMEM)
    vmem = pl.BlockSpec(memory_space=pltpu.VMEM)
    local = pl.pallas_call(
        functools.partial(gather_kernel, 8, rows, depth, slots),
        in_specs=[smem, smem, vmem, vmem],
        out_specs=vmem,
        out_shape=jax.ShapeDtypeStruct((patches, groups, 8, LANES), jnp.float32),
        scratch_shapes=[pltpu.VMEM((8 * rows * (depth // LANES), LANES), jnp.float32)],
        compiler_params=pltpu.CompilerParams(vmem_limit_bytes=VMEM_LIMIT),
        cost_estimate=pl.CostEstimate(flops=10**9, bytes_accessed=32 * rows * depth, transcendentals=0),
        name="donor_gather",
    )(asked_words, asked_weights, elastic, acoustic)
    interp = lax.all_to_all(local, "patch", split_axis=0, concat_axis=0, tiled=True).reshape(-1)

    depth_in = [elastic[0, 0], elastic[0, 1], elastic[0, 3], elastic[0, 4], acoustic[0, 0], acoustic[0, 2]]
    top_cells = jnp.stack([value[:, 0] for value in depth_in])
    bottom_cells = jnp.stack([value[:, depth - 1] for value in depth_in])
    from_above = lax.ppermute(bottom_cells, "layer", [(i, (i + 1) % layers) for i in range(layers)])
    from_below = lax.ppermute(top_cells, "layer", [(i, (i - 1) % layers) for i in range(layers)])
    at_top, at_bottom = layer == 0, layer == layers - 1
    ocean_row = from_above[4:5]
    basin_row = from_below[1:2]
    halo = jnp.concatenate([jnp.where(at_top, 0.0, from_above), jnp.where(at_bottom, 0.0, from_below)]).T
    gates = jnp.stack([at_top, at_bottom]).astype(jnp.float32)

    blocks = operator_blocks(cont_matrix, rows, slabs, me)
    far_operator = blocks[1] if slabs == 2 else jnp.concatenate(blocks[1:], axis=1)

    near = near_derivatives(blocks[0], elastic, acoustic)
    x, z = split(fringe_cells[0, 0, 0], depth)
    (row_block, row), (chunk, at_lane) = split(x, 8), split(z, LANES)
    fringe_words = ((row_block * (depth // LANES) + chunk) * 8 + row) * LANES + at_lane
    new_el, new_ac, opened = pl.pallas_call(
        functools.partial(section_kernel, rows, depth, slots, tile),
        grid=(rows // tile,),
        in_specs=[
            smem,
            smem,
            smem,
            smem,
            pl.BlockSpec((6, tile, depth), lambda i: (0, i, 0)),
            pl.BlockSpec((1, 5, tile, depth), lambda i: (0, 0, i, 0)),
            pl.BlockSpec((1, 3, tile, depth), lambda i: (0, 0, i, 0)),
            pl.BlockSpec((1, 3, tile, depth), lambda i: (0, 0, i, 0)),
            pl.BlockSpec((1, 2, tile, depth), lambda i: (0, 0, i, 0)),
            pl.BlockSpec((tile, 12), lambda i: (i, 0)),
            pl.BlockSpec((tile, 1), lambda i: (i, 0)),
            pl.BlockSpec((tile, 1), lambda i: (i, 0)),
            vmem,
            vmem,
        ],
        out_specs=[vmem, vmem, vmem],
        out_shape=[
            jax.ShapeDtypeStruct(elastic.shape, jnp.float32),
            jax.ShapeDtypeStruct(acoustic.shape, jnp.float32),
            jax.ShapeDtypeStruct((rows, depth), jnp.float32),
        ],
        compiler_params=pltpu.CompilerParams(vmem_limit_bytes=VMEM_LIMIT),
        cost_estimate=pl.CostEstimate(
            flops=100 * rows * depth, bytes_accessed=112 * rows * depth, transcendentals=0
        ),
        name="near_section",
    )(
        fringe_words.reshape(-1),
        donor_counts[0, 0, 0],
        interp,
        gates,
        near,
        elastic,
        acoustic,
        el_media,
        ac_media,
        halo,
        el_pair[0][:, None],
        ac_pair[0][:, None],
        ocean_row,
        basin_row,
    )

    far_tile = min(256, depth)
    new_el = add_far(
        new_el, far_operator, far[0], el_media, 0, 3, 2,
        (lambda b, l, m: l + 2.0 * m, lambda b, l, m: l), opened, far_tile,
    )
    new_el = add_far(new_el, far_operator, far[1], el_media, 2, 1, 4, (lambda m: m,), opened, far_tile)
    new_el = add_far(new_el, far_operator, far[2], el_media, 0, 1, 0, (lambda b: b,), opened, far_tile)
    new_el = add_far(new_el, far_operator, far[3], el_media, 0, 1, 1, (lambda b: b,), opened, far_tile)
    new_ac = add_far(new_ac, far_operator, far[4], ac_media, 1, 1, 1, (lambda b: -b,), opened, far_tile)
    new_ac = add_far(new_ac, far_operator, far[5], ac_media, 0, 1, 0, (lambda k: -k,), opened, far_tile)
    return new_el, new_ac


def solution(mesh):
    placed = (
        P("patch", None, "line", "layer"),
        P("patch", None, "line", "layer"),
        P("patch", None, "line", "layer"),
        P("patch", None, "line", "layer"),
        P(),
        P("patch", "line", "layer", None, None),
        P("patch", "line", "layer", None, None, None),
        P("patch", "line", "layer", None, None, None),
        P("patch", "line", "layer", None),
        P("patch", "line"),
        P("patch", "line"),
    )
    return jax.shard_map(
        per_device,
        mesh=mesh,
        in_specs=placed,
        out_specs=(P("patch", None, "line", "layer"), P("patch", None, "line", "layer")),
        check_vma=False,
    )
```

```python
import functools
import math

import jax
import jax.numpy as jnp
import numpy as np
from jax import lax
from jax.experimental import pallas as pl
from jax.experimental.pallas import tpu as pltpu
from jax.sharding import PartitionSpec as P

STEP = 0.25
PENALTY = 2.0
LANES = 128
VMEM_LIMIT = 56 * 1024 * 1024
FAR_VMEM_LIMIT = 24 * 1024 * 1024
HIGH = lax.Precision.HIGH
HIGHEST = lax.Precision.HIGHEST


def derivative_row(period):
    n = np.arange(1, period)
    sign = np.where(n % 2 == 0, 1.0, -1.0)
    row = np.zeros(period)
    row[1:] = (math.pi / period) * sign / np.tan(math.pi * n / period)
    return row


def operator_blocks(cont_matrix, rows, slabs, me):
    cont = cont_matrix.shape[0]
    match = cont_matrix.shape[1] // 2
    points = rows * slabs
    period = points + cont
    row = derivative_row(period)
    j = np.arange(rows)
    blocks = np.stack(
        [
            row[(o * rows + j[:, None] - j[None, :]) % period]
            for o in range(-(slabs - 1), slabs)
        ]
    ).astype(np.float32)
    to_tail = np.stack(
        [
            row[(s * rows + j[:, None] - points - np.arange(cont)[None, :]) % period]
            for s in range(slabs)
        ]
    ).astype(np.float32)
    tail_rows = lax.dynamic_index_in_dim(jnp.asarray(to_tail), me, 0, keepdims=False)
    folded = jnp.dot(tail_rows, cont_matrix, precision=HIGHEST)
    on_last = jnp.pad(folded[:, :match], ((0, 0), (rows - match, 0)))
    on_first = jnp.pad(folded[:, match:], ((0, 0), (0, rows - match)))
    table = jnp.asarray(blocks)
    out = []
    for distance in range(slabs):
        source = (me - distance) % slabs
        block = lax.dynamic_index_in_dim(table, me - source + slabs - 1, 0, keepdims=False)
        block = block + jnp.where(source == slabs - 1, on_last, 0.0)
        out.append(block + jnp.where(source == 0, on_first, 0.0))
    return out


def split(value, size):
    if size & (size - 1) == 0:
        return lax.shift_right_logical(value, size.bit_length() - 1), value & (size - 1)
    return lax.div(value, size), lax.rem(value, size)


def gather_kernel(fields, rows, depth, slots, words_ref, weights_ref, elastic_ref, acoustic_ref, out_ref, mixed):
    n_el = elastic_ref.shape[1]
    chunks = depth // LANES
    for f in range(fields):
        source = elastic_ref.at[0, f] if f < n_el else acoustic_ref.at[0, f - n_el]
        for c in range(chunks):
            mixed[pl.ds((c * fields + f) * rows, rows), :] = source[:, c * LANES : (c + 1) * LANES]
    lane = lax.broadcasted_iota(jnp.int32, (fields, LANES), 1)
    groups = out_ref.shape[1]

    def one_group(step, carry):
        def one_slot(r, values):
            first = (step * LANES + r) * 4
            total = None
            for s in range(4):
                start, at = split(words_ref[first + s], LANES)
                picked = mixed[pl.ds(start, fields, stride=rows), :]
                term = jnp.where(lane == at, picked * weights_ref[first + s], 0.0)
                total = term if total is None else total + term
            column = jnp.sum(total, axis=1, keepdims=True)
            return jnp.where(lane == r, column, values)

        values = lax.fori_loop(0, LANES, one_slot, jnp.zeros((fields, LANES), jnp.float32), unroll=16)
        out_ref[step // groups, step % groups] = values
        return carry

    lax.fori_loop(0, out_ref.shape[0] * groups, one_group, 0)


def near_kernel(n_el, d_ref, elastic_ref, acoustic_ref, out_ref):
    value = jnp.where(pl.program_id(0) < n_el, elastic_ref[0, 0], acoustic_ref[0, 0])
    out_ref[0] = jnp.dot(d_ref[...], value, precision=HIGH, preferred_element_type=jnp.float32)


def near_derivatives(operator, elastic, acoustic):
    rows, depth = elastic.shape[2:]
    return pl.pallas_call(
        functools.partial(near_kernel, 4),
        grid=(6,),
        in_specs=[
            pl.BlockSpec((rows, rows), lambda f: (0, 0)),
            pl.BlockSpec((1, 1, rows, depth), lambda f: (0, jnp.where(f < 3, f, 4), 0, 0)),
            pl.BlockSpec((1, 1, rows, depth), lambda f: (0, jnp.maximum(f - 4, 0), 0, 0)),
        ],
        out_specs=pl.BlockSpec((1, rows, depth), lambda f: (f, 0, 0)),
        out_shape=jax.ShapeDtypeStruct((6, rows, depth), jnp.float32),
        compiler_params=pltpu.CompilerParams(vmem_limit_bytes=VMEM_LIMIT),
        cost_estimate=pl.CostEstimate(
            flops=36 * rows * rows * depth, bytes_accessed=48 * rows * depth, transcendentals=0
        ),
        name="near_dx",
    )(operator, elastic, acoustic)


def section_kernel(
    rows, depth, slots, tile,
    words_ref, counts_ref, interp_ref, gates_ref,
    dx_ref, elastic_ref, acoustic_ref, el_media_ref, ac_media_ref, halo_ref,
    el_pair_ref, ac_pair_ref, ocean_row_ref, basin_row_ref,
    new_el_ref, new_ac_ref, open_ref,
):
    step = pl.program_id(0)
    here = pl.ds(pl.multiple_of(step * tile, tile), tile)
    lane = lax.broadcasted_iota(jnp.int32, (tile, depth), 1)

    def dz(value, slot):
        above = halo_ref[:, slot : slot + 1]
        below = halo_ref[:, 8 + slot : 9 + slot]
        following = jnp.where(lane == depth - 1, below, pltpu.roll(value, depth - 1, 1))
        previous = jnp.where(lane == 0, above, pltpu.roll(value, 1, 1))
        return (following - previous) * 0.5

    vx, vz, sxx, szz, sxz = [elastic_ref[0, f] for f in range(5)]
    p, ovx, ovz = [acoustic_ref[0, f] for f in range(3)]
    buoyancy = el_media_ref[0, 0]
    lame = el_media_ref[0, 1]
    shear = el_media_ref[0, 2]
    stiffness = lame + 2.0 * shear
    bulk = ac_media_ref[0, 0]
    ocean_buoyancy = ac_media_ref[0, 1]

    dx_vx = dx_ref[0]
    dz_vz = dz(vz, 1)
    new_el_ref[0, 0, here, :] = vx + STEP * (buoyancy * (dx_ref[2] + dz(sxz, 4)))
    new_el_ref[0, 1, here, :] = vz + STEP * (buoyancy * (dx_ref[3] + dz(szz, 3)))
    new_el_ref[0, 2, here, :] = sxx + STEP * (stiffness * dx_vx + lame * dz_vz)
    choose = lax.broadcasted_iota(jnp.int32, (tile, rows), 1)
    pressure = jnp.sum(jnp.where(el_pair_ref[...] == choose, ocean_row_ref[...], 0.0), axis=1, keepdims=True)
    velocity = jnp.sum(jnp.where(ac_pair_ref[...] == choose, basin_row_ref[...], 0.0), axis=1, keepdims=True)
    rate_szz = lame * dx_vx + stiffness * dz_vz
    rate_szz = rate_szz + jnp.where(lane == 0, gates_ref[0] * (PENALTY * (-pressure - szz)), 0.0)
    new_el_ref[0, 3, here, :] = szz + STEP * rate_szz
    new_el_ref[0, 4, here, :] = sxz + STEP * (shear * (dz(vx, 0) + dx_ref[1]))
    new_ac_ref[0, 0, here, :] = p - STEP * (bulk * (dx_ref[5] + dz(ovz, 7)))
    new_ac_ref[0, 1, here, :] = ovx - STEP * (ocean_buoyancy * dx_ref[4])
    rate_ovz = -ocean_buoyancy * dz(p, 5)
    rate_ovz = rate_ovz + jnp.where(lane == depth - 1, gates_ref[1] * (PENALTY * (velocity - ovz)), 0.0)
    new_ac_ref[0, 2, here, :] = ovz + STEP * rate_ovz
    open_ref[here, :] = jnp.ones((tile, depth), jnp.float32)

    @pl.when(step == pl.num_programs(0) - 1)
    def _():
        place = lax.broadcasted_iota(jnp.int32, (8, LANES), 0) * LANES
        place = place + lax.broadcasted_iota(jnp.int32, (8, LANES), 1)
        n_el = new_el_ref.shape[1]

        def one_patch(q, carry):
            def one_slot(r, inner):
                block, at = split(words_ref[q * slots + r], 8 * LANES)
                high, low = split(block, depth // LANES)
                at_row = pl.ds(pl.multiple_of(high * 8, 8), 8)
                at_lane = pl.ds(pl.multiple_of(low * LANES, LANES), LANES)
                hit = place == at
                group, within = split(r, LANES)
                first = (q * (slots // LANES) + group) * (8 * LANES) + within
                for f in range(8):
                    target = new_el_ref.at[0, f] if f < n_el else new_ac_ref.at[0, f - n_el]
                    target[at_row, at_lane] = jnp.where(hit, interp_ref[first + f * LANES], target[at_row, at_lane])
                open_ref[at_row, at_lane] = jnp.where(hit, 0.0, open_ref[at_row, at_lane])
                return inner

            return lax.fori_loop(0, counts_ref[q], one_slot, carry)

        lax.fori_loop(0, counts_ref.shape[0], one_patch, 0)


def far_kernel(coefficients, turn_ref, d_ref, far_ref, media_ref, open_ref, base_ref, next_ref, out_ref):
    del turn_ref, next_ref
    far = jnp.dot(d_ref[...], far_ref[...], precision=HIGH, preferred_element_type=jnp.float32)
    media = [media_ref[0, i] for i in range(media_ref.shape[1])]
    is_open = open_ref[...] > 0.5
    for i, coefficient in enumerate(coefficients):
        old = base_ref[0, i]
        out_ref[0, i] = jnp.where(is_open, old + (STEP * coefficient(*media)) * far, old)


def add_far(base, operator, far, at, media, first_media, n_media, first_field, coefficients, opened, turn):
    rows, reach = operator.shape
    width = far.shape[1]
    tile = math.gcd(math.gcd(width, at), 2 * LANES)
    n_out = len(coefficients)
    shift = at // tile
    return pl.pallas_call(
        functools.partial(far_kernel, coefficients),
        grid=(width // tile,),
        in_specs=[
            pl.BlockSpec(memory_space=pl.ANY),
            pl.BlockSpec((rows, reach), lambda i: (0, 0)),
            pl.BlockSpec((reach, tile), lambda i: (0, i)),
            pl.BlockSpec((1, n_media, rows, tile), lambda i: (0, first_media // n_media, 0, i + shift)),
            pl.BlockSpec((rows, tile), lambda i: (0, i + shift)),
            pl.BlockSpec((1, n_out, rows, tile), lambda i: (0, first_field // n_out, 0, i + shift)),
        ],
        out_specs=[
            pl.BlockSpec(memory_space=pl.ANY),
            pl.BlockSpec((1, n_out, rows, tile), lambda i: (0, first_field // n_out, 0, i + shift)),
        ],
        out_shape=[
            jax.ShapeDtypeStruct(turn.shape, turn.dtype),
            jax.ShapeDtypeStruct(base.shape, base.dtype),
        ],
        input_output_aliases={0: 0, 5: 1},
        compiler_params=pltpu.CompilerParams(vmem_limit_bytes=FAR_VMEM_LIMIT),
        cost_estimate=pl.CostEstimate(
            flops=6 * rows * reach * width,
            bytes_accessed=4 * rows * width * (3 + n_media + n_out),
            transcendentals=0,
        ),
        name="add_far",
    )(turn, operator, far, media, opened, base)


def per_device(
    elastic,
    acoustic,
    el_media,
    ac_media,
    cont_matrix,
    fringe_cells,
    donor_cells,
    donor_weights,
    donor_counts,
    el_pair,
    ac_pair,
):
    rows, depth = elastic.shape[2], elastic.shape[3]
    slabs = lax.axis_size("line")
    layers = lax.axis_size("layer")
    patches = lax.axis_size("patch")
    slots = fringe_cells.shape[-1]
    groups = slots // LANES
    me = lax.axis_index("line")
    layer = lax.axis_index("layer")
    tile = min(64, rows)

    def other_slabs(value):
        parts = [
            lax.ppermute(value, "line", [(i, (i + distance) % slabs) for i in range(slabs)])
            for distance in range(1, slabs)
        ]
        return parts[0] if slabs == 2 else jnp.concatenate(parts, axis=0)

    half, quarter = depth // 2, depth // 4
    pieces = [
        ("el", 0, 0, depth, "el", 0, 3, 2, (lambda b, l, m: l + 2.0 * m, lambda b, l, m: l)),
        ("ac", 0, 0, depth, "ac", 1, 1, 1, (lambda b: -b,)),
        ("ac", 1, 0, depth, "ac", 0, 1, 0, (lambda k: -k,)),
        ("el", 1, 0, depth, "el", 2, 1, 4, (lambda m: m,)),
        ("el", 2, 0, depth, "el", 0, 1, 0, (lambda b: b,)),
        ("el", 4, 0, half, "el", 0, 1, 1, (lambda b: b,)),
        ("el", 4, half, quarter, "el", 0, 1, 1, (lambda b: b,)),
        ("el", 4, half + quarter, quarter, "el", 0, 1, 1, (lambda b: b,)),
    ]
    far = []
    source = {"el": elastic, "ac": acoustic}
    for name, field, at, width, *_ in pieces:
        value = lax.slice(source[name], (0, field, 0, at), (1, field + 1, rows, at + width)).reshape(rows, width)
        value, source["el"], source["ac"] = lax.optimization_barrier((value, source["el"], source["ac"]))
        far.append(other_slabs(value))

    asked = jnp.concatenate([donor_cells[0, 0, 0].astype(jnp.float32), donor_weights[0, 0, 0]], axis=1)
    asked = lax.all_to_all(asked, "patch", split_axis=0, concat_axis=0, tiled=True)
    x, z = split(jnp.swapaxes(asked[:, :4], 1, 2).astype(jnp.int32), depth)
    chunk, at_lane = split(z, LANES)
    asked_words = ((chunk * (8 * rows) + x) * LANES + at_lane).reshape(-1)
    asked_weights = jnp.swapaxes(asked[:, 4:], 1, 2).reshape(-1)

    smem = pl.BlockSpec(memory_space=pltpu.SMEM)
    vmem = pl.BlockSpec(memory_space=pltpu.VMEM)
    local = pl.pallas_call(
        functools.partial(gather_kernel, 8, rows, depth, slots),
        in_specs=[smem, smem, vmem, vmem],
        out_specs=vmem,
        out_shape=jax.ShapeDtypeStruct((patches, groups, 8, LANES), jnp.float32),
        scratch_shapes=[pltpu.VMEM((8 * rows * (depth // LANES), LANES), jnp.float32)],
        compiler_params=pltpu.CompilerParams(vmem_limit_bytes=VMEM_LIMIT),
        cost_estimate=pl.CostEstimate(flops=10**9, bytes_accessed=32 * rows * depth, transcendentals=0),
        name="donor_gather",
    )(asked_words, asked_weights, elastic, acoustic)
    interp = lax.all_to_all(local, "patch", split_axis=0, concat_axis=0, tiled=True).reshape(-1)

    top = jnp.concatenate([elastic[0, :, :, 0], acoustic[0, :, :, 0]])
    bottom = jnp.concatenate([elastic[0, :, :, depth - 1], acoustic[0, :, :, depth - 1]])
    edges = lax.all_gather(jnp.concatenate([top, bottom]), "layer")
    at_top, at_bottom = layer == 0, layer == layers - 1
    from_above = lax.dynamic_index_in_dim(edges, (layer - 1) % layers, 0, keepdims=False)[8:]
    from_below = lax.dynamic_index_in_dim(edges, (layer + 1) % layers, 0, keepdims=False)[:8]
    ocean_row = from_above[5:6]
    basin_row = from_below[1:2]
    halo = jnp.concatenate([jnp.where(at_top, 0.0, from_above), jnp.where(at_bottom, 0.0, from_below)]).T
    gates = jnp.stack([at_top, at_bottom]).astype(jnp.float32)

    blocks = operator_blocks(cont_matrix, rows, slabs, me)
    far_operator = blocks[1] if slabs == 2 else jnp.concatenate(blocks[1:], axis=1)

    near = near_derivatives(blocks[0], elastic, acoustic)
    x, z = split(fringe_cells[0, 0, 0], depth)
    (row_block, row), (chunk, at_lane) = split(x, 8), split(z, LANES)
    fringe_words = ((row_block * (depth // LANES) + chunk) * 8 + row) * LANES + at_lane
    new_el, new_ac, opened = pl.pallas_call(
        functools.partial(section_kernel, rows, depth, slots, tile),
        grid=(rows // tile,),
        in_specs=[
            smem,
            smem,
            smem,
            smem,
            pl.BlockSpec((6, tile, depth), lambda i: (0, i, 0)),
            pl.BlockSpec((1, 5, tile, depth), lambda i: (0, 0, i, 0)),
            pl.BlockSpec((1, 3, tile, depth), lambda i: (0, 0, i, 0)),
            pl.BlockSpec((1, 3, tile, depth), lambda i: (0, 0, i, 0)),
            pl.BlockSpec((1, 2, tile, depth), lambda i: (0, 0, i, 0)),
            pl.BlockSpec((tile, 16), lambda i: (i, 0)),
            pl.BlockSpec((tile, 1), lambda i: (i, 0)),
            pl.BlockSpec((tile, 1), lambda i: (i, 0)),
            vmem,
            vmem,
        ],
        out_specs=[vmem, vmem, vmem],
        out_shape=[
            jax.ShapeDtypeStruct(elastic.shape, jnp.float32),
            jax.ShapeDtypeStruct(acoustic.shape, jnp.float32),
            jax.ShapeDtypeStruct((rows, depth), jnp.float32),
        ],
        compiler_params=pltpu.CompilerParams(vmem_limit_bytes=VMEM_LIMIT),
        cost_estimate=pl.CostEstimate(
            flops=100 * rows * depth, bytes_accessed=112 * rows * depth, transcendentals=0
        ),
        name="near_section",
    )(
        fringe_words.reshape(-1),
        donor_counts[0, 0, 0],
        interp,
        gates,
        near,
        elastic,
        acoustic,
        el_media,
        ac_media,
        halo,
        el_pair[0][:, None],
        ac_pair[0][:, None],
        ocean_row,
        basin_row,
    )

    turn = jnp.zeros((8, LANES), jnp.float32)
    section = {"el": new_el, "ac": new_ac}
    media = {"el": el_media, "ac": ac_media}
    for value, (_, _, at, _, target, first_media, n_media, first_field, coefficients) in zip(far, pieces):
        turn, section[target] = add_far(
            section[target], far_operator, value, at,
            media[target], first_media, n_media, first_field, coefficients, opened, turn,
        )
    return section["el"], section["ac"]


def solution(mesh):
    placed = (
        P("patch", None, "line", "layer"),
        P("patch", None, "line", "layer"),
        P("patch", None, "line", "layer"),
        P("patch", None, "line", "layer"),
        P(),
        P("patch", "line", "layer", None, None),
        P("patch", "line", "layer", None, None, None),
        P("patch", "line", "layer", None, None, None),
        P("patch", "line", "layer", None),
        P("patch", "line"),
        P("patch", "line"),
    )
    return jax.shard_map(
        per_device,
        mesh=mesh,
        in_specs=placed,
        out_specs=(P("patch", None, "line", "layer"), P("patch", None, "line", "layer")),
        check_vma=False,
    )
```

```python
import functools
import math

import jax
import jax.numpy as jnp
import numpy as np
from jax import lax
from jax.experimental import pallas as pl
from jax.experimental.pallas import tpu as pltpu
from jax.sharding import PartitionSpec as P

STEP = 0.25
PENALTY = 2.0
LANES = 128
VMEM_LIMIT = 56 * 1024 * 1024
FAR_VMEM_LIMIT = 24 * 1024 * 1024
HIGHEST = lax.Precision.HIGHEST


def derivative_row(period):
    n = np.arange(1, period)
    sign = np.where(n % 2 == 0, 1.0, -1.0)
    row = np.zeros(period)
    row[1:] = (math.pi / period) * sign / np.tan(math.pi * n / period)
    return row


def operator_tables(rows, slabs, cont):
    points = rows * slabs
    period = points + cont
    row = derivative_row(period)
    j = np.arange(rows)
    own = row[(j[:, None] - j[None, :]) % period]
    far, tail = [], []
    for me in range(slabs):
        mine = me * rows + j[:, None]
        others = np.concatenate([(me - d) % slabs * rows + j for d in range(1, slabs)])
        far.append(row[(mine - others[None, :]) % period])
        tail.append(row[(mine - points - np.arange(cont)[None, :]) % period])
    return tuple(np.asarray(table, np.float32) for table in (own, far, tail))


def continuation_on(cont_matrix, rows, slabs, sources):
    match = cont_matrix.shape[1] // 2
    on_last = jnp.pad(cont_matrix[:, :match], ((0, 0), (rows - match, 0)))
    on_first = jnp.pad(cont_matrix[:, match:], ((0, 0), (0, rows - match)))
    return jnp.concatenate(
        [
            jnp.where(source == slabs - 1, on_last, 0.0) + jnp.where(source == 0, on_first, 0.0)
            for source in sources
        ],
        axis=1,
    )


def split(value, size):
    if size & (size - 1) == 0:
        return lax.shift_right_logical(value, size.bit_length() - 1), value & (size - 1)
    return lax.div(value, size), lax.rem(value, size)


def take_kernel(pieces, elastic_ref, acoustic_ref, after_ref, *refs):
    del after_ref
    outs, semaphores = refs[: len(pieces)], refs[-1]
    copies = []
    for i, (name, field, at, width) in enumerate(pieces):
        source = elastic_ref if name == "el" else acoustic_ref
        copies.append(
            pltpu.make_async_copy(source.at[0, field, :, pl.ds(at, width)], outs[i], semaphores.at[i])
        )
    for copy in copies:
        copy.start()
    return copies


def take_only_kernel(pieces, *refs):
    for copy in take_kernel(pieces, *refs):
        copy.wait()


def take_and_edges_kernel(pieces, layers, elastic_ref, acoustic_ref, after_ref, *refs):
    n = len(pieces)
    edges_ref, tiles, edge_semaphores, semaphores = refs[n:]
    n_el, n_ac = elastic_ref.shape[1], acoustic_ref.shape[1]
    rows, depth = elastic_ref.shape[2:]
    loads = []
    for end, at in enumerate((0, depth - LANES)):
        for k, (source, first, count) in enumerate(((elastic_ref, 0, n_el), (acoustic_ref, n_el, n_ac))):
            loads.append(
                pltpu.make_async_copy(
                    source.at[0, :, :, pl.ds(at, LANES)],
                    tiles.at[end, pl.ds(first, count)],
                    edge_semaphores.at[2 * end + k],
                )
            )
    for load in loads:
        load.start()
    copies = take_kernel(pieces, elastic_ref, acoustic_ref, after_ref, *refs[:n], semaphores)
    for load in loads:
        load.wait()
    lane = lax.broadcasted_iota(jnp.int32, (rows, LANES), 1)
    columns = jnp.zeros((rows, LANES), jnp.float32)
    for f in range(n_el + n_ac):
        columns = jnp.where(lane == f, tiles[0, f, :, 0:1], columns)
        columns = jnp.where(lane == 8 + f, tiles[1, f, :, LANES - 1 : LANES], columns)
    lines = columns.T
    below = lax.rem(lax.axis_index("layer") + 1, layers)
    for to in range(layers):
        edges_ref[to] = jnp.where(to == below, lines[8:16], lines[0:8])
    for copy in copies:
        copy.wait()


def take_pieces(elastic, acoustic, after, pieces, layers=0):
    rows = elastic.shape[2]
    anywhere = pl.BlockSpec(memory_space=pl.ANY)
    out_shape = [jax.ShapeDtypeStruct((rows, width), jnp.float32) for _, _, _, width in pieces]
    out_specs = [anywhere] * len(pieces)
    scratch = [pltpu.SemaphoreType.DMA((len(pieces),))]
    kernel = functools.partial(take_only_kernel, pieces)
    if layers:
        out_shape.append(jax.ShapeDtypeStruct((layers, 8, rows), jnp.float32))
        out_specs.append(pl.BlockSpec(memory_space=pltpu.VMEM))
        scratch = [pltpu.VMEM((2, 8, rows, LANES), jnp.float32), pltpu.SemaphoreType.DMA((4,))] + scratch
        kernel = functools.partial(take_and_edges_kernel, pieces, layers)
    cells = sum(width for _, _, _, width in pieces) * rows
    return pl.pallas_call(
        kernel,
        in_specs=[anywhere] * 3,
        out_specs=out_specs,
        out_shape=out_shape,
        scratch_shapes=scratch,
        compiler_params=pltpu.CompilerParams(vmem_limit_bytes=VMEM_LIMIT),
        cost_estimate=pl.CostEstimate(flops=0, bytes_accessed=8 * cells, transcendentals=0),
        name="take_pieces",
    )(elastic, acoustic, after)


def gather_kernel(fields, rows, depth, words_ref, weights_ref, elastic_ref, acoustic_ref, out_ref, mixed):
    n_el = elastic_ref.shape[1]
    chunks = depth // LANES
    for f in range(fields):
        source = elastic_ref.at[0, f] if f < n_el else acoustic_ref.at[0, f - n_el]
        for c in range(chunks):
            mixed[pl.ds((c * fields + f) * rows, rows), :] = source[:, c * LANES : (c + 1) * LANES]
    lane = lax.broadcasted_iota(jnp.int32, (fields, LANES), 1)
    groups = out_ref.shape[1]

    def one_group(step, carry):
        patch, group = split(step, groups)

        def one_slot(r, values):
            slot = group * LANES + r
            total = None
            for s in range(4):
                start, at = split(words_ref[patch, s, slot], LANES)
                picked = mixed[pl.ds(start, fields, stride=rows), :]
                term = jnp.where(lane == at, picked * weights_ref[patch, 4 + s, slot], 0.0)
                total = term if total is None else total + term
            column = jnp.sum(total, axis=1, keepdims=True)
            return jnp.where(lane == r, column, values)

        values = lax.fori_loop(0, LANES, one_slot, jnp.zeros((fields, LANES), jnp.float32), unroll=16)
        out_ref[patch, group] = values
        return carry

    lax.fori_loop(0, out_ref.shape[0] * groups, one_group, 0)


def bf16_pair(value):
    high = value.astype(jnp.bfloat16)
    return high, (value - high.astype(jnp.float32)).astype(jnp.bfloat16)


def three_left(value):
    high, low = bf16_pair(value)
    return jnp.concatenate([high, high, low], axis=1)


def three_right(value):
    high, low = bf16_pair(value)
    return jnp.concatenate([high, low, high], axis=0)


def near_kernel(
    n_el, me_ref, own_ref, far_ref, tail_ref, own_cont_ref, far_cont_ref, elastic_ref, acoustic_ref,
    out_ref, far_operator_ref, operator,
):
    del me_ref

    @pl.when(pl.program_id(0) == 0)
    def _():
        def folded(table, cont):
            return table + jnp.dot(tail_ref[0], cont, precision=HIGHEST, preferred_element_type=jnp.float32)

        operator[...] = three_left(folded(own_ref[...], own_cont_ref[...]))
        far_operator_ref[...] = three_left(folded(far_ref[0], far_cont_ref[...]))

    value = jnp.where(pl.program_id(0) < n_el, elastic_ref[0, 0], acoustic_ref[0, 0])
    out_ref[0] = jnp.dot(operator[...], three_right(value), preferred_element_type=jnp.float32)


def near_derivatives(elastic, acoustic, cont_matrix, me, slabs):
    rows, depth = elastic.shape[2:]
    cont = cont_matrix.shape[0]
    reach = (slabs - 1) * rows
    own, far, tail = operator_tables(rows, slabs, cont)
    own_cont = continuation_on(cont_matrix, rows, slabs, [me])
    far_cont = continuation_on(cont_matrix, rows, slabs, [(me - d) % slabs for d in range(1, slabs)])
    return pl.pallas_call(
        functools.partial(near_kernel, 4),
        grid_spec=pltpu.PrefetchScalarGridSpec(
            num_scalar_prefetch=1,
            grid=(6,),
            in_specs=[
                pl.BlockSpec((rows, rows), lambda f, me: (0, 0)),
                pl.BlockSpec((1, rows, reach), lambda f, me: (me[0], 0, 0)),
                pl.BlockSpec((1, rows, cont), lambda f, me: (me[0], 0, 0)),
                pl.BlockSpec((cont, rows), lambda f, me: (0, 0)),
                pl.BlockSpec((cont, reach), lambda f, me: (0, 0)),
                pl.BlockSpec((1, 1, rows, depth), lambda f, me: (0, jnp.where(f < 3, f, 4), 0, 0)),
                pl.BlockSpec((1, 1, rows, depth), lambda f, me: (0, jnp.maximum(f - 4, 0), 0, 0)),
            ],
            out_specs=[
                pl.BlockSpec((1, rows, depth), lambda f, me: (f, 0, 0)),
                pl.BlockSpec((rows, 3 * reach), lambda f, me: (0, 0)),
            ],
            scratch_shapes=[pltpu.VMEM((rows, 3 * rows), jnp.bfloat16)],
        ),
        out_shape=[
            jax.ShapeDtypeStruct((6, rows, depth), jnp.float32),
            jax.ShapeDtypeStruct((rows, 3 * reach), jnp.bfloat16),
        ],
        compiler_params=pltpu.CompilerParams(vmem_limit_bytes=VMEM_LIMIT),
        cost_estimate=pl.CostEstimate(
            flops=36 * rows * rows * depth, bytes_accessed=60 * rows * depth, transcendentals=0
        ),
        name="near_dx",
    )(me.reshape(1), own, far, tail, own_cont, far_cont, elastic, acoustic)


def section_kernel(
    layers, rows, depth, tile,
    cells_ref, counts_ref, interp_ref,
    dx_ref, elastic_ref, acoustic_ref, el_media_ref, ac_media_ref, edges_ref, el_pair_ref, ac_pair_ref,
    new_el_ref, new_ac_ref, open_ref,
    columns,
):
    step = pl.program_id(0)
    here = pl.ds(pl.multiple_of(step * tile, tile), tile)
    lane = lax.broadcasted_iota(jnp.int32, (tile, depth), 1)
    layer = lax.axis_index("layer")
    at_top, at_bottom = layer == 0, layer == layers - 1
    from_above = edges_ref[lax.rem(layer + layers - 1, layers)]
    from_below = edges_ref[lax.rem(layer + 1, layers)]
    ocean_row = from_above[5:6]
    basin_row = from_below[1:2]

    @pl.when(step == 0)
    def _():
        pairs = jnp.concatenate([el_pair_ref[...], ac_pair_ref[...]]).astype(jnp.float32)
        lines = [
            jnp.where(at_top, 0.0, from_above),
            jnp.where(at_bottom, 0.0, from_below),
            pairs,
            jnp.zeros((LANES - 18, rows), jnp.float32),
        ]
        columns[...] = jnp.concatenate(lines).T

    halo = columns[here, :]

    def dz(value, slot):
        above = halo[:, slot : slot + 1]
        below = halo[:, 8 + slot : 9 + slot]
        following = jnp.where(lane == depth - 1, below, pltpu.roll(value, depth - 1, 1))
        previous = jnp.where(lane == 0, above, pltpu.roll(value, 1, 1))
        return (following - previous) * 0.5

    vx, vz, sxx, szz, sxz = [elastic_ref[0, f] for f in range(5)]
    p, ovx, ovz = [acoustic_ref[0, f] for f in range(3)]
    buoyancy = el_media_ref[0, 0]
    lame = el_media_ref[0, 1]
    shear = el_media_ref[0, 2]
    stiffness = lame + 2.0 * shear
    bulk = ac_media_ref[0, 0]
    ocean_buoyancy = ac_media_ref[0, 1]

    dx_vx = dx_ref[0]
    dz_vz = dz(vz, 1)
    new_el_ref[0, 0, here, :] = vx + STEP * (buoyancy * (dx_ref[2] + dz(sxz, 4)))
    new_el_ref[0, 1, here, :] = vz + STEP * (buoyancy * (dx_ref[3] + dz(szz, 3)))
    new_el_ref[0, 2, here, :] = sxx + STEP * (stiffness * dx_vx + lame * dz_vz)
    choose = lax.broadcasted_iota(jnp.int32, (tile, rows), 1).astype(jnp.float32)
    pressure = jnp.sum(jnp.where(halo[:, 16:17] == choose, ocean_row, 0.0), axis=1, keepdims=True)
    velocity = jnp.sum(jnp.where(halo[:, 17:18] == choose, basin_row, 0.0), axis=1, keepdims=True)
    rate_szz = lame * dx_vx + stiffness * dz_vz
    rate_szz = rate_szz + jnp.where((lane == 0) & at_top, PENALTY * (-pressure - szz), 0.0)
    new_el_ref[0, 3, here, :] = szz + STEP * rate_szz
    new_el_ref[0, 4, here, :] = sxz + STEP * (shear * (dz(vx, 0) + dx_ref[1]))
    new_ac_ref[0, 0, here, :] = p - STEP * (bulk * (dx_ref[5] + dz(ovz, 7)))
    new_ac_ref[0, 1, here, :] = ovx - STEP * (ocean_buoyancy * dx_ref[4])
    rate_ovz = -ocean_buoyancy * dz(p, 5)
    rate_ovz = rate_ovz + jnp.where((lane == depth - 1) & at_bottom, PENALTY * (velocity - ovz), 0.0)
    new_ac_ref[0, 2, here, :] = ovz + STEP * rate_ovz
    open_ref[here, :] = jnp.ones((tile, depth), jnp.float32)

    @pl.when(step == pl.num_programs(0) - 1)
    def _():
        place = lax.broadcasted_iota(jnp.int32, (8, LANES), 0) * LANES
        place = place + lax.broadcasted_iota(jnp.int32, (8, LANES), 1)
        n_el = new_el_ref.shape[1]

        def one_patch(q, carry):
            def one_slot(r, inner):
                x, z = split(cells_ref[0, 0, 0, q, r], depth)
                (high, row), (low, at) = split(x, 8), split(z, LANES)
                at_row = pl.ds(pl.multiple_of(high * 8, 8), 8)
                at_lane = pl.ds(pl.multiple_of(low * LANES, LANES), LANES)
                hit = place == row * LANES + at
                group, within = split(r, LANES)
                for f in range(8):
                    target = new_el_ref.at[0, f] if f < n_el else new_ac_ref.at[0, f - n_el]
                    target[at_row, at_lane] = jnp.where(hit, interp_ref[q, group, f, within], target[at_row, at_lane])
                open_ref[at_row, at_lane] = jnp.where(hit, 0.0, open_ref[at_row, at_lane])
                return inner

            return lax.fori_loop(0, counts_ref[0, 0, 0, q], one_slot, carry)

        lax.fori_loop(0, counts_ref.shape[3], one_patch, 0)


def far_kernel(coefficients, turn_ref, d_ref, far_ref, media_ref, open_ref, base_ref, next_ref, out_ref):
    del turn_ref, next_ref
    far = jnp.dot(d_ref[...], three_right(far_ref[...]), preferred_element_type=jnp.float32)
    media = [media_ref[0, i] for i in range(media_ref.shape[1])]
    is_open = open_ref[...] > 0.5
    for i, coefficient in enumerate(coefficients):
        old = base_ref[0, i]
        out_ref[0, i] = jnp.where(is_open, old + (STEP * coefficient(*media)) * far, old)


def add_far(base, operator, far, at, media, first_media, n_media, first_field, coefficients, opened, turn):
    rows, reach = operator.shape[0], far.shape[0]
    width = far.shape[1]
    tile = math.gcd(math.gcd(width, at), 2 * LANES)
    n_out = len(coefficients)
    shift = at // tile
    return pl.pallas_call(
        functools.partial(far_kernel, coefficients),
        grid=(width // tile,),
        in_specs=[
            pl.BlockSpec(memory_space=pl.ANY),
            pl.BlockSpec((rows, 3 * reach), lambda i: (0, 0)),
            pl.BlockSpec((reach, tile), lambda i: (0, i)),
            pl.BlockSpec((1, n_media, rows, tile), lambda i: (0, first_media // n_media, 0, i + shift)),
            pl.BlockSpec((rows, tile), lambda i: (0, i + shift)),
            pl.BlockSpec((1, n_out, rows, tile), lambda i: (0, first_field // n_out, 0, i + shift)),
        ],
        out_specs=[
            pl.BlockSpec(memory_space=pl.ANY),
            pl.BlockSpec((1, n_out, rows, tile), lambda i: (0, first_field // n_out, 0, i + shift)),
        ],
        out_shape=[
            jax.ShapeDtypeStruct(turn.shape, turn.dtype),
            jax.ShapeDtypeStruct(base.shape, base.dtype),
        ],
        input_output_aliases={0: 0, 5: 1},
        compiler_params=pltpu.CompilerParams(vmem_limit_bytes=FAR_VMEM_LIMIT),
        cost_estimate=pl.CostEstimate(
            flops=6 * rows * reach * width,
            bytes_accessed=4 * rows * width * (3 + n_media + n_out),
            transcendentals=0,
        ),
        name="add_far",
    )(turn, operator, far, media, opened, base)


def per_device(
    elastic,
    acoustic,
    el_media,
    ac_media,
    cont_matrix,
    fringe_cells,
    donor_cells,
    donor_weights,
    donor_counts,
    el_pair,
    ac_pair,
):
    rows, depth = elastic.shape[2], elastic.shape[3]
    slabs = lax.axis_size("line")
    layers = lax.axis_size("layer")
    patches = lax.axis_size("patch")
    slots = fringe_cells.shape[-1]
    groups = slots // LANES
    me = lax.axis_index("line")
    layer = lax.axis_index("layer")
    tile = min(64, rows)

    def other_slabs(value):
        parts = [
            lax.ppermute(value, "line", [(i, (i + distance) % slabs) for i in range(slabs)])
            for distance in range(1, slabs)
        ]
        return parts[0] if slabs == 2 else jnp.concatenate(parts, axis=0)

    half, quarter = depth // 2, depth // 4
    pieces = [
        ("el", 0, 0, depth, "el", 0, 3, 2, (lambda b, l, m: l + 2.0 * m, lambda b, l, m: l)),
        ("ac", 0, 0, depth, "ac", 1, 1, 1, (lambda b: -b,)),
        ("ac", 1, 0, depth, "ac", 0, 1, 0, (lambda k: -k,)),
        ("el", 1, 0, depth, "el", 2, 1, 4, (lambda m: m,)),
        ("el", 2, 0, depth, "el", 0, 1, 0, (lambda b: b,)),
        ("el", 4, 0, half, "el", 0, 1, 1, (lambda b: b,)),
        ("el", 4, half, quarter, "el", 0, 1, 1, (lambda b: b,)),
        ("el", 4, half + quarter, quarter, "el", 0, 1, 1, (lambda b: b,)),
    ]
    travelling = [piece[:4] for piece in pieces]
    (first,) = take_pieces(elastic, acoustic, cont_matrix, travelling[:1])
    *others, edges = take_pieces(elastic, acoustic, first, travelling[1:], layers)
    far = [other_slabs(value) for value in [first, *others]]

    x, z = split(donor_cells[0, 0, 0], depth)
    chunk, at_lane = split(z, LANES)
    words = (chunk * (8 * rows) + x) * LANES + at_lane
    asked = jnp.concatenate([words.astype(jnp.float32), donor_weights[0, 0, 0]], axis=1)
    asked = lax.all_to_all(asked, "patch", split_axis=0, concat_axis=0, tiled=True)
    asked_words = asked[:, :4].astype(jnp.int32)

    smem = pl.BlockSpec(memory_space=pltpu.SMEM)
    vmem = pl.BlockSpec(memory_space=pltpu.VMEM)
    local = pl.pallas_call(
        functools.partial(gather_kernel, 8, rows, depth),
        in_specs=[smem, smem, vmem, vmem],
        out_specs=vmem,
        out_shape=jax.ShapeDtypeStruct((patches, groups, 8, LANES), jnp.float32),
        scratch_shapes=[pltpu.VMEM((8 * rows * (depth // LANES), LANES), jnp.float32)],
        compiler_params=pltpu.CompilerParams(vmem_limit_bytes=VMEM_LIMIT),
        cost_estimate=pl.CostEstimate(flops=10**9, bytes_accessed=32 * rows * depth, transcendentals=0),
        name="donor_gather",
    )(asked_words, asked, elastic, acoustic)
    interp = lax.all_to_all(local, "patch", split_axis=0, concat_axis=0, tiled=True)
    edges = lax.all_to_all(edges, "layer", split_axis=0, concat_axis=0, tiled=True)

    near, far_operator = near_derivatives(elastic, acoustic, cont_matrix, me, slabs)
    new_el, new_ac, opened = pl.pallas_call(
        functools.partial(section_kernel, layers, rows, depth, tile),
        grid=(rows // tile,),
        in_specs=[
            smem,
            smem,
            smem,
            pl.BlockSpec((6, tile, depth), lambda i: (0, i, 0)),
            pl.BlockSpec((1, 5, tile, depth), lambda i: (0, 0, i, 0)),
            pl.BlockSpec((1, 3, tile, depth), lambda i: (0, 0, i, 0)),
            pl.BlockSpec((1, 3, tile, depth), lambda i: (0, 0, i, 0)),
            pl.BlockSpec((1, 2, tile, depth), lambda i: (0, 0, i, 0)),
            vmem,
            vmem,
            vmem,
        ],
        out_specs=[vmem, vmem, vmem],
        out_shape=[
            jax.ShapeDtypeStruct(elastic.shape, jnp.float32),
            jax.ShapeDtypeStruct(acoustic.shape, jnp.float32),
            jax.ShapeDtypeStruct((rows, depth), jnp.float32),
        ],
        scratch_shapes=[pltpu.VMEM((rows, LANES), jnp.float32)],
        compiler_params=pltpu.CompilerParams(vmem_limit_bytes=VMEM_LIMIT),
        cost_estimate=pl.CostEstimate(
            flops=100 * rows * depth, bytes_accessed=112 * rows * depth, transcendentals=0
        ),
        name="near_section",
    )(
        fringe_cells,
        donor_counts,
        interp,
        near,
        elastic,
        acoustic,
        el_media,
        ac_media,
        edges,
        el_pair,
        ac_pair,
    )

    turn = jnp.zeros((8, LANES), jnp.float32)
    section = {"el": new_el, "ac": new_ac}
    media = {"el": el_media, "ac": ac_media}
    for value, (_, _, at, _, target, first_media, n_media, first_field, coefficients) in zip(far, pieces):
        turn, section[target] = add_far(
            section[target], far_operator, value, at,
            media[target], first_media, n_media, first_field, coefficients, opened, turn,
        )
    return section["el"], section["ac"]


def solution(mesh):
    placed = (
        P("patch", None, "line", "layer"),
        P("patch", None, "line", "layer"),
        P("patch", None, "line", "layer"),
        P("patch", None, "line", "layer"),
        P(),
        P("patch", "line", "layer", None, None),
        P("patch", "line", "layer", None, None, None),
        P("patch", "line", "layer", None, None, None),
        P("patch", "line", "layer", None),
        P("patch", "line"),
        P("patch", "line"),
    )
    return jax.shard_map(
        per_device,
        mesh=mesh,
        in_specs=placed,
        out_specs=(P("patch", None, "line", "layer"), P("patch", None, "line", "layer")),
        check_vma=False,
    )
```

```python
import functools
import math

import jax
import jax.numpy as jnp
import numpy as np
from jax import lax
from jax.experimental import pallas as pl
from jax.experimental.pallas import tpu as pltpu
from jax.sharding import PartitionSpec as P

STEP = 0.25
PENALTY = 2.0
LANES = 128
VMEM_LIMIT = 56 * 1024 * 1024
FAR_VMEM_LIMIT = 24 * 1024 * 1024
HIGHEST = lax.Precision.HIGHEST


def derivative_row(period):
    n = np.arange(1, period)
    sign = np.where(n % 2 == 0, 1.0, -1.0)
    row = np.zeros(period)
    row[1:] = (math.pi / period) * sign / np.tan(math.pi * n / period)
    return row


def operator_tables(rows, slabs, cont):
    points = rows * slabs
    period = points + cont
    row = derivative_row(period)
    j = np.arange(rows)
    own = row[(j[:, None] - j[None, :]) % period]
    far, tail = [], []
    for me in range(slabs):
        mine = me * rows + j[:, None]
        others = np.concatenate([(me - d) % slabs * rows + j for d in range(1, slabs)])
        far.append(row[(mine - others[None, :]) % period])
        tail.append(row[(mine - points - np.arange(cont)[None, :]) % period])
    return tuple(np.asarray(table, np.float32) for table in (own, far, tail))


def continuation_on(cont_matrix, rows, slabs, sources):
    match = cont_matrix.shape[1] // 2
    on_last = jnp.pad(cont_matrix[:, :match], ((0, 0), (rows - match, 0)))
    on_first = jnp.pad(cont_matrix[:, match:], ((0, 0), (0, rows - match)))
    return jnp.concatenate(
        [
            jnp.where(source == slabs - 1, on_last, 0.0) + jnp.where(source == 0, on_first, 0.0)
            for source in sources
        ],
        axis=1,
    )


def split(value, size):
    if size & (size - 1) == 0:
        return lax.shift_right_logical(value, size.bit_length() - 1), value & (size - 1)
    return lax.div(value, size), lax.rem(value, size)


def take_kernel(pieces, parts, elastic_ref, acoustic_ref, after_ref, *refs):
    del after_ref
    n = len(pieces)
    outs, held, in_semaphores, out_semaphores = refs[:n], refs[n : 2 * n], refs[-2], refs[-1]
    rows = elastic_ref.shape[2]
    loads, stores = [], []
    for i, (name, field, at, width) in enumerate(pieces):
        source = elastic_ref if name == "el" else acoustic_ref
        for part in range(parts):
            here = pl.ds(part * (rows // parts), rows // parts)
            k = i * parts + part
            loads.append(
                pltpu.make_async_copy(source.at[0, field, here, pl.ds(at, width)], held[i].at[here], in_semaphores.at[k])
            )
            stores.append(pltpu.make_async_copy(held[i].at[here], outs[i].at[here], out_semaphores.at[k]))
    for load in loads:
        load.start()
    for load, store in zip(loads, stores):
        load.wait()
        store.start()
    return stores


def take_only_kernel(pieces, parts, *refs):
    for store in take_kernel(pieces, parts, *refs):
        store.wait()


def take_and_edges_kernel(pieces, parts, layers, elastic_ref, acoustic_ref, after_ref, *refs):
    n = len(pieces)
    edges_ref, tiles, edge_semaphores = refs[n : n + 3]
    n_el, n_ac = elastic_ref.shape[1], acoustic_ref.shape[1]
    rows, depth = elastic_ref.shape[2:]
    loads = []
    for end, at in enumerate((0, depth - LANES)):
        for k, (source, first, count) in enumerate(((elastic_ref, 0, n_el), (acoustic_ref, n_el, n_ac))):
            loads.append(
                pltpu.make_async_copy(
                    source.at[0, :, :, pl.ds(at, LANES)],
                    tiles.at[end, pl.ds(first, count)],
                    edge_semaphores.at[2 * end + k],
                )
            )
    for load in loads:
        load.start()
    stores = take_kernel(pieces, parts, elastic_ref, acoustic_ref, after_ref, *refs[:n], *refs[n + 3 :])
    for load in loads:
        load.wait()
    lane = lax.broadcasted_iota(jnp.int32, (rows, LANES), 1)
    columns = jnp.zeros((rows, LANES), jnp.float32)
    for f in range(n_el + n_ac):
        columns = jnp.where(lane == f, tiles[0, f, :, 0:1], columns)
        columns = jnp.where(lane == 8 + f, tiles[1, f, :, LANES - 1 : LANES], columns)
    lines = columns.T
    below = lax.rem(lax.axis_index("layer") + 1, layers)
    for to in range(layers):
        edges_ref[to] = jnp.where(to == below, lines[8:16], lines[0:8])
    for store in stores:
        store.wait()


def take_pieces(elastic, acoustic, after, pieces, layers=0):
    rows = elastic.shape[2]
    anywhere = pl.BlockSpec(memory_space=pl.ANY)
    out_shape = [jax.ShapeDtypeStruct((rows, width), jnp.float32) for _, _, _, width in pieces]
    out_specs = [anywhere] * len(pieces)
    parts = 2 if layers else 4
    scratch = [pltpu.VMEM((rows, width), jnp.float32) for _, _, _, width in pieces]
    scratch += [pltpu.SemaphoreType.DMA((len(pieces) * parts,))] * 2
    kernel = functools.partial(take_only_kernel, pieces, parts)
    if layers:
        out_shape.append(jax.ShapeDtypeStruct((layers, 8, rows), jnp.float32))
        out_specs.append(pl.BlockSpec(memory_space=pltpu.VMEM))
        scratch = [pltpu.VMEM((2, 8, rows, LANES), jnp.float32), pltpu.SemaphoreType.DMA((4,))] + scratch
        kernel = functools.partial(take_and_edges_kernel, pieces, parts, layers)
    cells = sum(width for _, _, _, width in pieces) * rows
    return pl.pallas_call(
        kernel,
        in_specs=[anywhere] * 3,
        out_specs=out_specs,
        out_shape=out_shape,
        scratch_shapes=scratch,
        compiler_params=pltpu.CompilerParams(vmem_limit_bytes=VMEM_LIMIT),
        cost_estimate=pl.CostEstimate(flops=0, bytes_accessed=8 * cells, transcendentals=0),
        name="take_pieces",
    )(elastic, acoustic, after)


def gather_kernel(fields, rows, depth, words_ref, weights_ref, elastic_ref, acoustic_ref, out_ref, mixed):
    n_el = elastic_ref.shape[1]
    chunks = depth // LANES
    for f in range(fields):
        source = elastic_ref.at[0, f] if f < n_el else acoustic_ref.at[0, f - n_el]
        for c in range(chunks):
            mixed[pl.ds((c * fields + f) * rows, rows), :] = source[:, c * LANES : (c + 1) * LANES]
    lane = lax.broadcasted_iota(jnp.int32, (fields, LANES), 1)
    groups = out_ref.shape[1]

    def one_group(step, carry):
        patch, group = split(step, groups)

        def one_slot(r, values):
            slot = group * LANES + r
            total = None
            for s in range(4):
                start, at = split(words_ref[patch, s, slot], LANES)
                picked = mixed[pl.ds(start, fields, stride=rows), :]
                term = jnp.where(lane == at, picked * weights_ref[patch, 4 + s, slot], 0.0)
                total = term if total is None else total + term
            column = jnp.sum(total, axis=1, keepdims=True)
            return jnp.where(lane == r, column, values)

        values = lax.fori_loop(0, LANES, one_slot, jnp.zeros((fields, LANES), jnp.float32), unroll=16)
        out_ref[patch, group] = values
        return carry

    lax.fori_loop(0, out_ref.shape[0] * groups, one_group, 0)


def bf16_pair(value):
    high = value.astype(jnp.bfloat16)
    return high, (value - high.astype(jnp.float32)).astype(jnp.bfloat16)


def three_left(value):
    high, low = bf16_pair(value)
    return jnp.concatenate([high, high, low], axis=1)


def three_right(value):
    high, low = bf16_pair(value)
    return jnp.concatenate([high, low, high], axis=0)


def near_kernel(
    n_el, me_ref, own_ref, far_ref, tail_ref, own_cont_ref, far_cont_ref, elastic_ref, acoustic_ref,
    out_ref, far_operator_ref, operator,
):
    del me_ref

    @pl.when(pl.program_id(0) == 0)
    def _():
        def folded(table, cont):
            return table + jnp.dot(tail_ref[0], cont, precision=HIGHEST, preferred_element_type=jnp.float32)

        operator[...] = three_left(folded(own_ref[...], own_cont_ref[...]))
        far_operator_ref[...] = three_left(folded(far_ref[0], far_cont_ref[...]))

    value = jnp.where(pl.program_id(0) < n_el, elastic_ref[0, 0], acoustic_ref[0, 0])
    out_ref[0] = jnp.dot(operator[...], three_right(value), preferred_element_type=jnp.float32)


def near_derivatives(elastic, acoustic, cont_matrix, me, slabs):
    rows, depth = elastic.shape[2:]
    cont = cont_matrix.shape[0]
    reach = (slabs - 1) * rows
    own, far, tail = operator_tables(rows, slabs, cont)
    own_cont = continuation_on(cont_matrix, rows, slabs, [me])
    far_cont = continuation_on(cont_matrix, rows, slabs, [(me - d) % slabs for d in range(1, slabs)])
    return pl.pallas_call(
        functools.partial(near_kernel, 4),
        grid_spec=pltpu.PrefetchScalarGridSpec(
            num_scalar_prefetch=1,
            grid=(6,),
            in_specs=[
                pl.BlockSpec((rows, rows), lambda f, me: (0, 0)),
                pl.BlockSpec((1, rows, reach), lambda f, me: (me[0], 0, 0)),
                pl.BlockSpec((1, rows, cont), lambda f, me: (me[0], 0, 0)),
                pl.BlockSpec((cont, rows), lambda f, me: (0, 0)),
                pl.BlockSpec((cont, reach), lambda f, me: (0, 0)),
                pl.BlockSpec((1, 1, rows, depth), lambda f, me: (0, jnp.where(f < 3, f, 4), 0, 0)),
                pl.BlockSpec((1, 1, rows, depth), lambda f, me: (0, jnp.maximum(f - 4, 0), 0, 0)),
            ],
            out_specs=[
                pl.BlockSpec((1, rows, depth), lambda f, me: (f, 0, 0)),
                pl.BlockSpec((rows, 3 * reach), lambda f, me: (0, 0)),
            ],
            scratch_shapes=[pltpu.VMEM((rows, 3 * rows), jnp.bfloat16)],
        ),
        out_shape=[
            jax.ShapeDtypeStruct((6, rows, depth), jnp.float32),
            jax.ShapeDtypeStruct((rows, 3 * reach), jnp.bfloat16),
        ],
        compiler_params=pltpu.CompilerParams(vmem_limit_bytes=VMEM_LIMIT),
        cost_estimate=pl.CostEstimate(
            flops=36 * rows * rows * depth, bytes_accessed=60 * rows * depth, transcendentals=0
        ),
        name="near_dx",
    )(me.reshape(1), own, far, tail, own_cont, far_cont, elastic, acoustic)


def section_kernel(
    layers, rows, depth, tile,
    cells_ref, counts_ref, interp_ref,
    dx_ref, elastic_ref, acoustic_ref, el_media_ref, ac_media_ref, edges_ref, el_pair_ref, ac_pair_ref,
    new_el_ref, new_ac_ref, open_ref,
    columns,
):
    step = pl.program_id(0)
    here = pl.ds(pl.multiple_of(step * tile, tile), tile)
    lane = lax.broadcasted_iota(jnp.int32, (tile, depth), 1)
    layer = lax.axis_index("layer")
    at_top, at_bottom = layer == 0, layer == layers - 1
    from_above = edges_ref[lax.rem(layer + layers - 1, layers)]
    from_below = edges_ref[lax.rem(layer + 1, layers)]
    ocean_row = from_above[5:6]
    basin_row = from_below[1:2]

    @pl.when(step == 0)
    def _():
        pairs = jnp.concatenate([el_pair_ref[...], ac_pair_ref[...]]).astype(jnp.float32)
        lines = [
            jnp.where(at_top, 0.0, from_above),
            jnp.where(at_bottom, 0.0, from_below),
            pairs,
            jnp.zeros((LANES - 18, rows), jnp.float32),
        ]
        columns[...] = jnp.concatenate(lines).T

    halo = columns[here, :]

    def dz(value, slot):
        above = halo[:, slot : slot + 1]
        below = halo[:, 8 + slot : 9 + slot]
        following = jnp.where(lane == depth - 1, below, pltpu.roll(value, depth - 1, 1))
        previous = jnp.where(lane == 0, above, pltpu.roll(value, 1, 1))
        return (following - previous) * 0.5

    vx, vz, sxx, szz, sxz = [elastic_ref[0, f] for f in range(5)]
    p, ovx, ovz = [acoustic_ref[0, f] for f in range(3)]
    buoyancy = el_media_ref[0, 0]
    lame = el_media_ref[0, 1]
    shear = el_media_ref[0, 2]
    stiffness = lame + 2.0 * shear
    bulk = ac_media_ref[0, 0]
    ocean_buoyancy = ac_media_ref[0, 1]

    dx_vx = dx_ref[0]
    dz_vz = dz(vz, 1)
    new_el_ref[0, 0, here, :] = vx + STEP * (buoyancy * (dx_ref[2] + dz(sxz, 4)))
    new_el_ref[0, 1, here, :] = vz + STEP * (buoyancy * (dx_ref[3] + dz(szz, 3)))
    new_el_ref[0, 2, here, :] = sxx + STEP * (stiffness * dx_vx + lame * dz_vz)
    choose = lax.broadcasted_iota(jnp.int32, (tile, rows), 1).astype(jnp.float32)
    pressure = jnp.sum(jnp.where(halo[:, 16:17] == choose, ocean_row, 0.0), axis=1, keepdims=True)
    velocity = jnp.sum(jnp.where(halo[:, 17:18] == choose, basin_row, 0.0), axis=1, keepdims=True)
    rate_szz = lame * dx_vx + stiffness * dz_vz
    rate_szz = rate_szz + jnp.where((lane == 0) & at_top, PENALTY * (-pressure - szz), 0.0)
    new_el_ref[0, 3, here, :] = szz + STEP * rate_szz
    new_el_ref[0, 4, here, :] = sxz + STEP * (shear * (dz(vx, 0) + dx_ref[1]))
    new_ac_ref[0, 0, here, :] = p - STEP * (bulk * (dx_ref[5] + dz(ovz, 7)))
    new_ac_ref[0, 1, here, :] = ovx - STEP * (ocean_buoyancy * dx_ref[4])
    rate_ovz = -ocean_buoyancy * dz(p, 5)
    rate_ovz = rate_ovz + jnp.where((lane == depth - 1) & at_bottom, PENALTY * (velocity - ovz), 0.0)
    new_ac_ref[0, 2, here, :] = ovz + STEP * rate_ovz
    open_ref[here, :] = jnp.ones((tile, depth), jnp.float32)

    @pl.when(step == pl.num_programs(0) - 1)
    def _():
        place = lax.broadcasted_iota(jnp.int32, (8, LANES), 0) * LANES
        place = place + lax.broadcasted_iota(jnp.int32, (8, LANES), 1)
        n_el = new_el_ref.shape[1]

        def one_patch(q, carry):
            def one_slot(r, inner):
                x, z = split(cells_ref[0, 0, 0, q, r], depth)
                (high, row), (low, at) = split(x, 8), split(z, LANES)
                at_row = pl.ds(pl.multiple_of(high * 8, 8), 8)
                at_lane = pl.ds(pl.multiple_of(low * LANES, LANES), LANES)
                hit = place == row * LANES + at
                group, within = split(r, LANES)
                for f in range(8):
                    target = new_el_ref.at[0, f] if f < n_el else new_ac_ref.at[0, f - n_el]
                    target[at_row, at_lane] = jnp.where(hit, interp_ref[q, group, f, within], target[at_row, at_lane])
                open_ref[at_row, at_lane] = jnp.where(hit, 0.0, open_ref[at_row, at_lane])
                return inner

            return lax.fori_loop(0, counts_ref[0, 0, 0, q], one_slot, carry)

        lax.fori_loop(0, counts_ref.shape[3], one_patch, 0)


def far_kernel(coefficients, turn_ref, d_ref, far_ref, media_ref, open_ref, base_ref, next_ref, out_ref):
    del turn_ref, next_ref
    far = jnp.dot(d_ref[...], three_right(far_ref[...]), preferred_element_type=jnp.float32)
    media = [media_ref[0, i] for i in range(media_ref.shape[1])]
    is_open = open_ref[...] > 0.5
    for i, coefficient in enumerate(coefficients):
        old = base_ref[0, i]
        out_ref[0, i] = jnp.where(is_open, old + (STEP * coefficient(*media)) * far, old)


def add_far(base, operator, far, at, media, first_media, n_media, first_field, coefficients, opened, turn):
    rows, reach = operator.shape[0], far.shape[0]
    width = far.shape[1]
    tile = math.gcd(math.gcd(width, at), 2 * LANES)
    n_out = len(coefficients)
    shift = at // tile
    return pl.pallas_call(
        functools.partial(far_kernel, coefficients),
        grid=(width // tile,),
        in_specs=[
            pl.BlockSpec(memory_space=pl.ANY),
            pl.BlockSpec((rows, 3 * reach), lambda i: (0, 0)),
            pl.BlockSpec((reach, tile), lambda i: (0, i)),
            pl.BlockSpec((1, n_media, rows, tile), lambda i: (0, first_media // n_media, 0, i + shift)),
            pl.BlockSpec((rows, tile), lambda i: (0, i + shift)),
            pl.BlockSpec((1, n_out, rows, tile), lambda i: (0, first_field // n_out, 0, i + shift)),
        ],
        out_specs=[
            pl.BlockSpec(memory_space=pl.ANY),
            pl.BlockSpec((1, n_out, rows, tile), lambda i: (0, first_field // n_out, 0, i + shift)),
        ],
        out_shape=[
            jax.ShapeDtypeStruct(turn.shape, turn.dtype),
            jax.ShapeDtypeStruct(base.shape, base.dtype),
        ],
        input_output_aliases={0: 0, 5: 1},
        compiler_params=pltpu.CompilerParams(vmem_limit_bytes=FAR_VMEM_LIMIT),
        cost_estimate=pl.CostEstimate(
            flops=6 * rows * reach * width,
            bytes_accessed=4 * rows * width * (3 + n_media + n_out),
            transcendentals=0,
        ),
        name="add_far",
    )(turn, operator, far, media, opened, base)


def per_device(
    elastic,
    acoustic,
    el_media,
    ac_media,
    cont_matrix,
    fringe_cells,
    donor_cells,
    donor_weights,
    donor_counts,
    el_pair,
    ac_pair,
):
    rows, depth = elastic.shape[2], elastic.shape[3]
    slabs = lax.axis_size("line")
    layers = lax.axis_size("layer")
    patches = lax.axis_size("patch")
    slots = fringe_cells.shape[-1]
    groups = slots // LANES
    me = lax.axis_index("line")
    layer = lax.axis_index("layer")
    tile = min(64, rows)

    def other_slabs(value):
        parts = [
            lax.ppermute(value, "line", [(i, (i + distance) % slabs) for i in range(slabs)])
            for distance in range(1, slabs)
        ]
        return parts[0] if slabs == 2 else jnp.concatenate(parts, axis=0)

    half, quarter = depth // 2, depth // 4
    pieces = [
        ("el", 0, 0, depth, "el", 0, 3, 2, (lambda b, l, m: l + 2.0 * m, lambda b, l, m: l)),
        ("ac", 0, 0, depth, "ac", 1, 1, 1, (lambda b: -b,)),
        ("ac", 1, 0, depth, "ac", 0, 1, 0, (lambda k: -k,)),
        ("el", 1, 0, depth, "el", 2, 1, 4, (lambda m: m,)),
        ("el", 2, 0, depth, "el", 0, 1, 0, (lambda b: b,)),
        ("el", 4, 0, half, "el", 0, 1, 1, (lambda b: b,)),
        ("el", 4, half, quarter, "el", 0, 1, 1, (lambda b: b,)),
        ("el", 4, half + quarter, quarter, "el", 0, 1, 1, (lambda b: b,)),
    ]
    travelling = [piece[:4] for piece in pieces]
    (first,) = take_pieces(elastic, acoustic, cont_matrix, travelling[:1])
    *others, edges = take_pieces(elastic, acoustic, first, travelling[1:], layers)
    far = [other_slabs(value) for value in [first, *others]]

    x, z = split(donor_cells[0, 0, 0], depth)
    chunk, at_lane = split(z, LANES)
    words = (chunk * (8 * rows) + x) * LANES + at_lane
    asked = jnp.concatenate([words.astype(jnp.float32), donor_weights[0, 0, 0]], axis=1)
    asked = lax.all_to_all(asked, "patch", split_axis=0, concat_axis=0, tiled=True)
    asked_words = asked[:, :4].astype(jnp.int32)

    smem = pl.BlockSpec(memory_space=pltpu.SMEM)
    vmem = pl.BlockSpec(memory_space=pltpu.VMEM)
    local = pl.pallas_call(
        functools.partial(gather_kernel, 8, rows, depth),
        in_specs=[smem, smem, vmem, vmem],
        out_specs=vmem,
        out_shape=jax.ShapeDtypeStruct((patches, groups, 8, LANES), jnp.float32),
        scratch_shapes=[pltpu.VMEM((8 * rows * (depth // LANES), LANES), jnp.float32)],
        compiler_params=pltpu.CompilerParams(vmem_limit_bytes=VMEM_LIMIT),
        cost_estimate=pl.CostEstimate(flops=10**9, bytes_accessed=32 * rows * depth, transcendentals=0),
        name="donor_gather",
    )(asked_words, asked, elastic, acoustic)
    interp = lax.all_to_all(local, "patch", split_axis=0, concat_axis=0, tiled=True)
    edges = lax.all_to_all(edges, "layer", split_axis=0, concat_axis=0, tiled=True)

    near, far_operator = near_derivatives(elastic, acoustic, cont_matrix, me, slabs)
    new_el, new_ac, opened = pl.pallas_call(
        functools.partial(section_kernel, layers, rows, depth, tile),
        grid=(rows // tile,),
        in_specs=[
            smem,
            smem,
            smem,
            pl.BlockSpec((6, tile, depth), lambda i: (0, i, 0)),
            pl.BlockSpec((1, 5, tile, depth), lambda i: (0, 0, i, 0)),
            pl.BlockSpec((1, 3, tile, depth), lambda i: (0, 0, i, 0)),
            pl.BlockSpec((1, 3, tile, depth), lambda i: (0, 0, i, 0)),
            pl.BlockSpec((1, 2, tile, depth), lambda i: (0, 0, i, 0)),
            vmem,
            vmem,
            vmem,
        ],
        out_specs=[vmem, vmem, vmem],
        out_shape=[
            jax.ShapeDtypeStruct(elastic.shape, jnp.float32),
            jax.ShapeDtypeStruct(acoustic.shape, jnp.float32),
            jax.ShapeDtypeStruct((rows, depth), jnp.float32),
        ],
        scratch_shapes=[pltpu.VMEM((rows, LANES), jnp.float32)],
        compiler_params=pltpu.CompilerParams(vmem_limit_bytes=VMEM_LIMIT),
        cost_estimate=pl.CostEstimate(
            flops=100 * rows * depth, bytes_accessed=112 * rows * depth, transcendentals=0
        ),
        name="near_section",
    )(
        fringe_cells,
        donor_counts,
        interp,
        near,
        elastic,
        acoustic,
        el_media,
        ac_media,
        edges,
        el_pair,
        ac_pair,
    )

    turn = jnp.zeros((8, LANES), jnp.float32)
    section = {"el": new_el, "ac": new_ac}
    media = {"el": el_media, "ac": ac_media}
    for value, (_, _, at, _, target, first_media, n_media, first_field, coefficients) in zip(far, pieces):
        turn, section[target] = add_far(
            section[target], far_operator, value, at,
            media[target], first_media, n_media, first_field, coefficients, opened, turn,
        )
    return section["el"], section["ac"]


def solution(mesh):
    placed = (
        P("patch", None, "line", "layer"),
        P("patch", None, "line", "layer"),
        P("patch", None, "line", "layer"),
        P("patch", None, "line", "layer"),
        P(),
        P("patch", "line", "layer", None, None),
        P("patch", "line", "layer", None, None, None),
        P("patch", "line", "layer", None, None, None),
        P("patch", "line", "layer", None),
        P("patch", "line"),
        P("patch", "line"),
    )
    return jax.shard_map(
        per_device,
        mesh=mesh,
        in_specs=placed,
        out_specs=(P("patch", None, "line", "layer"), P("patch", None, "line", "layer")),
        check_vma=False,
    )
```

```python
import functools
import math

import jax
import jax.numpy as jnp
import numpy as np
from jax import lax
from jax.experimental import pallas as pl
from jax.experimental.pallas import tpu as pltpu
from jax.sharding import PartitionSpec as P

STEP = 0.25
PENALTY = 2.0
LANES = 128
MIB = 1024 * 1024
HIGHEST = lax.Precision.HIGHEST


def derivative_row(period):
    n = np.arange(1, period)
    sign = np.where(n % 2 == 0, 1.0, -1.0)
    row = np.zeros(period)
    row[1:] = (math.pi / period) * sign / np.tan(math.pi * n / period)
    return row


def operator_tables(rows, slabs, cont):
    points = rows * slabs
    period = points + cont
    row = derivative_row(period)
    j = np.arange(rows)
    own = row[(j[:, None] - j[None, :]) % period]
    far, sent, tail = [], [], []
    for me in range(slabs):
        mine = me * rows + j[:, None]
        others = np.concatenate([(me - d) % slabs * rows + j for d in range(1, slabs)])
        far.append(row[(mine - others[None, :]) % period])
        toward = np.concatenate([(me + d) % slabs * rows + j for d in range(1, slabs)])
        sent.append(row[(toward[:, None] - me * rows - j[None, :]) % period])
        tail.append(row[(mine - points - np.arange(cont)[None, :]) % period])
    return tuple(np.asarray(table, np.float32) for table in (own, far, sent, tail))


def continuation_on(cont_matrix, rows, slabs, sources):
    match = cont_matrix.shape[1] // 2
    on_last = jnp.pad(cont_matrix[:, :match], ((0, 0), (rows - match, 0)))
    on_first = jnp.pad(cont_matrix[:, match:], ((0, 0), (0, rows - match)))
    return jnp.concatenate(
        [
            jnp.where(source == slabs - 1, on_last, 0.0) + jnp.where(source == 0, on_first, 0.0)
            for source in sources
        ],
        axis=1,
    )


def split(value, size):
    if size & (size - 1) == 0:
        return lax.shift_right_logical(value, size.bit_length() - 1), value & (size - 1)
    return lax.div(value, size), lax.rem(value, size)


def take_kernel(pieces, elastic_ref, acoustic_ref, outs, semaphores):
    copies = []
    for i, (name, field, at, width) in enumerate(pieces):
        source = elastic_ref if name == "el" else acoustic_ref
        copies.append(pltpu.make_async_copy(source.at[0, field, :, pl.ds(at, width)], outs[i], semaphores.at[i]))
    for copy in copies:
        copy.start()
    return copies


def take_only_kernel(pieces, elastic_ref, *refs):
    for copy in take_kernel(pieces, elastic_ref, None, refs[:-1], refs[-1]):
        copy.wait()


def take_and_edges_kernel(pieces, layers, after_ref, elastic_ref, acoustic_ref, *refs):
    del after_ref
    edges_ref, tiles, edge_semaphores, semaphores = refs[len(pieces) :]
    n_el, n_ac = elastic_ref.shape[1], acoustic_ref.shape[1]
    rows, depth = elastic_ref.shape[2:]
    loads = []
    for end, at in enumerate((0, depth - LANES)):
        for k, (source, first, count) in enumerate(((elastic_ref, 0, n_el), (acoustic_ref, n_el, n_ac))):
            loads.append(
                pltpu.make_async_copy(
                    source.at[0, :, :, pl.ds(at, LANES)],
                    tiles.at[end, pl.ds(first, count)],
                    edge_semaphores.at[2 * end + k],
                )
            )
    copies = take_kernel(pieces, elastic_ref, acoustic_ref, refs[: len(pieces)], semaphores)
    for load in loads:
        load.start()
    for load in loads:
        load.wait()
    lane = lax.broadcasted_iota(jnp.int32, (rows, LANES), 1)
    columns = jnp.zeros((rows, LANES), jnp.float32)
    for f in range(n_el + n_ac):
        columns = jnp.where(lane == f, tiles[0, f, :, 0:1], columns)
        columns = jnp.where(lane == 8 + f, tiles[1, f, :, LANES - 1 : LANES], columns)
    lines = columns.T
    below = lax.rem(lax.axis_index("layer") + 1, layers)
    for to in range(layers):
        edges_ref[to] = jnp.where(to == below, lines[8:16], lines[0:8])
    for copy in copies:
        copy.wait()


def take_pieces(elastic, acoustic, pieces, after=None, layers=0):
    rows = elastic.shape[2]
    anywhere = pl.BlockSpec(memory_space=pl.ANY)
    vmem = pl.BlockSpec(memory_space=pltpu.VMEM)
    out_shape = [jax.ShapeDtypeStruct((rows, width), jnp.float32) for _, _, _, width in pieces]
    scratch = [pltpu.SemaphoreType.DMA((len(pieces),))]
    kernel, operands = functools.partial(take_only_kernel, pieces), (elastic,)
    if layers:
        out_shape.append(jax.ShapeDtypeStruct((layers, 8, rows), jnp.float32))
        scratch = [pltpu.VMEM((2, 8, rows, LANES), jnp.float32), pltpu.SemaphoreType.DMA((4,))] + scratch
        kernel, operands = functools.partial(take_and_edges_kernel, pieces, layers), (after, elastic, acoustic)
    cells = sum(width for _, _, _, width in pieces) * rows
    return pl.pallas_call(
        kernel,
        in_specs=[anywhere] * len(operands),
        out_specs=[vmem] * len(out_shape),
        out_shape=out_shape,
        scratch_shapes=scratch,
        compiler_params=pltpu.CompilerParams(vmem_limit_bytes=(14 if layers else 60) * MIB),
        cost_estimate=pl.CostEstimate(flops=0, bytes_accessed=8 * cells, transcendentals=0),
        name="take_pieces",
    )(*operands)


def gather_kernel(fields, rows, depth, words_ref, weights_ref, elastic_ref, acoustic_ref, out_ref, mixed):
    n_el = elastic_ref.shape[1]
    chunks = depth // LANES
    for f in range(fields):
        source = elastic_ref.at[0, f] if f < n_el else acoustic_ref.at[0, f - n_el]
        for c in range(chunks):
            mixed[pl.ds((c * fields + f) * rows, rows), :] = source[:, c * LANES : (c + 1) * LANES]
    lane = lax.broadcasted_iota(jnp.int32, (fields, LANES), 1)
    groups = out_ref.shape[1]

    def one_group(step, carry):
        patch, group = split(step, groups)

        def one_slot(r, values):
            slot = group * LANES + r
            total = None
            for s in range(4):
                start, at = split(words_ref[patch, s, slot], LANES)
                picked = mixed[pl.ds(start, fields, stride=rows), :]
                term = jnp.where(lane == at, picked * weights_ref[patch, 4 + s, slot], 0.0)
                total = term if total is None else total + term
            column = jnp.sum(total, axis=1, keepdims=True)
            return jnp.where(lane == r, column, values)

        values = lax.fori_loop(0, LANES, one_slot, jnp.zeros((fields, LANES), jnp.float32), unroll=16)
        out_ref[patch, group] = values
        return carry

    lax.fori_loop(0, out_ref.shape[0] * groups, one_group, 0)


def bf16_pair(value):
    high = value.astype(jnp.bfloat16)
    return high, (value - high.astype(jnp.float32)).astype(jnp.bfloat16)


def three_left(value):
    high, low = bf16_pair(value)
    return jnp.concatenate([high, high, low], axis=1)


def three_right(value):
    high, low = bf16_pair(value)
    return jnp.concatenate([high, low, high], axis=0)


def near_kernel(
    n_el, me_ref, own_ref, far_ref, tail_ref, own_cont_ref, far_cont_ref, elastic_ref, acoustic_ref,
    out_ref, far_operator_ref, operator,
):
    del me_ref

    @pl.when(pl.program_id(0) == 0)
    def _():
        def folded(table, cont):
            return table + jnp.dot(tail_ref[0], cont, precision=HIGHEST, preferred_element_type=jnp.float32)

        operator[...] = three_left(folded(own_ref[...], own_cont_ref[...]))
        far_operator_ref[...] = three_left(folded(far_ref[0], far_cont_ref[...]))

    value = jnp.where(pl.program_id(0) < n_el, elastic_ref[0, 0], acoustic_ref[0, 0])
    out_ref[0] = jnp.dot(operator[...], three_right(value), preferred_element_type=jnp.float32)


def near_derivatives(elastic, acoustic, cont_matrix, tables, me, slabs):
    rows, depth = elastic.shape[2:]
    cont = cont_matrix.shape[0]
    reach = (slabs - 1) * rows
    own, far, _, tail = tables
    own_cont = continuation_on(cont_matrix, rows, slabs, [me])
    far_cont = continuation_on(cont_matrix, rows, slabs, [(me - d) % slabs for d in range(1, slabs)])
    return pl.pallas_call(
        functools.partial(near_kernel, 4),
        grid_spec=pltpu.PrefetchScalarGridSpec(
            num_scalar_prefetch=1,
            grid=(6,),
            in_specs=[
                pl.BlockSpec((rows, rows), lambda f, me: (0, 0)),
                pl.BlockSpec((1, rows, reach), lambda f, me: (me[0], 0, 0)),
                pl.BlockSpec((1, rows, cont), lambda f, me: (me[0], 0, 0)),
                pl.BlockSpec((cont, rows), lambda f, me: (0, 0)),
                pl.BlockSpec((cont, reach), lambda f, me: (0, 0)),
                pl.BlockSpec((1, 1, rows, depth), lambda f, me: (0, jnp.where(f < 3, f, 4), 0, 0)),
                pl.BlockSpec((1, 1, rows, depth), lambda f, me: (0, jnp.maximum(f - 4, 0), 0, 0)),
            ],
            out_specs=[
                pl.BlockSpec((1, rows, depth), lambda f, me: (f, 0, 0)),
                pl.BlockSpec((rows, 3 * reach), lambda f, me: (0, 0)),
            ],
            scratch_shapes=[pltpu.VMEM((rows, 3 * rows), jnp.bfloat16)],
        ),
        out_shape=[
            jax.ShapeDtypeStruct((6, rows, depth), jnp.float32),
            jax.ShapeDtypeStruct((rows, 3 * reach), jnp.bfloat16),
        ],
        compiler_params=pltpu.CompilerParams(vmem_limit_bytes=28 * MIB),
        cost_estimate=pl.CostEstimate(
            flops=36 * rows * rows * depth, bytes_accessed=60 * rows * depth, transcendentals=0
        ),
        name="near_dx",
    )(me.reshape(1), own, far, tail, own_cont, far_cont, elastic, acoustic)


def sent_kernel(rows, me_ref, turn_ref, sent_ref, tail_ref, cont_ref, piece_ref, out_ref):
    del turn_ref
    me, slabs = me_ref[0], tail_ref.shape[0]
    value = three_right(piece_ref[...])
    for d in range(1, slabs):
        here = pl.ds((d - 1) * rows, rows)
        tail = tail_ref[lax.rem(me + d, slabs)]
        block = sent_ref[0, here, :] + jnp.dot(
            tail, cont_ref[...], precision=HIGHEST, preferred_element_type=jnp.float32
        )
        out_ref[here, :] = jnp.dot(three_left(block), value, preferred_element_type=jnp.float32)


def sent_products(piece, cont_matrix, tables, me, slabs, turn):
    rows, width = piece.shape
    cont = cont_matrix.shape[0]
    reach = (slabs - 1) * rows
    _, _, sent, tail = tables
    return pl.pallas_call(
        functools.partial(sent_kernel, rows),
        grid_spec=pltpu.PrefetchScalarGridSpec(
            num_scalar_prefetch=1,
            grid=(1,),
            in_specs=[
                pl.BlockSpec(memory_space=pl.ANY),
                pl.BlockSpec((1, reach, rows), lambda i, me: (me[0], 0, 0)),
                pl.BlockSpec((slabs, rows, cont), lambda i, me: (0, 0, 0)),
                pl.BlockSpec((cont, rows), lambda i, me: (0, 0)),
                pl.BlockSpec((rows, width), lambda i, me: (0, 0)),
            ],
            out_specs=pl.BlockSpec((reach, width), lambda i, me: (0, 0)),
        ),
        out_shape=jax.ShapeDtypeStruct((reach, width), jnp.float32),
        compiler_params=pltpu.CompilerParams(vmem_limit_bytes=16 * MIB),
        cost_estimate=pl.CostEstimate(
            flops=6 * rows * reach * width, bytes_accessed=4 * rows * reach, transcendentals=0
        ),
        name="sent_products",
    )(me.reshape(1), turn, sent, tail, continuation_on(cont_matrix, rows, slabs, [me]), piece)


def section_kernel(
    layers, rows, depth, tile,
    cells_ref, counts_ref, interp_ref,
    dx_ref, elastic_ref, acoustic_ref, el_media_ref, ac_media_ref, edges_ref, el_pair_ref, ac_pair_ref,
    new_el_ref, new_ac_ref, open_ref,
    columns,
):
    step = pl.program_id(0)
    here = pl.ds(pl.multiple_of(step * tile, tile), tile)
    lane = lax.broadcasted_iota(jnp.int32, (tile, depth), 1)
    layer = lax.axis_index("layer")
    at_top, at_bottom = layer == 0, layer == layers - 1
    from_above = edges_ref[lax.rem(layer + layers - 1, layers)]
    from_below = edges_ref[lax.rem(layer + 1, layers)]
    ocean_row = from_above[5:6]
    basin_row = from_below[1:2]

    @pl.when(step == 0)
    def _():
        pairs = jnp.concatenate([el_pair_ref[...], ac_pair_ref[...]]).astype(jnp.float32)
        lines = [
            jnp.where(at_top, 0.0, from_above),
            jnp.where(at_bottom, 0.0, from_below),
            pairs,
            jnp.zeros((LANES - 18, rows), jnp.float32),
        ]
        columns[...] = jnp.concatenate(lines).T

    halo = columns[here, :]

    def dz(value, slot):
        above = halo[:, slot : slot + 1]
        below = halo[:, 8 + slot : 9 + slot]
        following = jnp.where(lane == depth - 1, below, pltpu.roll(value, depth - 1, 1))
        previous = jnp.where(lane == 0, above, pltpu.roll(value, 1, 1))
        return (following - previous) * 0.5

    vx, vz, sxx, szz, sxz = [elastic_ref[0, f] for f in range(5)]
    p, ovx, ovz = [acoustic_ref[0, f] for f in range(3)]
    buoyancy = el_media_ref[0, 0]
    lame = el_media_ref[0, 1]
    shear = el_media_ref[0, 2]
    stiffness = lame + 2.0 * shear
    bulk = ac_media_ref[0, 0]
    ocean_buoyancy = ac_media_ref[0, 1]

    dx_vx = dx_ref[0]
    dz_vz = dz(vz, 1)
    new_el_ref[0, 0, here, :] = vx + STEP * (buoyancy * (dx_ref[2] + dz(sxz, 4)))
    new_el_ref[0, 1, here, :] = vz + STEP * (buoyancy * (dx_ref[3] + dz(szz, 3)))
    new_el_ref[0, 2, here, :] = sxx + STEP * (stiffness * dx_vx + lame * dz_vz)
    choose = lax.broadcasted_iota(jnp.int32, (tile, rows), 1).astype(jnp.float32)
    pressure = jnp.sum(jnp.where(halo[:, 16:17] == choose, ocean_row, 0.0), axis=1, keepdims=True)
    velocity = jnp.sum(jnp.where(halo[:, 17:18] == choose, basin_row, 0.0), axis=1, keepdims=True)
    rate_szz = lame * dx_vx + stiffness * dz_vz
    rate_szz = rate_szz + jnp.where((lane == 0) & at_top, PENALTY * (-pressure - szz), 0.0)
    new_el_ref[0, 3, here, :] = szz + STEP * rate_szz
    new_el_ref[0, 4, here, :] = sxz + STEP * (shear * (dz(vx, 0) + dx_ref[1]))
    new_ac_ref[0, 0, here, :] = p - STEP * (bulk * (dx_ref[5] + dz(ovz, 7)))
    new_ac_ref[0, 1, here, :] = ovx - STEP * (ocean_buoyancy * dx_ref[4])
    rate_ovz = -ocean_buoyancy * dz(p, 5)
    rate_ovz = rate_ovz + jnp.where((lane == depth - 1) & at_bottom, PENALTY * (velocity - ovz), 0.0)
    new_ac_ref[0, 2, here, :] = ovz + STEP * rate_ovz
    open_ref[here, :] = jnp.ones((tile, depth), jnp.float32)

    @pl.when(step == pl.num_programs(0) - 1)
    def _():
        place = lax.broadcasted_iota(jnp.int32, (8, LANES), 0) * LANES
        place = place + lax.broadcasted_iota(jnp.int32, (8, LANES), 1)
        n_el = new_el_ref.shape[1]

        def one_patch(q, carry):
            def one_slot(r, inner):
                x, z = split(cells_ref[0, 0, 0, q, r], depth)
                (high, row), (low, at) = split(x, 8), split(z, LANES)
                at_row = pl.ds(pl.multiple_of(high * 8, 8), 8)
                at_lane = pl.ds(pl.multiple_of(low * LANES, LANES), LANES)
                hit = place == row * LANES + at
                group, within = split(r, LANES)
                for f in range(8):
                    target = new_el_ref.at[0, f] if f < n_el else new_ac_ref.at[0, f - n_el]
                    target[at_row, at_lane] = jnp.where(hit, interp_ref[q, group, f, within], target[at_row, at_lane])
                open_ref[at_row, at_lane] = jnp.where(hit, 0.0, open_ref[at_row, at_lane])
                return inner

            return lax.fori_loop(0, counts_ref[0, 0, 0, q], one_slot, carry)

        lax.fori_loop(0, counts_ref.shape[3], one_patch, 0)


def far_kernel(coefficients, turn_ref, d_ref, far_ref, media_ref, open_ref, base_ref, next_ref, out_ref):
    del turn_ref, next_ref
    far = jnp.dot(d_ref[...], three_right(far_ref[...]), preferred_element_type=jnp.float32)
    media = [media_ref[0, i] for i in range(media_ref.shape[1])]
    is_open = open_ref[...] > 0.5
    for i, coefficient in enumerate(coefficients):
        old = base_ref[0, i]
        out_ref[0, i] = jnp.where(is_open, old + (STEP * coefficient(*media)) * far, old)


def add_far(base, operator, far, at, media, first_media, n_media, first_field, coefficients, opened, turn):
    rows, reach = operator.shape[0], far.shape[0]
    width = far.shape[1]
    tile = math.gcd(math.gcd(width, at), 2 * LANES)
    n_out = len(coefficients)
    shift = at // tile
    return pl.pallas_call(
        functools.partial(far_kernel, coefficients),
        grid=(width // tile,),
        in_specs=[
            pl.BlockSpec(memory_space=pl.ANY),
            pl.BlockSpec((rows, 3 * reach), lambda i: (0, 0)),
            pl.BlockSpec((reach, tile), lambda i: (0, i)),
            pl.BlockSpec((1, n_media, rows, tile), lambda i: (0, first_media // n_media, 0, i + shift)),
            pl.BlockSpec((rows, tile), lambda i: (0, i + shift)),
            pl.BlockSpec((1, n_out, rows, tile), lambda i: (0, first_field // n_out, 0, i + shift)),
        ],
        out_specs=[
            pl.BlockSpec(memory_space=pl.ANY),
            pl.BlockSpec((1, n_out, rows, tile), lambda i: (0, first_field // n_out, 0, i + shift)),
        ],
        out_shape=[
            jax.ShapeDtypeStruct(turn.shape, turn.dtype),
            jax.ShapeDtypeStruct(base.shape, base.dtype),
        ],
        input_output_aliases={0: 0, 5: 1},
        compiler_params=pltpu.CompilerParams(vmem_limit_bytes=20 * MIB),
        cost_estimate=pl.CostEstimate(
            flops=6 * rows * reach * width,
            bytes_accessed=4 * rows * width * (3 + n_media + n_out),
            transcendentals=0,
        ),
        name="add_far",
    )(turn, operator, far, media, opened, base)


def per_device(
    elastic,
    acoustic,
    el_media,
    ac_media,
    cont_matrix,
    fringe_cells,
    donor_cells,
    donor_weights,
    donor_counts,
    el_pair,
    ac_pair,
):
    rows, depth = elastic.shape[2], elastic.shape[3]
    slabs = lax.axis_size("line")
    layers = lax.axis_size("layer")
    patches = lax.axis_size("patch")
    slots = fringe_cells.shape[-1]
    groups = slots // LANES
    me = lax.axis_index("line")
    layer = lax.axis_index("layer")
    tile = min(64, rows)

    def other_slabs(value):
        parts = [
            lax.ppermute(value, "line", [(i, (i + distance) % slabs) for i in range(slabs)])
            for distance in range(1, slabs)
        ]
        return parts[0] if slabs == 2 else jnp.concatenate(parts, axis=0)

    half, quarter = depth // 2, depth // 4
    pieces = [
        ("el", 0, 0, depth, "el", 0, 3, 2, (lambda b, l, m: l + 2.0 * m, lambda b, l, m: l)),
        ("ac", 0, 0, depth, "ac", 1, 1, 1, (lambda b: -b,)),
        ("ac", 1, 0, depth, "ac", 0, 1, 0, (lambda k: -k,)),
        ("el", 1, 0, depth, "el", 2, 1, 4, (lambda m: m,)),
        ("el", 2, 0, depth, "el", 0, 1, 0, (lambda b: b,)),
        ("el", 4, 0, half, "el", 0, 1, 1, (lambda b: b,)),
        ("el", 4, half, quarter, "el", 0, 1, 1, (lambda b: b,)),
        ("el", 4, half + quarter, quarter, "el", 0, 1, 1, (lambda b: b,)),
    ]
    travelling = [piece[:4] for piece in pieces]
    (first,) = take_pieces(elastic, acoustic, travelling[:1])
    *others, last, edges = take_pieces(elastic, acoustic, travelling[1:], first, layers)
    far = [other_slabs(value) for value in [first, *others]]
    tables = operator_tables(rows, slabs, cont_matrix.shape[0])

    x, z = split(donor_cells[0, 0, 0], depth)
    chunk, at_lane = split(z, LANES)
    words = (chunk * (8 * rows) + x) * LANES + at_lane
    asked = jnp.concatenate([words.astype(jnp.float32), donor_weights[0, 0, 0]], axis=1)
    asked = lax.all_to_all(asked, "patch", split_axis=0, concat_axis=0, tiled=True)
    asked_words = asked[:, :4].astype(jnp.int32)

    smem = pl.BlockSpec(memory_space=pltpu.SMEM)
    vmem = pl.BlockSpec(memory_space=pltpu.VMEM)
    local = pl.pallas_call(
        functools.partial(gather_kernel, 8, rows, depth),
        in_specs=[smem, smem, vmem, vmem],
        out_specs=vmem,
        out_shape=jax.ShapeDtypeStruct((patches, groups, 8, LANES), jnp.float32),
        scratch_shapes=[pltpu.VMEM((8 * rows * (depth // LANES), LANES), jnp.float32)],
        compiler_params=pltpu.CompilerParams(vmem_limit_bytes=24 * MIB),
        cost_estimate=pl.CostEstimate(flops=10**9, bytes_accessed=32 * rows * depth, transcendentals=0),
        name="donor_gather",
    )(asked_words, asked, elastic, acoustic)
    interp = lax.all_to_all(local, "patch", split_axis=0, concat_axis=0, tiled=True)
    edges = lax.all_to_all(edges, "layer", split_axis=0, concat_axis=0, tiled=True)

    near, far_operator = near_derivatives(elastic, acoustic, cont_matrix, tables, me, slabs)
    new_el, new_ac, opened = pl.pallas_call(
        functools.partial(section_kernel, layers, rows, depth, tile),
        grid=(rows // tile,),
        in_specs=[
            smem,
            smem,
            smem,
            pl.BlockSpec((6, tile, depth), lambda i: (0, i, 0)),
            pl.BlockSpec((1, 5, tile, depth), lambda i: (0, 0, i, 0)),
            pl.BlockSpec((1, 3, tile, depth), lambda i: (0, 0, i, 0)),
            pl.BlockSpec((1, 3, tile, depth), lambda i: (0, 0, i, 0)),
            pl.BlockSpec((1, 2, tile, depth), lambda i: (0, 0, i, 0)),
            vmem,
            vmem,
            vmem,
        ],
        out_specs=[vmem, vmem, vmem],
        out_shape=[
            jax.ShapeDtypeStruct(elastic.shape, jnp.float32),
            jax.ShapeDtypeStruct(acoustic.shape, jnp.float32),
            jax.ShapeDtypeStruct((rows, depth), jnp.float32),
        ],
        scratch_shapes=[pltpu.VMEM((rows, LANES), jnp.float32)],
        compiler_params=pltpu.CompilerParams(vmem_limit_bytes=28 * MIB),
        cost_estimate=pl.CostEstimate(
            flops=100 * rows * depth, bytes_accessed=112 * rows * depth, transcendentals=0
        ),
        name="near_section",
    )(
        fringe_cells,
        donor_counts,
        interp,
        near,
        elastic,
        acoustic,
        el_media,
        ac_media,
        edges,
        el_pair,
        ac_pair,
    )

    turn = jnp.zeros((8, LANES), jnp.float32)
    section = {"el": new_el, "ac": new_ac}
    media = {"el": el_media, "ac": ac_media}
    turns = []
    for value, (_, _, at, _, target, first_media, n_media, first_field, coefficients) in zip(far, pieces):
        turn, section[target] = add_far(
            section[target], far_operator, value, at,
            media[target], first_media, n_media, first_field, coefficients, opened, turn,
        )
        turns.append(turn)
    products = sent_products(last, cont_matrix, tables, me, slabs, turns[2])
    products = [
        lax.ppermute(
            lax.slice_in_dim(products, (d - 1) * rows, d * rows),
            "line",
            [(i, (i + d) % slabs) for i in range(slabs)],
        )
        for d in range(1, slabs)
    ]

    _, _, at, width, target, first_media, _, first_field, (coefficient,) = pieces[-1]
    corner = (0, first_field, 0, at)
    old = lax.dynamic_slice(section[target], corner, (1, 1, rows, width))
    scale = STEP * coefficient(media[target][:, first_media : first_media + 1, :, at : at + width])
    is_open = opened[None, None, :, at : at + width] > 0.5
    new = jnp.where(is_open, old + scale * functools.reduce(jnp.add, products)[None, None], old)
    section[target] = lax.dynamic_update_slice(section[target], new, corner)
    return section["el"], section["ac"]


def solution(mesh):
    placed = (
        P("patch", None, "line", "layer"),
        P("patch", None, "line", "layer"),
        P("patch", None, "line", "layer"),
        P("patch", None, "line", "layer"),
        P(),
        P("patch", "line", "layer", None, None),
        P("patch", "line", "layer", None, None, None),
        P("patch", "line", "layer", None, None, None),
        P("patch", "line", "layer", None),
        P("patch", "line"),
        P("patch", "line"),
    )
    return jax.shard_map(
        per_device,
        mesh=mesh,
        in_specs=placed,
        out_specs=(P("patch", None, "line", "layer"), P("patch", None, "line", "layer")),
        check_vma=False,
    )
```

```python
import functools
import math

import jax
import jax.numpy as jnp
import numpy as np
from jax import lax
from jax.experimental import pallas as pl
from jax.experimental.pallas import tpu as pltpu
from jax.sharding import PartitionSpec as P

STEP = 0.25
PENALTY = 2.0
LANES = 128
VMEM_LIMIT = 56 * 1024 * 1024
FAR_VMEM_LIMIT = 24 * 1024 * 1024
HIGHEST = lax.Precision.HIGHEST


def derivative_row(period):
    n = np.arange(1, period)
    sign = np.where(n % 2 == 0, 1.0, -1.0)
    row = np.zeros(period)
    row[1:] = (math.pi / period) * sign / np.tan(math.pi * n / period)
    return row


def operator_tables(rows, slabs, cont):
    points = rows * slabs
    period = points + cont
    row = derivative_row(period)
    j = np.arange(rows)
    own = row[(j[:, None] - j[None, :]) % period]
    far, sent, tail = [], [], []
    for me in range(slabs):
        mine = me * rows + j[:, None]
        others = np.concatenate([(me - d) % slabs * rows + j for d in range(1, slabs)])
        far.append(row[(mine - others[None, :]) % period])
        toward = np.concatenate([(me + d) % slabs * rows + j for d in range(1, slabs)])
        sent.append(row[(toward[:, None] - me * rows - j[None, :]) % period])
        tail.append(row[(mine - points - np.arange(cont)[None, :]) % period])
    return tuple(np.asarray(table, np.float32) for table in (own, far, sent, tail))


def continuation_on(cont_matrix, rows, slabs, sources):
    match = cont_matrix.shape[1] // 2
    on_last = jnp.pad(cont_matrix[:, :match], ((0, 0), (rows - match, 0)))
    on_first = jnp.pad(cont_matrix[:, match:], ((0, 0), (0, rows - match)))
    return jnp.concatenate(
        [
            jnp.where(source == slabs - 1, on_last, 0.0) + jnp.where(source == 0, on_first, 0.0)
            for source in sources
        ],
        axis=1,
    )


def split(value, size):
    if size & (size - 1) == 0:
        return lax.shift_right_logical(value, size.bit_length() - 1), value & (size - 1)
    return lax.div(value, size), lax.rem(value, size)


def through_vmem(parts, in_semaphores, out_semaphores):
    loads, stores = [], []
    for i, (source, target, buffer) in enumerate(parts):
        loads.append(pltpu.make_async_copy(source, buffer, in_semaphores.at[i]))
        stores.append(pltpu.make_async_copy(buffer, target, out_semaphores.at[i]))
    for load in loads:
        load.start()
    for load, store in zip(loads, stores):
        load.wait()
        store.start()
    return stores


def take_rows_kernel(field, first, parts, *refs):
    elastic_ref = refs[-5]
    out_ref, held, in_semaphores, out_semaphores = refs[-4:]
    size = out_ref.shape[0] // parts
    copies = []
    for part in range(parts):
        here = pl.ds(part * size, size)
        source = elastic_ref.at[0, field, pl.ds(first + part * size, size)]
        copies.append((source, out_ref.at[here], held.at[here]))
    for store in through_vmem(copies, in_semaphores, out_semaphores):
        store.wait()


def take_rows(elastic, field, first, count, after=None):
    depth = elastic.shape[3]
    parts = 2 if count % 32 == 0 else 1
    anywhere = pl.BlockSpec(memory_space=pl.ANY)
    operands = (elastic,) if after is None else (after, elastic)
    return pl.pallas_call(
        functools.partial(take_rows_kernel, field, first, parts),
        in_specs=[anywhere] * len(operands),
        out_specs=anywhere,
        out_shape=jax.ShapeDtypeStruct((count, depth), jnp.float32),
        scratch_shapes=[pltpu.VMEM((count, depth), jnp.float32)] + [pltpu.SemaphoreType.DMA((parts,))] * 2,
        compiler_params=pltpu.CompilerParams(vmem_limit_bytes=VMEM_LIMIT),
        cost_estimate=pl.CostEstimate(flops=0, bytes_accessed=8 * count * depth, transcendentals=0),
        name="take_rows",
    )(*operands)


def take_pieces_kernel(
    pieces, layers, after_ref, elastic_ref, acoustic_ref, cells_ref, weights_ref, *refs
):
    del after_ref
    n = len(pieces)
    outs, (edges_ref, asked_ref), held = refs[:n], refs[n : n + 2], refs[n + 2 : 2 * n + 2]
    tiles, edge_semaphores, in_semaphores, out_semaphores = refs[2 * n + 2 :]
    n_el, n_ac = elastic_ref.shape[1], acoustic_ref.shape[1]
    rows, depth = elastic_ref.shape[2:]
    parts = []
    for i, (name, field, at, width) in enumerate(pieces):
        source = elastic_ref if name == "el" else acoustic_ref
        parts.append((source.at[0, field, :, pl.ds(at, width)], outs[i], held[i]))
    loads = []
    for end, at in enumerate((0, depth - LANES)):
        for k, (source, first, count) in enumerate(((elastic_ref, 0, n_el), (acoustic_ref, n_el, n_ac))):
            loads.append(
                pltpu.make_async_copy(
                    source.at[0, :, :, pl.ds(at, LANES)],
                    tiles.at[end, pl.ds(first, count)],
                    edge_semaphores.at[2 * end + k],
                )
            )
    stores = through_vmem(parts, in_semaphores, out_semaphores)
    for load in loads:
        load.start()

    x, z = split(cells_ref[0, 0, 0], depth)
    chunk, lane = split(z, LANES)
    words = (chunk * ((n_el + n_ac) * rows) + x) * LANES + lane
    asked_ref[...] = jnp.concatenate([words.astype(jnp.float32), weights_ref[0, 0, 0]], axis=1)

    for load in loads:
        load.wait()
    lane = lax.broadcasted_iota(jnp.int32, (rows, LANES), 1)
    columns = jnp.zeros((rows, LANES), jnp.float32)
    for f in range(n_el + n_ac):
        columns = jnp.where(lane == f, tiles[0, f, :, 0:1], columns)
        columns = jnp.where(lane == 8 + f, tiles[1, f, :, LANES - 1 : LANES], columns)
    lines = columns.T
    below = lax.rem(lax.axis_index("layer") + 1, layers)
    for to in range(layers):
        edges_ref[to] = jnp.where(to == below, lines[8:16], lines[0:8])
    for store in stores:
        store.wait()


def take_pieces(elastic, acoustic, cells, weights, pieces, after, layers):
    rows = elastic.shape[2]
    patches, corners, slots = cells.shape[3:]
    n = len(pieces)
    anywhere = pl.BlockSpec(memory_space=pl.ANY)
    vmem = pl.BlockSpec(memory_space=pltpu.VMEM)
    travelling = [jax.ShapeDtypeStruct((rows, width), jnp.float32) for _, _, _, width in pieces]
    cost = sum(width for _, _, _, width in pieces) * rows
    return pl.pallas_call(
        functools.partial(take_pieces_kernel, pieces, layers),
        in_specs=[anywhere] * 3 + [vmem] * 2,
        out_specs=[anywhere] * n + [vmem] * 2,
        out_shape=travelling
        + [
            jax.ShapeDtypeStruct((layers, 8, rows), jnp.float32),
            jax.ShapeDtypeStruct((patches, 2 * corners, slots), jnp.float32),
        ],
        scratch_shapes=[pltpu.VMEM(piece.shape, jnp.float32) for piece in travelling]
        + [pltpu.VMEM((2, 8, rows, LANES), jnp.float32), pltpu.SemaphoreType.DMA((4,))]
        + [pltpu.SemaphoreType.DMA((n,))] * 2,
        compiler_params=pltpu.CompilerParams(vmem_limit_bytes=VMEM_LIMIT),
        cost_estimate=pl.CostEstimate(flops=0, bytes_accessed=8 * cost, transcendentals=0),
        name="take_pieces",
    )(after, elastic, acoustic, cells, weights)


def gather_kernel(fields, rows, depth, words_ref, weights_ref, elastic_ref, acoustic_ref, out_ref, mixed):
    n_el = elastic_ref.shape[1]
    chunks = depth // LANES
    for f in range(fields):
        source = elastic_ref.at[0, f] if f < n_el else acoustic_ref.at[0, f - n_el]
        for c in range(chunks):
            mixed[pl.ds((c * fields + f) * rows, rows), :] = source[:, c * LANES : (c + 1) * LANES]
    lane = lax.broadcasted_iota(jnp.int32, (fields, LANES), 1)
    groups = out_ref.shape[1]

    def one_group(step, carry):
        patch, group = split(step, groups)

        def one_slot(r, values):
            slot = group * LANES + r
            total = None
            for s in range(4):
                start, at = split(words_ref[patch, s, slot], LANES)
                picked = mixed[pl.ds(start, fields, stride=rows), :]
                term = jnp.where(lane == at, picked * weights_ref[patch, 4 + s, slot], 0.0)
                total = term if total is None else total + term
            column = jnp.sum(total, axis=1, keepdims=True)
            return jnp.where(lane == r, column, values)

        values = lax.fori_loop(0, LANES, one_slot, jnp.zeros((fields, LANES), jnp.float32), unroll=16)
        out_ref[patch, group] = values
        return carry

    lax.fori_loop(0, out_ref.shape[0] * groups, one_group, 0)


def bf16_pair(value):
    high = value.astype(jnp.bfloat16)
    return high, (value - high.astype(jnp.float32)).astype(jnp.bfloat16)


def three_left(value):
    high, low = bf16_pair(value)
    return jnp.concatenate([high, high, low], axis=1)


def three_right(value):
    high, low = bf16_pair(value)
    return jnp.concatenate([high, low, high], axis=0)


def near_kernel(
    n_el, me_ref, own_ref, far_ref, tail_ref, own_cont_ref, far_cont_ref, elastic_ref, acoustic_ref,
    out_ref, far_operator_ref, operator,
):
    del me_ref

    @pl.when(pl.program_id(0) == 0)
    def _():
        def folded(table, cont):
            return table + jnp.dot(tail_ref[0], cont, precision=HIGHEST, preferred_element_type=jnp.float32)

        operator[...] = three_left(folded(own_ref[...], own_cont_ref[...]))
        far_operator_ref[...] = three_left(folded(far_ref[0], far_cont_ref[...]))

    value = jnp.where(pl.program_id(0) < n_el, elastic_ref[0, 0], acoustic_ref[0, 0])
    out_ref[0] = jnp.dot(operator[...], three_right(value), preferred_element_type=jnp.float32)


def near_derivatives(elastic, acoustic, cont_matrix, tables, me, slabs):
    rows, depth = elastic.shape[2:]
    cont = cont_matrix.shape[0]
    reach = (slabs - 1) * rows
    own, far, _, tail = tables
    own_cont = continuation_on(cont_matrix, rows, slabs, [me])
    far_cont = continuation_on(cont_matrix, rows, slabs, [(me - d) % slabs for d in range(1, slabs)])
    return pl.pallas_call(
        functools.partial(near_kernel, 4),
        grid_spec=pltpu.PrefetchScalarGridSpec(
            num_scalar_prefetch=1,
            grid=(6,),
            in_specs=[
                pl.BlockSpec((rows, rows), lambda f, me: (0, 0)),
                pl.BlockSpec((1, rows, reach), lambda f, me: (me[0], 0, 0)),
                pl.BlockSpec((1, rows, cont), lambda f, me: (me[0], 0, 0)),
                pl.BlockSpec((cont, rows), lambda f, me: (0, 0)),
                pl.BlockSpec((cont, reach), lambda f, me: (0, 0)),
                pl.BlockSpec((1, 1, rows, depth), lambda f, me: (0, jnp.where(f < 3, f, 4), 0, 0)),
                pl.BlockSpec((1, 1, rows, depth), lambda f, me: (0, jnp.maximum(f - 4, 0), 0, 0)),
            ],
            out_specs=[
                pl.BlockSpec((1, rows, depth), lambda f, me: (f, 0, 0)),
                pl.BlockSpec((rows, 3 * reach), lambda f, me: (0, 0)),
            ],
            scratch_shapes=[pltpu.VMEM((rows, 3 * rows), jnp.bfloat16)],
        ),
        out_shape=[
            jax.ShapeDtypeStruct((6, rows, depth), jnp.float32),
            jax.ShapeDtypeStruct((rows, 3 * reach), jnp.bfloat16),
        ],
        compiler_params=pltpu.CompilerParams(vmem_limit_bytes=VMEM_LIMIT),
        cost_estimate=pl.CostEstimate(
            flops=36 * rows * rows * depth, bytes_accessed=60 * rows * depth, transcendentals=0
        ),
        name="near_dx",
    )(me.reshape(1), own, far, tail, own_cont, far_cont, elastic, acoustic)


def sent_kernel(rows, me_ref, turn_ref, sent_ref, tail_ref, cont_ref, piece_ref, out_ref):
    del turn_ref
    me, slabs = me_ref[0], tail_ref.shape[0]
    value = three_right(piece_ref[...])
    for d in range(1, slabs):
        here = pl.ds((d - 1) * rows, rows)
        tail = tail_ref[lax.rem(me + d, slabs)]
        block = sent_ref[0, here, :] + jnp.dot(
            tail, cont_ref[...], precision=HIGHEST, preferred_element_type=jnp.float32
        )
        out_ref[here, :] = jnp.dot(three_left(block), value, preferred_element_type=jnp.float32)


def sent_products(piece, cont_matrix, tables, me, slabs, turn):
    rows, width = piece.shape
    cont = cont_matrix.shape[0]
    reach = (slabs - 1) * rows
    _, _, sent, tail = tables
    return pl.pallas_call(
        functools.partial(sent_kernel, rows),
        grid_spec=pltpu.PrefetchScalarGridSpec(
            num_scalar_prefetch=1,
            grid=(1,),
            in_specs=[
                pl.BlockSpec(memory_space=pl.ANY),
                pl.BlockSpec((1, reach, rows), lambda i, me: (me[0], 0, 0)),
                pl.BlockSpec((slabs, rows, cont), lambda i, me: (0, 0, 0)),
                pl.BlockSpec((cont, rows), lambda i, me: (0, 0)),
                pl.BlockSpec((rows, width), lambda i, me: (0, 0)),
            ],
            out_specs=pl.BlockSpec((reach, width), lambda i, me: (0, 0)),
        ),
        out_shape=jax.ShapeDtypeStruct((reach, width), jnp.float32),
        compiler_params=pltpu.CompilerParams(vmem_limit_bytes=VMEM_LIMIT),
        cost_estimate=pl.CostEstimate(
            flops=6 * rows * reach * width, bytes_accessed=4 * rows * reach, transcendentals=0
        ),
        name="sent_products",
    )(me.reshape(1), turn, sent, tail, continuation_on(cont_matrix, rows, slabs, [me]), piece)


def section_kernel(
    layers, rows, depth, tile,
    cells_ref, counts_ref, interp_ref,
    dx_ref, elastic_ref, acoustic_ref, el_media_ref, ac_media_ref, edges_ref, el_pair_ref, ac_pair_ref,
    new_el_ref, new_ac_ref, open_ref,
    columns,
):
    step = pl.program_id(0)
    here = pl.ds(pl.multiple_of(step * tile, tile), tile)
    lane = lax.broadcasted_iota(jnp.int32, (tile, depth), 1)
    layer = lax.axis_index("layer")
    at_top, at_bottom = layer == 0, layer == layers - 1
    from_above = edges_ref[lax.rem(layer + layers - 1, layers)]
    from_below = edges_ref[lax.rem(layer + 1, layers)]
    ocean_row = from_above[5:6]
    basin_row = from_below[1:2]

    @pl.when(step == 0)
    def _():
        pairs = jnp.concatenate([el_pair_ref[...], ac_pair_ref[...]]).astype(jnp.float32)
        lines = [
            jnp.where(at_top, 0.0, from_above),
            jnp.where(at_bottom, 0.0, from_below),
            pairs,
            jnp.zeros((LANES - 18, rows), jnp.float32),
        ]
        columns[...] = jnp.concatenate(lines).T

    halo = columns[here, :]

    def dz(value, slot):
        above = halo[:, slot : slot + 1]
        below = halo[:, 8 + slot : 9 + slot]
        following = jnp.where(lane == depth - 1, below, pltpu.roll(value, depth - 1, 1))
        previous = jnp.where(lane == 0, above, pltpu.roll(value, 1, 1))
        return (following - previous) * 0.5

    vx, vz, sxx, szz, sxz = [elastic_ref[0, f] for f in range(5)]
    p, ovx, ovz = [acoustic_ref[0, f] for f in range(3)]
    buoyancy = el_media_ref[0, 0]
    lame = el_media_ref[0, 1]
    shear = el_media_ref[0, 2]
    stiffness = lame + 2.0 * shear
    bulk = ac_media_ref[0, 0]
    ocean_buoyancy = ac_media_ref[0, 1]

    dx_vx = dx_ref[0]
    dz_vz = dz(vz, 1)
    new_el_ref[0, 0, here, :] = vx + STEP * (buoyancy * (dx_ref[2] + dz(sxz, 4)))
    new_el_ref[0, 1, here, :] = vz + STEP * (buoyancy * (dx_ref[3] + dz(szz, 3)))
    new_el_ref[0, 2, here, :] = sxx + STEP * (stiffness * dx_vx + lame * dz_vz)
    choose = lax.broadcasted_iota(jnp.int32, (tile, rows), 1).astype(jnp.float32)
    pressure = jnp.sum(jnp.where(halo[:, 16:17] == choose, ocean_row, 0.0), axis=1, keepdims=True)
    velocity = jnp.sum(jnp.where(halo[:, 17:18] == choose, basin_row, 0.0), axis=1, keepdims=True)
    rate_szz = lame * dx_vx + stiffness * dz_vz
    rate_szz = rate_szz + jnp.where((lane == 0) & at_top, PENALTY * (-pressure - szz), 0.0)
    new_el_ref[0, 3, here, :] = szz + STEP * rate_szz
    new_el_ref[0, 4, here, :] = sxz + STEP * (shear * (dz(vx, 0) + dx_ref[1]))
    new_ac_ref[0, 0, here, :] = p - STEP * (bulk * (dx_ref[5] + dz(ovz, 7)))
    new_ac_ref[0, 1, here, :] = ovx - STEP * (ocean_buoyancy * dx_ref[4])
    rate_ovz = -ocean_buoyancy * dz(p, 5)
    rate_ovz = rate_ovz + jnp.where((lane == depth - 1) & at_bottom, PENALTY * (velocity - ovz), 0.0)
    new_ac_ref[0, 2, here, :] = ovz + STEP * rate_ovz
    open_ref[here, :] = jnp.ones((tile, depth), jnp.float32)

    @pl.when(step == pl.num_programs(0) - 1)
    def _():
        place = lax.broadcasted_iota(jnp.int32, (8, LANES), 0) * LANES
        place = place + lax.broadcasted_iota(jnp.int32, (8, LANES), 1)
        n_el = new_el_ref.shape[1]

        def one_patch(q, carry):
            def one_slot(r, inner):
                x, z = split(cells_ref[0, 0, 0, q, r], depth)
                (high, row), (low, at) = split(x, 8), split(z, LANES)
                at_row = pl.ds(pl.multiple_of(high * 8, 8), 8)
                at_lane = pl.ds(pl.multiple_of(low * LANES, LANES), LANES)
                hit = place == row * LANES + at
                group, within = split(r, LANES)
                for f in range(8):
                    target = new_el_ref.at[0, f] if f < n_el else new_ac_ref.at[0, f - n_el]
                    target[at_row, at_lane] = jnp.where(hit, interp_ref[q, group, f, within], target[at_row, at_lane])
                open_ref[at_row, at_lane] = jnp.where(hit, 0.0, open_ref[at_row, at_lane])
                return inner

            return lax.fori_loop(0, counts_ref[0, 0, 0, q], one_slot, carry)

        lax.fori_loop(0, counts_ref.shape[3], one_patch, 0)


def far_kernel(coefficients, turn_ref, d_ref, media_ref, open_ref, base_ref, *refs):
    del turn_ref
    *far_refs, next_ref, out_ref = refs
    del next_ref
    far_field = jnp.concatenate([far_ref[...] for far_ref in far_refs], axis=0)
    far = jnp.dot(d_ref[...], three_right(far_field), preferred_element_type=jnp.float32)
    media = [media_ref[0, i] for i in range(media_ref.shape[1])]
    is_open = open_ref[...] > 0.5
    for i, coefficient in enumerate(coefficients):
        old = base_ref[0, i]
        out_ref[0, i] = jnp.where(is_open, old + (STEP * coefficient(*media)) * far, old)


def add_far(base, operator, far, at, media, first_media, n_media, first_field, coefficients, opened, turn):
    rows, reach = operator.shape[0], operator.shape[1] // 3
    width = far[0].shape[1]
    tile = math.gcd(math.gcd(width, at), 2 * LANES)
    n_out = len(coefficients)
    shift = at // tile
    return pl.pallas_call(
        functools.partial(far_kernel, coefficients),
        grid=(width // tile,),
        in_specs=[
            pl.BlockSpec(memory_space=pl.ANY),
            pl.BlockSpec((rows, 3 * reach), lambda i: (0, 0)),
            pl.BlockSpec((1, n_media, rows, tile), lambda i: (0, first_media // n_media, 0, i + shift)),
            pl.BlockSpec((rows, tile), lambda i: (0, i + shift)),
            pl.BlockSpec((1, n_out, rows, tile), lambda i: (0, first_field // n_out, 0, i + shift)),
        ]
        + [pl.BlockSpec((part.shape[0], tile), lambda i: (0, i)) for part in far],
        out_specs=[
            pl.BlockSpec(memory_space=pl.ANY),
            pl.BlockSpec((1, n_out, rows, tile), lambda i: (0, first_field // n_out, 0, i + shift)),
        ],
        out_shape=[
            jax.ShapeDtypeStruct(turn.shape, turn.dtype),
            jax.ShapeDtypeStruct(base.shape, base.dtype),
        ],
        input_output_aliases={0: 0, 4: 1},
        compiler_params=pltpu.CompilerParams(vmem_limit_bytes=FAR_VMEM_LIMIT),
        cost_estimate=pl.CostEstimate(
            flops=6 * rows * reach * width,
            bytes_accessed=4 * rows * width * (3 + n_media + n_out),
            transcendentals=0,
        ),
        name="add_far",
    )(turn, operator, media, opened, base, *far)


def per_device(
    elastic,
    acoustic,
    el_media,
    ac_media,
    cont_matrix,
    fringe_cells,
    donor_cells,
    donor_weights,
    donor_counts,
    el_pair,
    ac_pair,
):
    rows, depth = elastic.shape[2], elastic.shape[3]
    slabs = lax.axis_size("line")
    layers = lax.axis_size("layer")
    patches = lax.axis_size("patch")
    slots = fringe_cells.shape[-1]
    groups = slots // LANES
    me = lax.axis_index("line")
    layer = lax.axis_index("layer")
    tile = min(64, rows)

    def to_others(value):
        return [
            lax.ppermute(value, "line", [(i, (i + distance) % slabs) for i in range(slabs)])
            for distance in range(1, slabs)
        ]

    most = depth - depth // 4
    pieces = [
        ("el", 0, 0, depth, "el", 0, 3, 2, (lambda b, l, m: l + 2.0 * m, lambda b, l, m: l)),
        ("ac", 0, 0, depth, "ac", 1, 1, 1, (lambda b: -b,)),
        ("ac", 1, 0, depth, "ac", 0, 1, 0, (lambda k: -k,)),
        ("el", 1, 0, depth, "el", 2, 1, 4, (lambda m: m,)),
        ("el", 2, 0, depth, "el", 0, 1, 0, (lambda b: b,)),
        ("el", 4, 0, most, "el", 0, 1, 1, (lambda b: b,)),
        ("el", 4, most, depth - most, "el", 0, 1, 1, (lambda b: b,)),
    ]
    early = rows // 4
    first = take_rows(elastic, 0, 0, early)
    second = take_rows(elastic, 0, early, rows - early, first)
    *others, last, edges, asked = take_pieces(
        elastic, acoustic, donor_cells, donor_weights, [piece[:4] for piece in pieces[1:]], second, layers
    )
    far = [[part for pair in zip(to_others(first), to_others(second)) for part in pair]]
    far += [to_others(value) for value in others]

    asked = lax.all_to_all(asked, "patch", split_axis=0, concat_axis=0, tiled=True)
    asked_words = asked[:, :4].astype(jnp.int32)

    smem = pl.BlockSpec(memory_space=pltpu.SMEM)
    vmem = pl.BlockSpec(memory_space=pltpu.VMEM)
    local = pl.pallas_call(
        functools.partial(gather_kernel, 8, rows, depth),
        in_specs=[smem, smem, vmem, vmem],
        out_specs=vmem,
        out_shape=jax.ShapeDtypeStruct((patches, groups, 8, LANES), jnp.float32),
        scratch_shapes=[pltpu.VMEM((8 * rows * (depth // LANES), LANES), jnp.float32)],
        compiler_params=pltpu.CompilerParams(vmem_limit_bytes=VMEM_LIMIT),
        cost_estimate=pl.CostEstimate(flops=10**9, bytes_accessed=32 * rows * depth, transcendentals=0),
        name="donor_gather",
    )(asked_words, asked, elastic, acoustic)
    interp = lax.all_to_all(local, "patch", split_axis=0, concat_axis=0, tiled=True)
    edges = lax.all_to_all(edges, "layer", split_axis=0, concat_axis=0, tiled=True)

    tables = operator_tables(rows, slabs, cont_matrix.shape[0])
    near, far_operator = near_derivatives(elastic, acoustic, cont_matrix, tables, me, slabs)
    new_el, new_ac, opened = pl.pallas_call(
        functools.partial(section_kernel, layers, rows, depth, tile),
        grid=(rows // tile,),
        in_specs=[
            smem,
            smem,
            smem,
            pl.BlockSpec((6, tile, depth), lambda i: (0, i, 0)),
            pl.BlockSpec((1, 5, tile, depth), lambda i: (0, 0, i, 0)),
            pl.BlockSpec((1, 3, tile, depth), lambda i: (0, 0, i, 0)),
            pl.BlockSpec((1, 3, tile, depth), lambda i: (0, 0, i, 0)),
            pl.BlockSpec((1, 2, tile, depth), lambda i: (0, 0, i, 0)),
            vmem,
            vmem,
            vmem,
        ],
        out_specs=[vmem, vmem, vmem],
        out_shape=[
            jax.ShapeDtypeStruct(elastic.shape, jnp.float32),
            jax.ShapeDtypeStruct(acoustic.shape, jnp.float32),
            jax.ShapeDtypeStruct((rows, depth), jnp.float32),
        ],
        scratch_shapes=[pltpu.VMEM((rows, LANES), jnp.float32)],
        compiler_params=pltpu.CompilerParams(vmem_limit_bytes=VMEM_LIMIT),
        cost_estimate=pl.CostEstimate(
            flops=100 * rows * depth, bytes_accessed=112 * rows * depth, transcendentals=0
        ),
        name="near_section",
    )(
        fringe_cells,
        donor_counts,
        interp,
        near,
        elastic,
        acoustic,
        el_media,
        ac_media,
        edges,
        el_pair,
        ac_pair,
    )

    turn = jnp.zeros((8, LANES), jnp.float32)
    section = {"el": new_el, "ac": new_ac}
    media = {"el": el_media, "ac": ac_media}
    turns = []
    for value, (_, _, at, _, target, first_media, n_media, first_field, coefficients) in zip(far, pieces):
        turn, section[target] = add_far(
            section[target], far_operator, value, at,
            media[target], first_media, n_media, first_field, coefficients, opened, turn,
        )
        turns.append(turn)

    products = sent_products(last, cont_matrix, tables, me, slabs, turns[2])
    _, _, at, width, target, first_media, _, first_field, (coefficient,) = pieces[-1]
    for start, count in ((0, rows - early), (rows - early, early)):
        received = [
            lax.ppermute(
                lax.slice_in_dim(products, (d - 1) * rows + start, (d - 1) * rows + start + count),
                "line",
                [(i, (i + d) % slabs) for i in range(slabs)],
            )
            for d in range(1, slabs)
        ]
        corner = (0, first_field, start, at)
        here = (slice(start, start + count), slice(at, at + width))
        old = lax.dynamic_slice(section[target], corner, (1, 1, count, width))
        scale = STEP * coefficient(media[target][(slice(None), slice(first_media, first_media + 1)) + here])
        far_part = functools.reduce(jnp.add, received)[None, None]
        new = jnp.where(opened[here] > 0.5, old + scale * far_part, old)
        section[target] = lax.optimization_barrier(lax.dynamic_update_slice(section[target], new, corner))
    return section["el"], section["ac"]


def solution(mesh):
    placed = (
        P("patch", None, "line", "layer"),
        P("patch", None, "line", "layer"),
        P("patch", None, "line", "layer"),
        P("patch", None, "line", "layer"),
        P(),
        P("patch", "line", "layer", None, None),
        P("patch", "line", "layer", None, None, None),
        P("patch", "line", "layer", None, None, None),
        P("patch", "line", "layer", None),
        P("patch", "line"),
        P("patch", "line"),
    )
    return jax.shard_map(
        per_device,
        mesh=mesh,
        in_specs=placed,
        out_specs=(P("patch", None, "line", "layer"), P("patch", None, "line", "layer")),
        check_vma=False,
    )
```

```python
import functools
import math

import jax
import jax.numpy as jnp
import numpy as np
from jax import lax
from jax.experimental import pallas as pl
from jax.experimental.pallas import tpu as pltpu
from jax.sharding import PartitionSpec as P

STEP = 0.25
PENALTY = 2.0
LANES = 128
VMEM_LIMIT = 56 * 1024 * 1024
FAR_VMEM_LIMIT = 24 * 1024 * 1024
HIGHEST = lax.Precision.HIGHEST


def derivative_row(period):
    n = np.arange(1, period)
    sign = np.where(n % 2 == 0, 1.0, -1.0)
    row = np.zeros(period)
    row[1:] = (math.pi / period) * sign / np.tan(math.pi * n / period)
    return row


def operator_tables(rows, slabs, cont):
    points = rows * slabs
    period = points + cont
    row = derivative_row(period)
    j = np.arange(rows)
    own = row[(j[:, None] - j[None, :]) % period]
    far, tail = [], []
    for me in range(slabs):
        mine = me * rows + j[:, None]
        others = np.concatenate([(me - d) % slabs * rows + j for d in range(1, slabs)])
        far.append(row[(mine - others[None, :]) % period])
        tail.append(row[(mine - points - np.arange(cont)[None, :]) % period])
    return tuple(np.asarray(table, np.float32) for table in (own, far, tail))


def continuation_on(cont_matrix, rows, slabs, sources):
    match = cont_matrix.shape[1] // 2
    on_last = jnp.pad(cont_matrix[:, :match], ((0, 0), (rows - match, 0)))
    on_first = jnp.pad(cont_matrix[:, match:], ((0, 0), (0, rows - match)))
    return jnp.concatenate(
        [
            jnp.where(source == slabs - 1, on_last, 0.0) + jnp.where(source == 0, on_first, 0.0)
            for source in sources
        ],
        axis=1,
    )


def split(value, size):
    if size & (size - 1) == 0:
        return lax.shift_right_logical(value, size.bit_length() - 1), value & (size - 1)
    return lax.div(value, size), lax.rem(value, size)


def take_kernel(pieces, parts, elastic_ref, acoustic_ref, *refs):
    n = len(pieces)
    outs, held, in_semaphores, out_semaphores = refs[:n], refs[n : 2 * n], refs[-2], refs[-1]
    rows = elastic_ref.shape[2]
    loads, stores = [], []
    for i, (name, field, at, width) in enumerate(pieces):
        source = elastic_ref if name == "el" else acoustic_ref
        for part in range(parts):
            here = pl.ds(part * (rows // parts), rows // parts)
            k = i * parts + part
            loads.append(
                pltpu.make_async_copy(source.at[0, field, here, pl.ds(at, width)], held[i].at[here], in_semaphores.at[k])
            )
            stores.append(pltpu.make_async_copy(held[i].at[here], outs[i].at[here], out_semaphores.at[k]))
    for load in loads:
        load.start()
    for load, store in zip(loads, stores):
        load.wait()
        store.start()
    return stores


def take_only_kernel(pieces, parts, elastic_ref, *refs):
    for store in take_kernel(pieces, parts, elastic_ref, None, *refs):
        store.wait()


def take_and_edges_kernel(
    pieces, parts, layers, after_ref, elastic_ref, acoustic_ref, cells_ref, weights_ref, *refs
):
    del after_ref
    n = len(pieces)
    edges_ref, asked_ref, tiles, edge_semaphores = refs[n : n + 4]
    n_el, n_ac = elastic_ref.shape[1], acoustic_ref.shape[1]
    rows, depth = elastic_ref.shape[2:]
    loads = []
    for end, at in enumerate((0, depth - LANES)):
        for k, (source, first, count) in enumerate(((elastic_ref, 0, n_el), (acoustic_ref, n_el, n_ac))):
            loads.append(
                pltpu.make_async_copy(
                    source.at[0, :, :, pl.ds(at, LANES)],
                    tiles.at[end, pl.ds(first, count)],
                    edge_semaphores.at[2 * end + k],
                )
            )
    for load in loads:
        load.start()
    stores = take_kernel(pieces, parts, elastic_ref, acoustic_ref, *refs[:n], *refs[n + 4 :])

    x, z = split(cells_ref[0, 0, 0], depth)
    chunk, at_lane = split(z, LANES)
    words = (chunk * ((n_el + n_ac) * rows) + x) * LANES + at_lane
    asked_ref[...] = jnp.concatenate([words.astype(jnp.float32), weights_ref[0, 0, 0]], axis=1)

    for load in loads:
        load.wait()
    lane = lax.broadcasted_iota(jnp.int32, (rows, LANES), 1)
    columns = jnp.zeros((rows, LANES), jnp.float32)
    for f in range(n_el + n_ac):
        columns = jnp.where(lane == f, tiles[0, f, :, 0:1], columns)
        columns = jnp.where(lane == 8 + f, tiles[1, f, :, LANES - 1 : LANES], columns)
    lines = columns.T
    below = lax.rem(lax.axis_index("layer") + 1, layers)
    for to in range(layers):
        edges_ref[to] = jnp.where(to == below, lines[8:16], lines[0:8])
    for store in stores:
        store.wait()


def take_pieces(elastic, acoustic, pieces, after=None, cells=None, weights=None, layers=0):
    rows = elastic.shape[2]
    anywhere = pl.BlockSpec(memory_space=pl.ANY)
    vmem = pl.BlockSpec(memory_space=pltpu.VMEM)
    out_shape = [jax.ShapeDtypeStruct((rows, width), jnp.float32) for _, _, _, width in pieces]
    in_specs, out_specs = [anywhere], [anywhere] * len(pieces)
    parts = 2 if layers else 4
    scratch = [pltpu.VMEM((rows, width), jnp.float32) for _, _, _, width in pieces]
    scratch += [pltpu.SemaphoreType.DMA((len(pieces) * parts,))] * 2
    kernel, operands = functools.partial(take_only_kernel, pieces, parts), (elastic,)
    if layers:
        patches, corners, slots = cells.shape[3:]
        out_shape.append(jax.ShapeDtypeStruct((layers, 8, rows), jnp.float32))
        out_shape.append(jax.ShapeDtypeStruct((patches, 2 * corners, slots), jnp.float32))
        in_specs, out_specs = [anywhere] * 3 + [vmem] * 2, out_specs + [vmem] * 2
        scratch = [pltpu.VMEM((2, 8, rows, LANES), jnp.float32), pltpu.SemaphoreType.DMA((4,))] + scratch
        kernel = functools.partial(take_and_edges_kernel, pieces, parts, layers)
        operands = (after, elastic, acoustic, cells, weights)
    cost = sum(width for _, _, _, width in pieces) * rows
    return pl.pallas_call(
        kernel,
        in_specs=in_specs,
        out_specs=out_specs,
        out_shape=out_shape,
        scratch_shapes=scratch,
        compiler_params=pltpu.CompilerParams(vmem_limit_bytes=VMEM_LIMIT),
        cost_estimate=pl.CostEstimate(flops=0, bytes_accessed=8 * cost, transcendentals=0),
        name="take_pieces",
    )(*operands)


def gather_kernel(fields, rows, depth, words_ref, weights_ref, elastic_ref, acoustic_ref, out_ref, mixed):
    n_el = elastic_ref.shape[1]
    chunks = depth // LANES
    for f in range(fields):
        source = elastic_ref.at[0, f] if f < n_el else acoustic_ref.at[0, f - n_el]
        for c in range(chunks):
            mixed[pl.ds((c * fields + f) * rows, rows), :] = source[:, c * LANES : (c + 1) * LANES]
    lane = lax.broadcasted_iota(jnp.int32, (fields, LANES), 1)
    groups = out_ref.shape[1]

    def one_group(step, carry):
        patch, group = split(step, groups)

        def one_slot(r, values):
            slot = group * LANES + r
            total = None
            for s in range(4):
                start, at = split(words_ref[patch, s, slot], LANES)
                picked = mixed[pl.ds(start, fields, stride=rows), :]
                term = jnp.where(lane == at, picked * weights_ref[patch, 4 + s, slot], 0.0)
                total = term if total is None else total + term
            column = jnp.sum(total, axis=1, keepdims=True)
            return jnp.where(lane == r, column, values)

        values = lax.fori_loop(0, LANES, one_slot, jnp.zeros((fields, LANES), jnp.float32), unroll=16)
        out_ref[patch, group] = values
        return carry

    lax.fori_loop(0, out_ref.shape[0] * groups, one_group, 0)


def bf16_pair(value):
    high = value.astype(jnp.bfloat16)
    return high, (value - high.astype(jnp.float32)).astype(jnp.bfloat16)


def three_left(value):
    high, low = bf16_pair(value)
    return jnp.concatenate([high, high, low], axis=1)


def three_right(value):
    high, low = bf16_pair(value)
    return jnp.concatenate([high, low, high], axis=0)


def near_kernel(
    n_el, me_ref, own_ref, far_ref, tail_ref, own_cont_ref, far_cont_ref, elastic_ref, acoustic_ref,
    out_ref, far_operator_ref, operator,
):
    del me_ref

    @pl.when(pl.program_id(0) == 0)
    def _():
        def folded(table, cont):
            return table + jnp.dot(tail_ref[0], cont, precision=HIGHEST, preferred_element_type=jnp.float32)

        operator[...] = three_left(folded(own_ref[...], own_cont_ref[...]))
        far_operator_ref[...] = three_left(folded(far_ref[0], far_cont_ref[...]))

    value = jnp.where(pl.program_id(0) < n_el, elastic_ref[0, 0], acoustic_ref[0, 0])
    out_ref[0] = jnp.dot(operator[...], three_right(value), preferred_element_type=jnp.float32)


def near_derivatives(elastic, acoustic, cont_matrix, me, slabs):
    rows, depth = elastic.shape[2:]
    cont = cont_matrix.shape[0]
    reach = (slabs - 1) * rows
    own, far, tail = operator_tables(rows, slabs, cont)
    own_cont = continuation_on(cont_matrix, rows, slabs, [me])
    far_cont = continuation_on(cont_matrix, rows, slabs, [(me - d) % slabs for d in range(1, slabs)])
    return pl.pallas_call(
        functools.partial(near_kernel, 4),
        grid_spec=pltpu.PrefetchScalarGridSpec(
            num_scalar_prefetch=1,
            grid=(6,),
            in_specs=[
                pl.BlockSpec((rows, rows), lambda f, me: (0, 0)),
                pl.BlockSpec((1, rows, reach), lambda f, me: (me[0], 0, 0)),
                pl.BlockSpec((1, rows, cont), lambda f, me: (me[0], 0, 0)),
                pl.BlockSpec((cont, rows), lambda f, me: (0, 0)),
                pl.BlockSpec((cont, reach), lambda f, me: (0, 0)),
                pl.BlockSpec((1, 1, rows, depth), lambda f, me: (0, jnp.where(f < 3, f, 4), 0, 0)),
                pl.BlockSpec((1, 1, rows, depth), lambda f, me: (0, jnp.maximum(f - 4, 0), 0, 0)),
            ],
            out_specs=[
                pl.BlockSpec((1, rows, depth), lambda f, me: (f, 0, 0)),
                pl.BlockSpec((rows, 3 * reach), lambda f, me: (0, 0)),
            ],
            scratch_shapes=[pltpu.VMEM((rows, 3 * rows), jnp.bfloat16)],
        ),
        out_shape=[
            jax.ShapeDtypeStruct((6, rows, depth), jnp.float32),
            jax.ShapeDtypeStruct((rows, 3 * reach), jnp.bfloat16),
        ],
        compiler_params=pltpu.CompilerParams(vmem_limit_bytes=VMEM_LIMIT),
        cost_estimate=pl.CostEstimate(
            flops=36 * rows * rows * depth, bytes_accessed=60 * rows * depth, transcendentals=0
        ),
        name="near_dx",
    )(me.reshape(1), own, far, tail, own_cont, far_cont, elastic, acoustic)


def section_kernel(
    layers, rows, depth, tile,
    cells_ref, counts_ref, interp_ref,
    dx_ref, elastic_ref, acoustic_ref, el_media_ref, ac_media_ref, edges_ref, el_pair_ref, ac_pair_ref,
    new_el_ref, new_ac_ref, open_ref,
    columns,
):
    step = pl.program_id(0)
    here = pl.ds(pl.multiple_of(step * tile, tile), tile)
    lane = lax.broadcasted_iota(jnp.int32, (tile, depth), 1)
    layer = lax.axis_index("layer")
    at_top, at_bottom = layer == 0, layer == layers - 1
    from_above = edges_ref[lax.rem(layer + layers - 1, layers)]
    from_below = edges_ref[lax.rem(layer + 1, layers)]
    ocean_row = from_above[5:6]
    basin_row = from_below[1:2]

    @pl.when(step == 0)
    def _():
        pairs = jnp.concatenate([el_pair_ref[...], ac_pair_ref[...]]).astype(jnp.float32)
        lines = [
            jnp.where(at_top, 0.0, from_above),
            jnp.where(at_bottom, 0.0, from_below),
            pairs,
            jnp.zeros((LANES - 18, rows), jnp.float32),
        ]
        columns[...] = jnp.concatenate(lines).T

    halo = columns[here, :]

    def dz(value, slot):
        above = halo[:, slot : slot + 1]
        below = halo[:, 8 + slot : 9 + slot]
        following = jnp.where(lane == depth - 1, below, pltpu.roll(value, depth - 1, 1))
        previous = jnp.where(lane == 0, above, pltpu.roll(value, 1, 1))
        return (following - previous) * 0.5

    vx, vz, sxx, szz, sxz = [elastic_ref[0, f] for f in range(5)]
    p, ovx, ovz = [acoustic_ref[0, f] for f in range(3)]
    buoyancy = el_media_ref[0, 0]
    lame = el_media_ref[0, 1]
    shear = el_media_ref[0, 2]
    stiffness = lame + 2.0 * shear
    bulk = ac_media_ref[0, 0]
    ocean_buoyancy = ac_media_ref[0, 1]

    dx_vx = dx_ref[0]
    dz_vz = dz(vz, 1)
    new_el_ref[0, 0, here, :] = vx + STEP * (buoyancy * (dx_ref[2] + dz(sxz, 4)))
    new_el_ref[0, 1, here, :] = vz + STEP * (buoyancy * (dx_ref[3] + dz(szz, 3)))
    new_el_ref[0, 2, here, :] = sxx + STEP * (stiffness * dx_vx + lame * dz_vz)
    choose = lax.broadcasted_iota(jnp.int32, (tile, rows), 1).astype(jnp.float32)
    pressure = jnp.sum(jnp.where(halo[:, 16:17] == choose, ocean_row, 0.0), axis=1, keepdims=True)
    velocity = jnp.sum(jnp.where(halo[:, 17:18] == choose, basin_row, 0.0), axis=1, keepdims=True)
    rate_szz = lame * dx_vx + stiffness * dz_vz
    rate_szz = rate_szz + jnp.where((lane == 0) & at_top, PENALTY * (-pressure - szz), 0.0)
    new_el_ref[0, 3, here, :] = szz + STEP * rate_szz
    new_el_ref[0, 4, here, :] = sxz + STEP * (shear * (dz(vx, 0) + dx_ref[1]))
    new_ac_ref[0, 0, here, :] = p - STEP * (bulk * (dx_ref[5] + dz(ovz, 7)))
    new_ac_ref[0, 1, here, :] = ovx - STEP * (ocean_buoyancy * dx_ref[4])
    rate_ovz = -ocean_buoyancy * dz(p, 5)
    rate_ovz = rate_ovz + jnp.where((lane == depth - 1) & at_bottom, PENALTY * (velocity - ovz), 0.0)
    new_ac_ref[0, 2, here, :] = ovz + STEP * rate_ovz
    open_ref[here, :] = jnp.ones((tile, depth), jnp.float32)

    @pl.when(step == pl.num_programs(0) - 1)
    def _():
        place = lax.broadcasted_iota(jnp.int32, (8, LANES), 0) * LANES
        place = place + lax.broadcasted_iota(jnp.int32, (8, LANES), 1)
        n_el = new_el_ref.shape[1]

        def one_patch(q, carry):
            def one_slot(r, inner):
                x, z = split(cells_ref[0, 0, 0, q, r], depth)
                (high, row), (low, at) = split(x, 8), split(z, LANES)
                at_row = pl.ds(pl.multiple_of(high * 8, 8), 8)
                at_lane = pl.ds(pl.multiple_of(low * LANES, LANES), LANES)
                hit = place == row * LANES + at
                group, within = split(r, LANES)
                for f in range(8):
                    target = new_el_ref.at[0, f] if f < n_el else new_ac_ref.at[0, f - n_el]
                    target[at_row, at_lane] = jnp.where(hit, interp_ref[q, group, f, within], target[at_row, at_lane])
                open_ref[at_row, at_lane] = jnp.where(hit, 0.0, open_ref[at_row, at_lane])
                return inner

            return lax.fori_loop(0, counts_ref[0, 0, 0, q], one_slot, carry)

        lax.fori_loop(0, counts_ref.shape[3], one_patch, 0)


def far_kernel(coefficients, turn_ref, d_ref, far_ref, media_ref, open_ref, base_ref, next_ref, out_ref):
    del turn_ref, next_ref
    far = jnp.dot(d_ref[...], three_right(far_ref[...]), preferred_element_type=jnp.float32)
    media = [media_ref[0, i] for i in range(media_ref.shape[1])]
    is_open = open_ref[...] > 0.5
    for i, coefficient in enumerate(coefficients):
        old = base_ref[0, i]
        out_ref[0, i] = jnp.where(is_open, old + (STEP * coefficient(*media)) * far, old)


def add_far(base, operator, far, at, media, first_media, n_media, first_field, coefficients, opened, turn):
    rows, reach = operator.shape[0], far.shape[0]
    width = far.shape[1]
    tile = math.gcd(math.gcd(width, at), 2 * LANES)
    n_out = len(coefficients)
    shift = at // tile
    return pl.pallas_call(
        functools.partial(far_kernel, coefficients),
        grid=(width // tile,),
        in_specs=[
            pl.BlockSpec(memory_space=pl.ANY),
            pl.BlockSpec((rows, 3 * reach), lambda i: (0, 0)),
            pl.BlockSpec((reach, tile), lambda i: (0, i)),
            pl.BlockSpec((1, n_media, rows, tile), lambda i: (0, first_media // n_media, 0, i + shift)),
            pl.BlockSpec((rows, tile), lambda i: (0, i + shift)),
            pl.BlockSpec((1, n_out, rows, tile), lambda i: (0, first_field // n_out, 0, i + shift)),
        ],
        out_specs=[
            pl.BlockSpec(memory_space=pl.ANY),
            pl.BlockSpec((1, n_out, rows, tile), lambda i: (0, first_field // n_out, 0, i + shift)),
        ],
        out_shape=[
            jax.ShapeDtypeStruct(turn.shape, turn.dtype),
            jax.ShapeDtypeStruct(base.shape, base.dtype),
        ],
        input_output_aliases={0: 0, 5: 1},
        compiler_params=pltpu.CompilerParams(vmem_limit_bytes=FAR_VMEM_LIMIT),
        cost_estimate=pl.CostEstimate(
            flops=6 * rows * reach * width,
            bytes_accessed=4 * rows * width * (3 + n_media + n_out),
            transcendentals=0,
        ),
        name="add_far",
    )(turn, operator, far, media, opened, base)


def per_device(
    elastic,
    acoustic,
    el_media,
    ac_media,
    cont_matrix,
    fringe_cells,
    donor_cells,
    donor_weights,
    donor_counts,
    el_pair,
    ac_pair,
):
    rows, depth = elastic.shape[2], elastic.shape[3]
    slabs = lax.axis_size("line")
    layers = lax.axis_size("layer")
    patches = lax.axis_size("patch")
    slots = fringe_cells.shape[-1]
    groups = slots // LANES
    me = lax.axis_index("line")
    layer = lax.axis_index("layer")
    tile = min(64, rows)

    def other_slabs(value):
        parts = [
            lax.ppermute(value, "line", [(i, (i + distance) % slabs) for i in range(slabs)])
            for distance in range(1, slabs)
        ]
        return parts[0] if slabs == 2 else jnp.concatenate(parts, axis=0)

    half, quarter = depth // 2, depth // 4
    pieces = [
        ("el", 0, 0, depth, "el", 0, 3, 2, (lambda b, l, m: l + 2.0 * m, lambda b, l, m: l)),
        ("ac", 0, 0, depth, "ac", 1, 1, 1, (lambda b: -b,)),
        ("ac", 1, 0, depth, "ac", 0, 1, 0, (lambda k: -k,)),
        ("el", 1, 0, depth, "el", 2, 1, 4, (lambda m: m,)),
        ("el", 2, 0, depth, "el", 0, 1, 0, (lambda b: b,)),
        ("el", 4, 0, half, "el", 0, 1, 1, (lambda b: b,)),
        ("el", 4, half, quarter, "el", 0, 1, 1, (lambda b: b,)),
        ("el", 4, half + quarter, quarter, "el", 0, 1, 1, (lambda b: b,)),
    ]
    travelling = [piece[:4] for piece in pieces]
    (first,) = take_pieces(elastic, acoustic, travelling[:1])
    *others, edges, asked = take_pieces(
        elastic, acoustic, travelling[1:], first, donor_cells, donor_weights, layers
    )
    far = [other_slabs(value) for value in [first, *others]]

    asked = lax.all_to_all(asked, "patch", split_axis=0, concat_axis=0, tiled=True)
    asked_words = asked[:, :4].astype(jnp.int32)

    smem = pl.BlockSpec(memory_space=pltpu.SMEM)
    vmem = pl.BlockSpec(memory_space=pltpu.VMEM)
    local = pl.pallas_call(
        functools.partial(gather_kernel, 8, rows, depth),
        in_specs=[smem, smem, vmem, vmem],
        out_specs=vmem,
        out_shape=jax.ShapeDtypeStruct((patches, groups, 8, LANES), jnp.float32),
        scratch_shapes=[pltpu.VMEM((8 * rows * (depth // LANES), LANES), jnp.float32)],
        compiler_params=pltpu.CompilerParams(vmem_limit_bytes=VMEM_LIMIT),
        cost_estimate=pl.CostEstimate(flops=10**9, bytes_accessed=32 * rows * depth, transcendentals=0),
        name="donor_gather",
    )(asked_words, asked, elastic, acoustic)
    interp = lax.all_to_all(local, "patch", split_axis=0, concat_axis=0, tiled=True)
    edges = lax.all_to_all(edges, "layer", split_axis=0, concat_axis=0, tiled=True)

    near, far_operator = near_derivatives(elastic, acoustic, cont_matrix, me, slabs)
    new_el, new_ac, opened = pl.pallas_call(
        functools.partial(section_kernel, layers, rows, depth, tile),
        grid=(rows // tile,),
        in_specs=[
            smem,
            smem,
            smem,
            pl.BlockSpec((6, tile, depth), lambda i: (0, i, 0)),
            pl.BlockSpec((1, 5, tile, depth), lambda i: (0, 0, i, 0)),
            pl.BlockSpec((1, 3, tile, depth), lambda i: (0, 0, i, 0)),
            pl.BlockSpec((1, 3, tile, depth), lambda i: (0, 0, i, 0)),
            pl.BlockSpec((1, 2, tile, depth), lambda i: (0, 0, i, 0)),
            vmem,
            vmem,
            vmem,
        ],
        out_specs=[vmem, vmem, vmem],
        out_shape=[
            jax.ShapeDtypeStruct(elastic.shape, jnp.float32),
            jax.ShapeDtypeStruct(acoustic.shape, jnp.float32),
            jax.ShapeDtypeStruct((rows, depth), jnp.float32),
        ],
        scratch_shapes=[pltpu.VMEM((rows, LANES), jnp.float32)],
        compiler_params=pltpu.CompilerParams(vmem_limit_bytes=VMEM_LIMIT),
        cost_estimate=pl.CostEstimate(
            flops=100 * rows * depth, bytes_accessed=112 * rows * depth, transcendentals=0
        ),
        name="near_section",
    )(
        fringe_cells,
        donor_counts,
        interp,
        near,
        elastic,
        acoustic,
        el_media,
        ac_media,
        edges,
        el_pair,
        ac_pair,
    )

    turn = jnp.zeros((8, LANES), jnp.float32)
    section = {"el": new_el, "ac": new_ac}
    media = {"el": el_media, "ac": ac_media}
    for value, (_, _, at, _, target, first_media, n_media, first_field, coefficients) in zip(far, pieces):
        turn, section[target] = add_far(
            section[target], far_operator, value, at,
            media[target], first_media, n_media, first_field, coefficients, opened, turn,
        )
    return section["el"], section["ac"]


def solution(mesh):
    placed = (
        P("patch", None, "line", "layer"),
        P("patch", None, "line", "layer"),
        P("patch", None, "line", "layer"),
        P("patch", None, "line", "layer"),
        P(),
        P("patch", "line", "layer", None, None),
        P("patch", "line", "layer", None, None, None),
        P("patch", "line", "layer", None, None, None),
        P("patch", "line", "layer", None),
        P("patch", "line"),
        P("patch", "line"),
    )
    return jax.shard_map(
        per_device,
        mesh=mesh,
        in_specs=placed,
        out_specs=(P("patch", None, "line", "layer"), P("patch", None, "line", "layer")),
        check_vma=False,
    )
```

```python
import functools
import math

import jax
import jax.numpy as jnp
import numpy as np
from jax import lax
from jax.experimental import pallas as pl
from jax.experimental.pallas import tpu as pltpu
from jax.sharding import PartitionSpec as P

STEP = 0.25
PENALTY = 2.0
LANES = 128
MIB = 1024 * 1024
HIGHEST = lax.Precision.HIGHEST


def in_hbm(array):
    return pltpu.with_memory_space_constraint(array, pltpu.HBM)


def derivative_row(period):
    n = np.arange(1, period)
    sign = np.where(n % 2 == 0, 1.0, -1.0)
    row = np.zeros(period)
    row[1:] = (math.pi / period) * sign / np.tan(math.pi * n / period)
    return row


def operator_tables(rows, slabs, cont):
    points = rows * slabs
    period = points + cont
    row = derivative_row(period)
    j = np.arange(rows)
    own = row[(j[:, None] - j[None, :]) % period]
    far, tail = [], []
    for me in range(slabs):
        mine = me * rows + j[:, None]
        others = np.concatenate([(me - d) % slabs * rows + j for d in range(1, slabs)])
        far.append(row[(mine - others[None, :]) % period])
        tail.append(row[(mine - points - np.arange(cont)[None, :]) % period])
    return tuple(jnp.asarray(np.asarray(table, np.float32)) for table in (own, far, tail))


def continuation_on(cont_matrix, rows, slabs, sources):
    match = cont_matrix.shape[1] // 2
    on_last = jnp.pad(cont_matrix[:, :match], ((0, 0), (rows - match, 0)))
    on_first = jnp.pad(cont_matrix[:, match:], ((0, 0), (0, rows - match)))
    return jnp.concatenate(
        [
            jnp.where(source == slabs - 1, on_last, 0.0) + jnp.where(source == 0, on_first, 0.0)
            for source in sources
        ],
        axis=1,
    )


def split(value, size):
    if size & (size - 1) == 0:
        return lax.shift_right_logical(value, size.bit_length() - 1), value & (size - 1)
    return lax.div(value, size), lax.rem(value, size)


def take_kernel(pieces, elastic_ref, acoustic_ref, outs, semaphores):
    copies = []
    for i, (name, field, at, width) in enumerate(pieces):
        source = elastic_ref if name == "el" else acoustic_ref
        copies.append(pltpu.make_async_copy(source.at[0, field, :, pl.ds(at, width)], outs[i], semaphores.at[i]))
    for copy in copies:
        copy.start()
    return copies


def take_only_kernel(pieces, elastic_ref, *refs):
    for copy in take_kernel(pieces, elastic_ref, None, refs[:-1], refs[-1]):
        copy.wait()


def take_and_edges_kernel(
    pieces, layers, after_ref, elastic_ref, acoustic_ref, cells_ref, weights_ref, *refs
):
    del after_ref
    n = len(pieces)
    edges_ref, asked_ref, tiles, edge_semaphores, semaphores = refs[n:]
    n_el, n_ac = elastic_ref.shape[1], acoustic_ref.shape[1]
    rows, depth = elastic_ref.shape[2:]
    loads = []
    for end, at in enumerate((0, depth - LANES)):
        for k, (source, first, count) in enumerate(((elastic_ref, 0, n_el), (acoustic_ref, n_el, n_ac))):
            loads.append(
                pltpu.make_async_copy(
                    source.at[0, :, :, pl.ds(at, LANES)],
                    tiles.at[end, pl.ds(first, count)],
                    edge_semaphores.at[2 * end + k],
                )
            )
    copies = take_kernel(pieces, elastic_ref, acoustic_ref, refs[:n], semaphores)
    for load in loads:
        load.start()

    x, z = split(cells_ref[0, 0, 0], depth)
    chunk, at_lane = split(z, LANES)
    words = (chunk * ((n_el + n_ac) * rows) + x) * LANES + at_lane
    asked_ref[...] = jnp.concatenate([words.astype(jnp.float32), weights_ref[0, 0, 0]], axis=1)

    for load in loads:
        load.wait()
    lane = lax.broadcasted_iota(jnp.int32, (rows, LANES), 1)
    columns = jnp.zeros((rows, LANES), jnp.float32)
    for f in range(n_el + n_ac):
        columns = jnp.where(lane == f, tiles[0, f, :, 0:1], columns)
        columns = jnp.where(lane == 8 + f, tiles[1, f, :, LANES - 1 : LANES], columns)
    lines = columns.T
    below = lax.rem(lax.axis_index("layer") + 1, layers)
    for to in range(layers):
        edges_ref[to] = jnp.where(to == below, lines[8:16], lines[0:8])
    for copy in copies:
        copy.wait()


def take_pieces(elastic, acoustic, pieces, after=None, cells=None, weights=None, layers=0):
    rows = elastic.shape[2]
    anywhere = pl.BlockSpec(memory_space=pl.ANY)
    vmem = pl.BlockSpec(memory_space=pltpu.VMEM)
    out_shape = [pltpu.VMEM((rows, width), jnp.float32) for _, _, _, width in pieces]
    in_specs, out_specs = [anywhere], [vmem] * len(pieces)
    scratch = [pltpu.SemaphoreType.DMA((len(pieces),))]
    kernel, operands = functools.partial(take_only_kernel, pieces), (in_hbm(elastic),)
    if layers:
        patches, corners, slots = cells.shape[3:]
        out_shape.append(jax.ShapeDtypeStruct((layers, 8, rows), jnp.float32))
        out_shape.append(jax.ShapeDtypeStruct((patches, 2 * corners, slots), jnp.float32))
        in_specs, out_specs = [anywhere] * 3 + [vmem] * 2, out_specs + [vmem] * 2
        scratch = [pltpu.VMEM((2, 8, rows, LANES), jnp.float32), pltpu.SemaphoreType.DMA((4,))] + scratch
        kernel = functools.partial(take_and_edges_kernel, pieces, layers)
        operands = (after, in_hbm(elastic), in_hbm(acoustic), cells, weights)
    cost = sum(width for _, _, _, width in pieces) * rows
    return pl.pallas_call(
        kernel,
        in_specs=in_specs,
        out_specs=out_specs,
        out_shape=out_shape,
        scratch_shapes=scratch,
        compiler_params=pltpu.CompilerParams(vmem_limit_bytes=16 * MIB),
        cost_estimate=pl.CostEstimate(flops=0, bytes_accessed=8 * cost, transcendentals=0),
        name="take_pieces",
    )(*operands)


def gather_kernel(fields, rows, depth, words_ref, weights_ref, elastic_ref, acoustic_ref, out_ref, mixed):
    n_el = elastic_ref.shape[1]
    chunks = depth // LANES
    for f in range(fields):
        source = elastic_ref.at[0, f] if f < n_el else acoustic_ref.at[0, f - n_el]
        for c in range(chunks):
            mixed[pl.ds((c * fields + f) * rows, rows), :] = source[:, c * LANES : (c + 1) * LANES]
    lane = lax.broadcasted_iota(jnp.int32, (fields, LANES), 1)
    groups = out_ref.shape[1]

    def one_group(step, carry):
        patch, group = split(step, groups)

        def one_slot(r, values):
            slot = group * LANES + r
            total = None
            for s in range(4):
                start, at = split(words_ref[patch, s, slot], LANES)
                picked = mixed[pl.ds(start, fields, stride=rows), :]
                term = jnp.where(lane == at, picked * weights_ref[patch, 4 + s, slot], 0.0)
                total = term if total is None else total + term
            column = jnp.sum(total, axis=1, keepdims=True)
            return jnp.where(lane == r, column, values)

        values = lax.fori_loop(0, LANES, one_slot, jnp.zeros((fields, LANES), jnp.float32), unroll=16)
        out_ref[patch, group] = values
        return carry

    lax.fori_loop(0, out_ref.shape[0] * groups, one_group, 0)


def bf16_pair(value):
    high = value.astype(jnp.bfloat16)
    return high, (value - high.astype(jnp.float32)).astype(jnp.bfloat16)


def three_left(value):
    high, low = bf16_pair(value)
    return jnp.concatenate([high, high, low], axis=1)


def three_right(value):
    high, low = bf16_pair(value)
    return jnp.concatenate([high, low, high], axis=0)


def near_kernel(
    n_el, me_ref, own_ref, far_ref, tail_ref, own_cont_ref, far_cont_ref, elastic_ref, acoustic_ref,
    out_ref, far_operator_ref, operator,
):
    del me_ref

    @pl.when(pl.program_id(0) == 0)
    def _():
        def folded(table, cont):
            return table + jnp.dot(tail_ref[0], cont, precision=HIGHEST, preferred_element_type=jnp.float32)

        operator[...] = three_left(folded(own_ref[...], own_cont_ref[...]))
        far_operator_ref[...] = three_left(folded(far_ref[0], far_cont_ref[...]))

    value = jnp.where(pl.program_id(0) < n_el, elastic_ref[0, 0], acoustic_ref[0, 0])
    out_ref[0] = jnp.dot(operator[...], three_right(value), preferred_element_type=jnp.float32)


def near_derivatives(elastic, acoustic, cont_matrix, me, slabs):
    rows, depth = elastic.shape[2:]
    cont = cont_matrix.shape[0]
    reach = (slabs - 1) * rows
    own, far, tail = operator_tables(rows, slabs, cont)
    own_cont = continuation_on(cont_matrix, rows, slabs, [me])
    far_cont = continuation_on(cont_matrix, rows, slabs, [(me - d) % slabs for d in range(1, slabs)])
    return pl.pallas_call(
        functools.partial(near_kernel, 4),
        grid_spec=pltpu.PrefetchScalarGridSpec(
            num_scalar_prefetch=1,
            grid=(6,),
            in_specs=[
                pl.BlockSpec((rows, rows), lambda f, me: (0, 0)),
                pl.BlockSpec((1, rows, reach), lambda f, me: (me[0], 0, 0)),
                pl.BlockSpec((1, rows, cont), lambda f, me: (me[0], 0, 0)),
                pl.BlockSpec((cont, rows), lambda f, me: (0, 0)),
                pl.BlockSpec((cont, reach), lambda f, me: (0, 0)),
                pl.BlockSpec((1, 1, rows, depth), lambda f, me: (0, jnp.where(f < 3, f, 4), 0, 0)),
                pl.BlockSpec((1, 1, rows, depth), lambda f, me: (0, jnp.maximum(f - 4, 0), 0, 0)),
            ],
            out_specs=[
                pl.BlockSpec((1, rows, depth), lambda f, me: (f, 0, 0)),
                pl.BlockSpec((rows, 3 * reach), lambda f, me: (0, 0)),
            ],
            scratch_shapes=[pltpu.VMEM((rows, 3 * rows), jnp.bfloat16)],
        ),
        out_shape=[
            pltpu.VMEM((6, rows, depth), jnp.float32),
            pltpu.VMEM((rows, 3 * reach), jnp.bfloat16),
        ],
        compiler_params=pltpu.CompilerParams(vmem_limit_bytes=24 * MIB),
        cost_estimate=pl.CostEstimate(
            flops=36 * rows * rows * depth, bytes_accessed=60 * rows * depth, transcendentals=0
        ),
        name="near_dx",
    )(
        me.reshape(1), in_hbm(own), in_hbm(far), in_hbm(tail), own_cont, far_cont, in_hbm(elastic), in_hbm(acoustic)
    )


def section_kernel(
    layers, rows, depth, tile,
    cells_ref, counts_ref, interp_ref,
    dx_ref, elastic_ref, acoustic_ref, el_media_ref, ac_media_ref, edges_ref, el_pair_ref, ac_pair_ref,
    new_el_ref, new_ac_ref, open_ref,
    columns,
):
    step = pl.program_id(0)
    here = pl.ds(pl.multiple_of(step * tile, tile), tile)
    lane = lax.broadcasted_iota(jnp.int32, (tile, depth), 1)
    layer = lax.axis_index("layer")
    at_top, at_bottom = layer == 0, layer == layers - 1
    from_above = edges_ref[lax.rem(layer + layers - 1, layers)]
    from_below = edges_ref[lax.rem(layer + 1, layers)]
    ocean_row = from_above[5:6]
    basin_row = from_below[1:2]

    @pl.when(step == 0)
    def _():
        pairs = jnp.concatenate([el_pair_ref[...], ac_pair_ref[...]]).astype(jnp.float32)
        lines = [
            jnp.where(at_top, 0.0, from_above),
            jnp.where(at_bottom, 0.0, from_below),
            pairs,
            jnp.zeros((LANES - 18, rows), jnp.float32),
        ]
        columns[...] = jnp.concatenate(lines).T

    halo = columns[here, :]

    def dz(value, slot):
        above = halo[:, slot : slot + 1]
        below = halo[:, 8 + slot : 9 + slot]
        following = jnp.where(lane == depth - 1, below, pltpu.roll(value, depth - 1, 1))
        previous = jnp.where(lane == 0, above, pltpu.roll(value, 1, 1))
        return (following - previous) * 0.5

    vx, vz, sxx, szz, sxz = [elastic_ref[0, f] for f in range(5)]
    p, ovx, ovz = [acoustic_ref[0, f] for f in range(3)]
    buoyancy = el_media_ref[0, 0]
    lame = el_media_ref[0, 1]
    shear = el_media_ref[0, 2]
    stiffness = lame + 2.0 * shear
    bulk = ac_media_ref[0, 0]
    ocean_buoyancy = ac_media_ref[0, 1]

    dx_vx = dx_ref[0]
    dz_vz = dz(vz, 1)
    new_el_ref[0, 0, here, :] = vx + STEP * (buoyancy * (dx_ref[2] + dz(sxz, 4)))
    new_el_ref[0, 1, here, :] = vz + STEP * (buoyancy * (dx_ref[3] + dz(szz, 3)))
    new_el_ref[0, 2, here, :] = sxx + STEP * (stiffness * dx_vx + lame * dz_vz)
    choose = lax.broadcasted_iota(jnp.int32, (tile, rows), 1).astype(jnp.float32)
    pressure = jnp.sum(jnp.where(halo[:, 16:17] == choose, ocean_row, 0.0), axis=1, keepdims=True)
    velocity = jnp.sum(jnp.where(halo[:, 17:18] == choose, basin_row, 0.0), axis=1, keepdims=True)
    rate_szz = lame * dx_vx + stiffness * dz_vz
    rate_szz = rate_szz + jnp.where((lane == 0) & at_top, PENALTY * (-pressure - szz), 0.0)
    new_el_ref[0, 3, here, :] = szz + STEP * rate_szz
    new_el_ref[0, 4, here, :] = sxz + STEP * (shear * (dz(vx, 0) + dx_ref[1]))
    new_ac_ref[0, 0, here, :] = p - STEP * (bulk * (dx_ref[5] + dz(ovz, 7)))
    new_ac_ref[0, 1, here, :] = ovx - STEP * (ocean_buoyancy * dx_ref[4])
    rate_ovz = -ocean_buoyancy * dz(p, 5)
    rate_ovz = rate_ovz + jnp.where((lane == depth - 1) & at_bottom, PENALTY * (velocity - ovz), 0.0)
    new_ac_ref[0, 2, here, :] = ovz + STEP * rate_ovz
    open_ref[here, :] = jnp.ones((tile, depth), jnp.float32)

    @pl.when(step == pl.num_programs(0) - 1)
    def _():
        place = lax.broadcasted_iota(jnp.int32, (8, LANES), 0) * LANES
        place = place + lax.broadcasted_iota(jnp.int32, (8, LANES), 1)
        n_el = new_el_ref.shape[1]

        def one_patch(q, carry):
            def one_slot(r, inner):
                x, z = split(cells_ref[0, 0, 0, q, r], depth)
                (high, row), (low, at) = split(x, 8), split(z, LANES)
                at_row = pl.ds(pl.multiple_of(high * 8, 8), 8)
                at_lane = pl.ds(pl.multiple_of(low * LANES, LANES), LANES)
                hit = place == row * LANES + at
                group, within = split(r, LANES)
                for f in range(8):
                    target = new_el_ref.at[0, f] if f < n_el else new_ac_ref.at[0, f - n_el]
                    target[at_row, at_lane] = jnp.where(hit, interp_ref[q, group, f, within], target[at_row, at_lane])
                open_ref[at_row, at_lane] = jnp.where(hit, 0.0, open_ref[at_row, at_lane])
                return inner

            return lax.fori_loop(0, counts_ref[0, 0, 0, q], one_slot, carry)

        lax.fori_loop(0, counts_ref.shape[3], one_patch, 0)


def far_kernel(coefficients, turn_ref, d_ref, far_ref, media_ref, open_ref, base_ref, next_ref, out_ref):
    del turn_ref, next_ref
    far = jnp.dot(d_ref[...], three_right(far_ref[...]), preferred_element_type=jnp.float32)
    media = [media_ref[0, i] for i in range(media_ref.shape[1])]
    is_open = open_ref[...] > 0.5
    for i, coefficient in enumerate(coefficients):
        old = base_ref[0, i]
        out_ref[0, i] = jnp.where(is_open, old + (STEP * coefficient(*media)) * far, old)


def add_far(base, operator, far, at, media, first_media, n_media, first_field, coefficients, opened, turn):
    rows, reach = operator.shape[0], far.shape[0]
    width = far.shape[1]
    tile = math.gcd(math.gcd(width, at), 2 * LANES)
    n_out = len(coefficients)
    shift = at // tile
    return pl.pallas_call(
        functools.partial(far_kernel, coefficients),
        grid=(width // tile,),
        in_specs=[
            pl.BlockSpec(memory_space=pl.ANY),
            pl.BlockSpec((rows, 3 * reach), lambda i: (0, 0)),
            pl.BlockSpec((reach, tile), lambda i: (0, i)),
            pl.BlockSpec((1, n_media, rows, tile), lambda i: (0, first_media // n_media, 0, i + shift)),
            pl.BlockSpec((rows, tile), lambda i: (0, i + shift)),
            pl.BlockSpec((1, n_out, rows, tile), lambda i: (0, first_field // n_out, 0, i + shift)),
        ],
        out_specs=[
            pl.BlockSpec(memory_space=pl.ANY),
            pl.BlockSpec((1, n_out, rows, tile), lambda i: (0, first_field // n_out, 0, i + shift)),
        ],
        out_shape=[
            jax.ShapeDtypeStruct(turn.shape, turn.dtype),
            jax.ShapeDtypeStruct(base.shape, base.dtype),
        ],
        input_output_aliases={0: 0, 5: 1},
        compiler_params=pltpu.CompilerParams(vmem_limit_bytes=16 * MIB),
        cost_estimate=pl.CostEstimate(
            flops=6 * rows * reach * width,
            bytes_accessed=4 * rows * width * (3 + n_media + n_out),
            transcendentals=0,
        ),
        name="add_far",
    )(turn, operator, far, in_hbm(media), opened, base)


def per_device(
    elastic,
    acoustic,
    el_media,
    ac_media,
    cont_matrix,
    fringe_cells,
    donor_cells,
    donor_weights,
    donor_counts,
    el_pair,
    ac_pair,
):
    rows, depth = elastic.shape[2], elastic.shape[3]
    slabs = lax.axis_size("line")
    layers = lax.axis_size("layer")
    patches = lax.axis_size("patch")
    slots = fringe_cells.shape[-1]
    groups = slots // LANES
    me = lax.axis_index("line")
    layer = lax.axis_index("layer")
    tile = min(64, rows)

    def other_slabs(value):
        parts = [
            lax.ppermute(value, "line", [(i, (i + distance) % slabs) for i in range(slabs)])
            for distance in range(1, slabs)
        ]
        return parts[0] if slabs == 2 else jnp.concatenate(parts, axis=0)

    half, quarter = depth // 2, depth // 4
    pieces = [
        ("el", 0, 0, depth, "el", 0, 3, 2, (lambda b, l, m: l + 2.0 * m, lambda b, l, m: l)),
        ("ac", 0, 0, depth, "ac", 1, 1, 1, (lambda b: -b,)),
        ("ac", 1, 0, depth, "ac", 0, 1, 0, (lambda k: -k,)),
        ("el", 1, 0, depth, "el", 2, 1, 4, (lambda m: m,)),
        ("el", 2, 0, depth, "el", 0, 1, 0, (lambda b: b,)),
        ("el", 4, 0, half, "el", 0, 1, 1, (lambda b: b,)),
        ("el", 4, half, quarter, "el", 0, 1, 1, (lambda b: b,)),
        ("el", 4, half + quarter, quarter, "el", 0, 1, 1, (lambda b: b,)),
    ]
    travelling = [piece[:4] for piece in pieces]
    (first,) = take_pieces(elastic, acoustic, travelling[:1])
    *others, edges, asked = take_pieces(
        elastic, acoustic, travelling[1:], first, donor_cells, donor_weights, layers
    )
    far = [other_slabs(value) for value in [first, *others]]

    asked = lax.all_to_all(asked, "patch", split_axis=0, concat_axis=0, tiled=True)
    asked_words = asked[:, :4].astype(jnp.int32)

    smem = pl.BlockSpec(memory_space=pltpu.SMEM)
    vmem = pl.BlockSpec(memory_space=pltpu.VMEM)
    local = pl.pallas_call(
        functools.partial(gather_kernel, 8, rows, depth),
        in_specs=[smem, smem, vmem, vmem],
        out_specs=vmem,
        out_shape=jax.ShapeDtypeStruct((patches, groups, 8, LANES), jnp.float32),
        scratch_shapes=[pltpu.VMEM((8 * rows * (depth // LANES), LANES), jnp.float32)],
        compiler_params=pltpu.CompilerParams(vmem_limit_bytes=24 * MIB),
        cost_estimate=pl.CostEstimate(flops=10**9, bytes_accessed=32 * rows * depth, transcendentals=0),
        name="donor_gather",
    )(asked_words, asked, in_hbm(elastic), in_hbm(acoustic))
    interp = lax.all_to_all(local, "patch", split_axis=0, concat_axis=0, tiled=True)
    edges = lax.all_to_all(edges, "layer", split_axis=0, concat_axis=0, tiled=True)

    near, far_operator = near_derivatives(elastic, acoustic, cont_matrix, me, slabs)
    new_el, new_ac, opened = pl.pallas_call(
        functools.partial(section_kernel, layers, rows, depth, tile),
        grid=(rows // tile,),
        in_specs=[
            smem,
            smem,
            smem,
            pl.BlockSpec((6, tile, depth), lambda i: (0, i, 0)),
            pl.BlockSpec((1, 5, tile, depth), lambda i: (0, 0, i, 0)),
            pl.BlockSpec((1, 3, tile, depth), lambda i: (0, 0, i, 0)),
            pl.BlockSpec((1, 3, tile, depth), lambda i: (0, 0, i, 0)),
            pl.BlockSpec((1, 2, tile, depth), lambda i: (0, 0, i, 0)),
            vmem,
            vmem,
            vmem,
        ],
        out_specs=[vmem, vmem, vmem],
        out_shape=[
            jax.ShapeDtypeStruct(elastic.shape, jnp.float32),
            jax.ShapeDtypeStruct(acoustic.shape, jnp.float32),
            pltpu.VMEM((rows, depth), jnp.float32),
        ],
        scratch_shapes=[pltpu.VMEM((rows, LANES), jnp.float32)],
        compiler_params=pltpu.CompilerParams(vmem_limit_bytes=32 * MIB),
        cost_estimate=pl.CostEstimate(
            flops=100 * rows * depth, bytes_accessed=112 * rows * depth, transcendentals=0
        ),
        name="near_section",
    )(
        fringe_cells,
        donor_counts,
        interp,
        near,
        in_hbm(elastic),
        in_hbm(acoustic),
        in_hbm(el_media),
        in_hbm(ac_media),
        edges,
        el_pair,
        ac_pair,
    )

    turn = jnp.zeros((8, LANES), jnp.float32)
    section = {"el": new_el, "ac": new_ac}
    media = {"el": el_media, "ac": ac_media}
    for value, (_, _, at, _, target, first_media, n_media, first_field, coefficients) in zip(far, pieces):
        turn, section[target] = add_far(
            section[target], far_operator, value, at,
            media[target], first_media, n_media, first_field, coefficients, opened, turn,
        )
    return section["el"], section["ac"]


def solution(mesh):
    placed = (
        P("patch", None, "line", "layer"),
        P("patch", None, "line", "layer"),
        P("patch", None, "line", "layer"),
        P("patch", None, "line", "layer"),
        P(),
        P("patch", "line", "layer", None, None),
        P("patch", "line", "layer", None, None, None),
        P("patch", "line", "layer", None, None, None),
        P("patch", "line", "layer", None),
        P("patch", "line"),
        P("patch", "line"),
    )
    return jax.shard_map(
        per_device,
        mesh=mesh,
        in_specs=placed,
        out_specs=(P("patch", None, "line", "layer"), P("patch", None, "line", "layer")),
        check_vma=False,
    )
```

```python
import functools
import math

import jax
import jax.numpy as jnp
import numpy as np
from jax import lax
from jax.experimental import pallas as pl
from jax.experimental.pallas import tpu as pltpu
from jax.sharding import PartitionSpec as P

STEP = 0.25
PENALTY = 2.0
LANES = 128
MIB = 1024 * 1024
HIGHEST = lax.Precision.HIGHEST


def in_hbm(array):
    return pltpu.with_memory_space_constraint(array, pltpu.HBM)


def derivative_row(period):
    n = np.arange(1, period)
    sign = np.where(n % 2 == 0, 1.0, -1.0)
    row = np.zeros(period)
    row[1:] = (math.pi / period) * sign / np.tan(math.pi * n / period)
    return row


def operator_tables(rows, slabs, cont):
    points = rows * slabs
    period = points + cont
    row = derivative_row(period)
    j = np.arange(rows)
    own = row[(j[:, None] - j[None, :]) % period]
    far, tail = [], []
    for me in range(slabs):
        mine = me * rows + j[:, None]
        others = np.concatenate([(me - d) % slabs * rows + j for d in range(1, slabs)])
        far.append(row[(mine - others[None, :]) % period])
        tail.append(row[(mine - points - np.arange(cont)[None, :]) % period])
    return tuple(jnp.asarray(np.asarray(table, np.float32)) for table in (own, far, tail))


def continuation_on(cont_matrix, rows, slabs, sources):
    match = cont_matrix.shape[1] // 2
    on_last = jnp.pad(cont_matrix[:, :match], ((0, 0), (rows - match, 0)))
    on_first = jnp.pad(cont_matrix[:, match:], ((0, 0), (0, rows - match)))
    return jnp.concatenate(
        [
            jnp.where(source == slabs - 1, on_last, 0.0) + jnp.where(source == 0, on_first, 0.0)
            for source in sources
        ],
        axis=1,
    )


def split(value, size):
    if size & (size - 1) == 0:
        return lax.shift_right_logical(value, size.bit_length() - 1), value & (size - 1)
    return lax.div(value, size), lax.rem(value, size)


def take_kernel(pieces, parts, elastic_ref, acoustic_ref, *refs):
    n = len(pieces)
    outs, held, in_semaphores, out_semaphores = refs[:n], refs[n : 2 * n], refs[-2], refs[-1]
    rows = elastic_ref.shape[2]
    loads, stores = [], []
    for i, (name, field, at, width) in enumerate(pieces):
        source = elastic_ref if name == "el" else acoustic_ref
        for part in range(parts):
            here = pl.ds(part * (rows // parts), rows // parts)
            k = i * parts + part
            loads.append(
                pltpu.make_async_copy(source.at[0, field, here, pl.ds(at, width)], held[i].at[here], in_semaphores.at[k])
            )
            stores.append(pltpu.make_async_copy(held[i].at[here], outs[i].at[here], out_semaphores.at[k]))
    for load in loads:
        load.start()
    for load, store in zip(loads, stores):
        load.wait()
        store.start()
    return stores


def take_first_kernel(field, elastic_ref, out_ref, semaphore):
    copy = pltpu.make_async_copy(elastic_ref.at[0, field], out_ref, semaphore)
    copy.start()
    copy.wait()


def take_first(elastic, field):
    rows, depth = elastic.shape[2:]
    return pl.pallas_call(
        functools.partial(take_first_kernel, field),
        in_specs=[pl.BlockSpec(memory_space=pl.ANY)],
        out_specs=pl.BlockSpec(memory_space=pltpu.VMEM),
        out_shape=pltpu.VMEM((rows, depth), jnp.float32),
        scratch_shapes=[pltpu.SemaphoreType.DMA],
        compiler_params=pltpu.CompilerParams(vmem_limit_bytes=16 * MIB),
        cost_estimate=pl.CostEstimate(flops=0, bytes_accessed=8 * rows * depth, transcendentals=0),
        name="take_first",
    )(in_hbm(elastic))


def take_and_edges_kernel(
    pieces, parts, layers, after_ref, elastic_ref, acoustic_ref, cells_ref, weights_ref, *refs
):
    del after_ref
    n = len(pieces)
    edges_ref, asked_ref, tiles, edge_semaphores = refs[n : n + 4]
    n_el, n_ac = elastic_ref.shape[1], acoustic_ref.shape[1]
    rows, depth = elastic_ref.shape[2:]
    loads = []
    for end, at in enumerate((0, depth - LANES)):
        for k, (source, first, count) in enumerate(((elastic_ref, 0, n_el), (acoustic_ref, n_el, n_ac))):
            loads.append(
                pltpu.make_async_copy(
                    source.at[0, :, :, pl.ds(at, LANES)],
                    tiles.at[end, pl.ds(first, count)],
                    edge_semaphores.at[2 * end + k],
                )
            )
    for load in loads:
        load.start()
    stores = take_kernel(pieces, parts, elastic_ref, acoustic_ref, *refs[:n], *refs[n + 4 :])

    x, z = split(cells_ref[0, 0, 0], depth)
    chunk, at_lane = split(z, LANES)
    words = (chunk * ((n_el + n_ac) * rows) + x) * LANES + at_lane
    asked_ref[...] = jnp.concatenate([words.astype(jnp.float32), weights_ref[0, 0, 0]], axis=1)

    for load in loads:
        load.wait()
    lane = lax.broadcasted_iota(jnp.int32, (rows, LANES), 1)
    columns = jnp.zeros((rows, LANES), jnp.float32)
    for f in range(n_el + n_ac):
        columns = jnp.where(lane == f, tiles[0, f, :, 0:1], columns)
        columns = jnp.where(lane == 8 + f, tiles[1, f, :, LANES - 1 : LANES], columns)
    lines = columns.T
    below = lax.rem(lax.axis_index("layer") + 1, layers)
    for to in range(layers):
        edges_ref[to] = jnp.where(to == below, lines[8:16], lines[0:8])
    for store in stores:
        store.wait()


def take_pieces(elastic, acoustic, pieces, after, cells, weights, layers):
    rows = elastic.shape[2]
    anywhere = pl.BlockSpec(memory_space=pl.ANY)
    vmem = pl.BlockSpec(memory_space=pltpu.VMEM)
    out_shape = [jax.ShapeDtypeStruct((rows, width), jnp.float32) for _, _, _, width in pieces]
    parts = 2
    scratch = [pltpu.VMEM((2, 8, rows, LANES), jnp.float32), pltpu.SemaphoreType.DMA((4,))]
    scratch += [pltpu.VMEM((rows, width), jnp.float32) for _, _, _, width in pieces]
    scratch += [pltpu.SemaphoreType.DMA((len(pieces) * parts,))] * 2
    patches, corners, slots = cells.shape[3:]
    out_shape.append(jax.ShapeDtypeStruct((layers, 8, rows), jnp.float32))
    out_shape.append(jax.ShapeDtypeStruct((patches, 2 * corners, slots), jnp.float32))
    cost = sum(width for _, _, _, width in pieces) * rows
    return pl.pallas_call(
        functools.partial(take_and_edges_kernel, pieces, parts, layers),
        in_specs=[anywhere] * 3 + [vmem] * 2,
        out_specs=[anywhere] * len(pieces) + [vmem] * 2,
        out_shape=out_shape,
        scratch_shapes=scratch,
        compiler_params=pltpu.CompilerParams(vmem_limit_bytes=24 * MIB),
        cost_estimate=pl.CostEstimate(flops=0, bytes_accessed=8 * cost, transcendentals=0),
        name="take_pieces",
    )(after, in_hbm(elastic), in_hbm(acoustic), cells, weights)


def gather_kernel(fields, rows, depth, words_ref, weights_ref, elastic_ref, acoustic_ref, out_ref, mixed):
    n_el = elastic_ref.shape[1]
    chunks = depth // LANES
    for f in range(fields):
        source = elastic_ref.at[0, f] if f < n_el else acoustic_ref.at[0, f - n_el]
        for c in range(chunks):
            mixed[pl.ds((c * fields + f) * rows, rows), :] = source[:, c * LANES : (c + 1) * LANES]
    lane = lax.broadcasted_iota(jnp.int32, (fields, LANES), 1)
    groups = out_ref.shape[1]

    def one_group(step, carry):
        patch, group = split(step, groups)

        def one_slot(r, values):
            slot = group * LANES + r
            total = None
            for s in range(4):
                start, at = split(words_ref[patch, s, slot], LANES)
                picked = mixed[pl.ds(start, fields, stride=rows), :]
                term = jnp.where(lane == at, picked * weights_ref[patch, 4 + s, slot], 0.0)
                total = term if total is None else total + term
            column = jnp.sum(total, axis=1, keepdims=True)
            return jnp.where(lane == r, column, values)

        values = lax.fori_loop(0, LANES, one_slot, jnp.zeros((fields, LANES), jnp.float32), unroll=16)
        out_ref[patch, group] = values
        return carry

    lax.fori_loop(0, out_ref.shape[0] * groups, one_group, 0)


def bf16_pair(value):
    high = value.astype(jnp.bfloat16)
    return high, (value - high.astype(jnp.float32)).astype(jnp.bfloat16)


def three_left(value):
    high, low = bf16_pair(value)
    return jnp.concatenate([high, high, low], axis=1)


def three_right(value):
    high, low = bf16_pair(value)
    return jnp.concatenate([high, low, high], axis=0)


def near_kernel(
    n_el, me_ref, own_ref, far_ref, tail_ref, own_cont_ref, far_cont_ref, elastic_ref, acoustic_ref,
    out_ref, far_operator_ref, operator,
):
    del me_ref

    @pl.when(pl.program_id(0) == 0)
    def _():
        def folded(table, cont):
            return table + jnp.dot(tail_ref[0], cont, precision=HIGHEST, preferred_element_type=jnp.float32)

        operator[...] = three_left(folded(own_ref[...], own_cont_ref[...]))
        far_operator_ref[...] = three_left(folded(far_ref[0], far_cont_ref[...]))

    value = jnp.where(pl.program_id(0) < n_el, elastic_ref[0, 0], acoustic_ref[0, 0])
    out_ref[0] = jnp.dot(operator[...], three_right(value), preferred_element_type=jnp.float32)


def near_derivatives(elastic, acoustic, cont_matrix, me, slabs):
    rows, depth = elastic.shape[2:]
    cont = cont_matrix.shape[0]
    reach = (slabs - 1) * rows
    own, far, tail = operator_tables(rows, slabs, cont)
    own_cont = continuation_on(cont_matrix, rows, slabs, [me])
    far_cont = continuation_on(cont_matrix, rows, slabs, [(me - d) % slabs for d in range(1, slabs)])
    return pl.pallas_call(
        functools.partial(near_kernel, 4),
        grid_spec=pltpu.PrefetchScalarGridSpec(
            num_scalar_prefetch=1,
            grid=(6,),
            in_specs=[
                pl.BlockSpec((rows, rows), lambda f, me: (0, 0)),
                pl.BlockSpec((1, rows, reach), lambda f, me: (me[0], 0, 0)),
                pl.BlockSpec((1, rows, cont), lambda f, me: (me[0], 0, 0)),
                pl.BlockSpec((cont, rows), lambda f, me: (0, 0)),
                pl.BlockSpec((cont, reach), lambda f, me: (0, 0)),
                pl.BlockSpec((1, 1, rows, depth), lambda f, me: (0, jnp.where(f < 3, f, 4), 0, 0)),
                pl.BlockSpec((1, 1, rows, depth), lambda f, me: (0, jnp.maximum(f - 4, 0), 0, 0)),
            ],
            out_specs=[
                pl.BlockSpec((1, rows, depth), lambda f, me: (f, 0, 0)),
                pl.BlockSpec((rows, 3 * reach), lambda f, me: (0, 0)),
            ],
            scratch_shapes=[pltpu.VMEM((rows, 3 * rows), jnp.bfloat16)],
        ),
        out_shape=[
            pltpu.HBM((6, rows, depth), jnp.float32),
            pltpu.VMEM((rows, 3 * reach), jnp.bfloat16),
        ],
        compiler_params=pltpu.CompilerParams(vmem_limit_bytes=24 * MIB),
        cost_estimate=pl.CostEstimate(
            flops=36 * rows * rows * depth, bytes_accessed=60 * rows * depth, transcendentals=0
        ),
        name="near_dx",
    )(
        me.reshape(1), in_hbm(own), in_hbm(far), in_hbm(tail), own_cont, far_cont, in_hbm(elastic), in_hbm(acoustic)
    )


def section_kernel(
    layers, rows, depth, tile,
    cells_ref, counts_ref, interp_ref,
    dx_ref, elastic_ref, acoustic_ref, el_media_ref, ac_media_ref, edges_ref, el_pair_ref, ac_pair_ref,
    new_el_ref, new_ac_ref, open_ref,
    columns,
):
    step = pl.program_id(0)
    here = pl.ds(pl.multiple_of(step * tile, tile), tile)
    lane = lax.broadcasted_iota(jnp.int32, (tile, depth), 1)
    layer = lax.axis_index("layer")
    at_top, at_bottom = layer == 0, layer == layers - 1
    from_above = edges_ref[lax.rem(layer + layers - 1, layers)]
    from_below = edges_ref[lax.rem(layer + 1, layers)]
    ocean_row = from_above[5:6]
    basin_row = from_below[1:2]

    @pl.when(step == 0)
    def _():
        pairs = jnp.concatenate([el_pair_ref[...], ac_pair_ref[...]]).astype(jnp.float32)
        lines = [
            jnp.where(at_top, 0.0, from_above),
            jnp.where(at_bottom, 0.0, from_below),
            pairs,
            jnp.zeros((LANES - 18, rows), jnp.float32),
        ]
        columns[...] = jnp.concatenate(lines).T

    halo = columns[here, :]

    def dz(value, slot):
        above = halo[:, slot : slot + 1]
        below = halo[:, 8 + slot : 9 + slot]
        following = jnp.where(lane == depth - 1, below, pltpu.roll(value, depth - 1, 1))
        previous = jnp.where(lane == 0, above, pltpu.roll(value, 1, 1))
        return (following - previous) * 0.5

    vx, vz, sxx, szz, sxz = [elastic_ref[0, f] for f in range(5)]
    p, ovx, ovz = [acoustic_ref[0, f] for f in range(3)]
    buoyancy = el_media_ref[0, 0]
    lame = el_media_ref[0, 1]
    shear = el_media_ref[0, 2]
    stiffness = lame + 2.0 * shear
    bulk = ac_media_ref[0, 0]
    ocean_buoyancy = ac_media_ref[0, 1]

    dx_vx = dx_ref[0]
    dz_vz = dz(vz, 1)
    new_el_ref[0, 0, here, :] = vx + STEP * (buoyancy * (dx_ref[2] + dz(sxz, 4)))
    new_el_ref[0, 1, here, :] = vz + STEP * (buoyancy * (dx_ref[3] + dz(szz, 3)))
    new_el_ref[0, 2, here, :] = sxx + STEP * (stiffness * dx_vx + lame * dz_vz)
    choose = lax.broadcasted_iota(jnp.int32, (tile, rows), 1).astype(jnp.float32)
    pressure = jnp.sum(jnp.where(halo[:, 16:17] == choose, ocean_row, 0.0), axis=1, keepdims=True)
    velocity = jnp.sum(jnp.where(halo[:, 17:18] == choose, basin_row, 0.0), axis=1, keepdims=True)
    rate_szz = lame * dx_vx + stiffness * dz_vz
    rate_szz = rate_szz + jnp.where((lane == 0) & at_top, PENALTY * (-pressure - szz), 0.0)
    new_el_ref[0, 3, here, :] = szz + STEP * rate_szz
    new_el_ref[0, 4, here, :] = sxz + STEP * (shear * (dz(vx, 0) + dx_ref[1]))
    new_ac_ref[0, 0, here, :] = p - STEP * (bulk * (dx_ref[5] + dz(ovz, 7)))
    new_ac_ref[0, 1, here, :] = ovx - STEP * (ocean_buoyancy * dx_ref[4])
    rate_ovz = -ocean_buoyancy * dz(p, 5)
    rate_ovz = rate_ovz + jnp.where((lane == depth - 1) & at_bottom, PENALTY * (velocity - ovz), 0.0)
    new_ac_ref[0, 2, here, :] = ovz + STEP * rate_ovz
    open_ref[here, :] = jnp.ones((tile, depth), jnp.float32)

    @pl.when(step == pl.num_programs(0) - 1)
    def _():
        place = lax.broadcasted_iota(jnp.int32, (8, LANES), 0) * LANES
        place = place + lax.broadcasted_iota(jnp.int32, (8, LANES), 1)
        n_el = new_el_ref.shape[1]

        def one_patch(q, carry):
            def one_slot(r, inner):
                x, z = split(cells_ref[0, 0, 0, q, r], depth)
                (high, row), (low, at) = split(x, 8), split(z, LANES)
                at_row = pl.ds(pl.multiple_of(high * 8, 8), 8)
                at_lane = pl.ds(pl.multiple_of(low * LANES, LANES), LANES)
                hit = place == row * LANES + at
                group, within = split(r, LANES)
                for f in range(8):
                    target = new_el_ref.at[0, f] if f < n_el else new_ac_ref.at[0, f - n_el]
                    target[at_row, at_lane] = jnp.where(hit, interp_ref[q, group, f, within], target[at_row, at_lane])
                open_ref[at_row, at_lane] = jnp.where(hit, 0.0, open_ref[at_row, at_lane])
                return inner

            return lax.fori_loop(0, counts_ref[0, 0, 0, q], one_slot, carry)

        lax.fori_loop(0, counts_ref.shape[3], one_patch, 0)


def far_kernel(coefficients, turn_ref, d_ref, far_ref, media_ref, open_ref, base_ref, next_ref, out_ref):
    del turn_ref, next_ref
    far = jnp.dot(d_ref[...], three_right(far_ref[...]), preferred_element_type=jnp.float32)
    media = [media_ref[0, i] for i in range(media_ref.shape[1])]
    is_open = open_ref[...] > 0.5
    for i, coefficient in enumerate(coefficients):
        old = base_ref[0, i]
        out_ref[0, i] = jnp.where(is_open, old + (STEP * coefficient(*media)) * far, old)


def add_far(base, operator, far, at, media, first_media, n_media, first_field, coefficients, opened, turn):
    rows, reach = operator.shape[0], far.shape[0]
    width = far.shape[1]
    tile = math.gcd(math.gcd(width, at), 2 * LANES)
    n_out = len(coefficients)
    shift = at // tile
    return pl.pallas_call(
        functools.partial(far_kernel, coefficients),
        grid=(width // tile,),
        in_specs=[
            pl.BlockSpec(memory_space=pl.ANY),
            pl.BlockSpec((rows, 3 * reach), lambda i: (0, 0)),
            pl.BlockSpec((reach, tile), lambda i: (0, i)),
            pl.BlockSpec((1, n_media, rows, tile), lambda i: (0, first_media // n_media, 0, i + shift)),
            pl.BlockSpec((rows, tile), lambda i: (0, i + shift)),
            pl.BlockSpec((1, n_out, rows, tile), lambda i: (0, first_field // n_out, 0, i + shift)),
        ],
        out_specs=[
            pl.BlockSpec(memory_space=pl.ANY),
            pl.BlockSpec((1, n_out, rows, tile), lambda i: (0, first_field // n_out, 0, i + shift)),
        ],
        out_shape=[
            jax.ShapeDtypeStruct(turn.shape, turn.dtype),
            jax.ShapeDtypeStruct(base.shape, base.dtype),
        ],
        input_output_aliases={0: 0, 5: 1},
        compiler_params=pltpu.CompilerParams(vmem_limit_bytes=16 * MIB),
        cost_estimate=pl.CostEstimate(
            flops=6 * rows * reach * width,
            bytes_accessed=4 * rows * width * (3 + n_media + n_out),
            transcendentals=0,
        ),
        name="add_far",
    )(turn, operator, far, in_hbm(media), opened, base)


def prepare_kernel(coefficient, field, at, base_ref, media_ref, open_ref, same_ref, old_ref, scale_ref, semaphore):
    del same_ref
    load = pltpu.make_async_copy(base_ref.at[0, field, :, pl.ds(at, old_ref.shape[1])], old_ref, semaphore)
    load.start()
    scale_ref[...] = jnp.where(open_ref[...] > 0.5, STEP * coefficient(media_ref[0, 0]), 0.0)
    load.wait()


def prepare_last(base, media, first_media, field, coefficient, opened, at, width):
    rows = opened.shape[0]
    anywhere = pl.BlockSpec(memory_space=pl.ANY)
    vmem = pl.BlockSpec(memory_space=pltpu.VMEM)
    return pl.pallas_call(
        functools.partial(prepare_kernel, coefficient, field, at),
        grid=(1,),
        in_specs=[
            anywhere,
            pl.BlockSpec((1, 1, rows, width), lambda i: (0, first_media, 0, at // width)),
            pl.BlockSpec((rows, width), lambda i: (0, at // width)),
        ],
        out_specs=[anywhere, vmem, vmem],
        out_shape=[
            jax.ShapeDtypeStruct(base.shape, base.dtype),
            pltpu.VMEM((rows, width), jnp.float32),
            pltpu.VMEM((rows, width), jnp.float32),
        ],
        scratch_shapes=[pltpu.SemaphoreType.DMA],
        input_output_aliases={0: 0},
        compiler_params=pltpu.CompilerParams(vmem_limit_bytes=16 * MIB),
        cost_estimate=pl.CostEstimate(flops=rows * width, bytes_accessed=20 * rows * width, transcendentals=0),
        name="prepare_last",
    )(base, in_hbm(media), opened)


def finish_kernel(field, at, parts, d_ref, far_ref, old_ref, scale_ref, base_ref, out_ref, held, semaphores):
    del base_ref
    rows, width = old_ref.shape[0] // parts, old_ref.shape[1]
    far_field = three_right(far_ref[...])
    stores = []
    for part in range(parts):
        here = pl.ds(part * rows, rows)
        far = jnp.dot(d_ref[here, :], far_field, preferred_element_type=jnp.float32)
        held[here, :] = old_ref[here, :] + scale_ref[here, :] * far
        stores.append(
            pltpu.make_async_copy(
                held.at[here], out_ref.at[0, field, here, pl.ds(at, width)], semaphores.at[part]
            )
        )
        stores[-1].start()
    for store in stores:
        store.wait()


def finish_last(base, operator, far, old, scale, field, at):
    rows, width = old.shape
    parts = 4
    anywhere = pl.BlockSpec(memory_space=pl.ANY)
    vmem = pl.BlockSpec(memory_space=pltpu.VMEM)
    return pl.pallas_call(
        functools.partial(finish_kernel, field, at, parts),
        in_specs=[vmem] * 4 + [anywhere],
        out_specs=anywhere,
        out_shape=jax.ShapeDtypeStruct(base.shape, base.dtype),
        scratch_shapes=[pltpu.VMEM((rows, width), jnp.float32), pltpu.SemaphoreType.DMA((parts,))],
        input_output_aliases={4: 0},
        compiler_params=pltpu.CompilerParams(vmem_limit_bytes=16 * MIB),
        cost_estimate=pl.CostEstimate(
            flops=2 * rows * operator.shape[1] * width, bytes_accessed=4 * rows * width, transcendentals=0
        ),
        name="finish_last",
    )(operator, far, old, scale, base)


def per_device(
    elastic,
    acoustic,
    el_media,
    ac_media,
    cont_matrix,
    fringe_cells,
    donor_cells,
    donor_weights,
    donor_counts,
    el_pair,
    ac_pair,
):
    rows, depth = elastic.shape[2], elastic.shape[3]
    slabs = lax.axis_size("line")
    layers = lax.axis_size("layer")
    patches = lax.axis_size("patch")
    slots = fringe_cells.shape[-1]
    groups = slots // LANES
    me = lax.axis_index("line")
    layer = lax.axis_index("layer")
    tile = min(64, rows)

    def other_slabs(value):
        parts = [
            lax.ppermute(value, "line", [(i, (i + distance) % slabs) for i in range(slabs)])
            for distance in range(1, slabs)
        ]
        return parts[0] if slabs == 2 else jnp.concatenate(parts, axis=0)

    half, quarter = depth // 2, depth // 4
    pieces = [
        ("el", 0, 0, depth, "el", 0, 3, 2, (lambda b, l, m: l + 2.0 * m, lambda b, l, m: l)),
        ("ac", 0, 0, depth, "ac", 1, 1, 1, (lambda b: -b,)),
        ("ac", 1, 0, depth, "ac", 0, 1, 0, (lambda k: -k,)),
        ("el", 1, 0, depth, "el", 2, 1, 4, (lambda m: m,)),
        ("el", 2, 0, depth, "el", 0, 1, 0, (lambda b: b,)),
        ("el", 4, 0, half, "el", 0, 1, 1, (lambda b: b,)),
        ("el", 4, half, quarter, "el", 0, 1, 1, (lambda b: b,)),
        ("el", 4, half + quarter, quarter, "el", 0, 1, 1, (lambda b: b,)),
    ]
    travelling = [piece[:4] for piece in pieces]
    first = take_first(elastic, travelling[0][1])
    *others, edges, asked = take_pieces(
        elastic, acoustic, travelling[1:], first, donor_cells, donor_weights, layers
    )
    far = [other_slabs(value) for value in [first, *others]]

    asked = lax.all_to_all(asked, "patch", split_axis=0, concat_axis=0, tiled=True)
    asked_words = asked[:, :4].astype(jnp.int32)

    smem = pl.BlockSpec(memory_space=pltpu.SMEM)
    vmem = pl.BlockSpec(memory_space=pltpu.VMEM)
    local = pl.pallas_call(
        functools.partial(gather_kernel, 8, rows, depth),
        in_specs=[smem, smem, vmem, vmem],
        out_specs=vmem,
        out_shape=jax.ShapeDtypeStruct((patches, groups, 8, LANES), jnp.float32),
        scratch_shapes=[pltpu.VMEM((8 * rows * (depth // LANES), LANES), jnp.float32)],
        compiler_params=pltpu.CompilerParams(vmem_limit_bytes=24 * MIB),
        cost_estimate=pl.CostEstimate(flops=10**9, bytes_accessed=32 * rows * depth, transcendentals=0),
        name="donor_gather",
    )(asked_words, asked, in_hbm(elastic), in_hbm(acoustic))
    interp = lax.all_to_all(local, "patch", split_axis=0, concat_axis=0, tiled=True)
    edges = lax.all_to_all(edges, "layer", split_axis=0, concat_axis=0, tiled=True)

    near, far_operator = near_derivatives(elastic, acoustic, cont_matrix, me, slabs)
    new_el, new_ac, opened = pl.pallas_call(
        functools.partial(section_kernel, layers, rows, depth, tile),
        grid=(rows // tile,),
        in_specs=[
            smem,
            smem,
            smem,
            pl.BlockSpec((6, tile, depth), lambda i: (0, i, 0)),
            pl.BlockSpec((1, 5, tile, depth), lambda i: (0, 0, i, 0)),
            pl.BlockSpec((1, 3, tile, depth), lambda i: (0, 0, i, 0)),
            pl.BlockSpec((1, 3, tile, depth), lambda i: (0, 0, i, 0)),
            pl.BlockSpec((1, 2, tile, depth), lambda i: (0, 0, i, 0)),
            vmem,
            vmem,
            vmem,
        ],
        out_specs=[vmem, vmem, vmem],
        out_shape=[
            jax.ShapeDtypeStruct(elastic.shape, jnp.float32),
            jax.ShapeDtypeStruct(acoustic.shape, jnp.float32),
            pltpu.VMEM((rows, depth), jnp.float32),
        ],
        scratch_shapes=[pltpu.VMEM((rows, LANES), jnp.float32)],
        compiler_params=pltpu.CompilerParams(vmem_limit_bytes=32 * MIB),
        cost_estimate=pl.CostEstimate(
            flops=100 * rows * depth, bytes_accessed=112 * rows * depth, transcendentals=0
        ),
        name="near_section",
    )(
        fringe_cells,
        donor_counts,
        interp,
        near,
        in_hbm(elastic),
        in_hbm(acoustic),
        in_hbm(el_media),
        in_hbm(ac_media),
        edges,
        el_pair,
        ac_pair,
    )

    turn = jnp.zeros((8, LANES), jnp.float32)
    section = {"el": new_el, "ac": new_ac}
    media = {"el": el_media, "ac": ac_media}
    for value, (_, _, at, _, target, first_media, n_media, first_field, coefficients) in zip(far[:-1], pieces):
        turn, section[target] = add_far(
            section[target], far_operator, value, at,
            media[target], first_media, n_media, first_field, coefficients, opened, turn,
        )

    _, _, at, width, target, first_media, _, field, (coefficient,) = pieces[-1]
    base, old, scale = prepare_last(
        section[target], media[target], first_media, field, coefficient, opened, at, width
    )
    section[target] = finish_last(base, far_operator, far[-1], old, scale, field, at)
    return section["el"], section["ac"]


def solution(mesh):
    placed = (
        P("patch", None, "line", "layer"),
        P("patch", None, "line", "layer"),
        P("patch", None, "line", "layer"),
        P("patch", None, "line", "layer"),
        P(),
        P("patch", "line", "layer", None, None),
        P("patch", "line", "layer", None, None, None),
        P("patch", "line", "layer", None, None, None),
        P("patch", "line", "layer", None),
        P("patch", "line"),
        P("patch", "line"),
    )
    return jax.shard_map(
        per_device,
        mesh=mesh,
        in_specs=placed,
        out_specs=(P("patch", None, "line", "layer"), P("patch", None, "line", "layer")),
        check_vma=False,
    )
```

```python
import functools
import math

import jax
import jax.numpy as jnp
import numpy as np
from jax import lax
from jax.experimental import pallas as pl
from jax.experimental.pallas import tpu as pltpu
from jax.sharding import PartitionSpec as P

STEP = 0.25
PENALTY = 2.0
LANES = 128
MIB = 1024 * 1024
HIGHEST = lax.Precision.HIGHEST


def in_hbm(array):
    return pltpu.with_memory_space_constraint(array, pltpu.HBM)


def derivative_row(period):
    n = np.arange(1, period)
    sign = np.where(n % 2 == 0, 1.0, -1.0)
    row = np.zeros(period)
    row[1:] = (math.pi / period) * sign / np.tan(math.pi * n / period)
    return row


def operator_tables(rows, slabs, cont):
    points = rows * slabs
    period = points + cont
    row = derivative_row(period)
    j = np.arange(rows)
    own = row[(j[:, None] - j[None, :]) % period]
    far, tail = [], []
    for me in range(slabs):
        mine = me * rows + j[:, None]
        others = np.concatenate([(me - d) % slabs * rows + j for d in range(1, slabs)])
        far.append(row[(mine - others[None, :]) % period])
        tail.append(row[(mine - points - np.arange(cont)[None, :]) % period])
    return tuple(jnp.asarray(np.asarray(table, np.float32)) for table in (own, far, tail))


def continuation_on(cont_matrix, rows, slabs, sources):
    match = cont_matrix.shape[1] // 2
    on_last = jnp.pad(cont_matrix[:, :match], ((0, 0), (rows - match, 0)))
    on_first = jnp.pad(cont_matrix[:, match:], ((0, 0), (0, rows - match)))
    return jnp.concatenate(
        [
            jnp.where(source == slabs - 1, on_last, 0.0) + jnp.where(source == 0, on_first, 0.0)
            for source in sources
        ],
        axis=1,
    )


def split(value, size):
    if size & (size - 1) == 0:
        return lax.shift_right_logical(value, size.bit_length() - 1), value & (size - 1)
    return lax.div(value, size), lax.rem(value, size)


def take_kernel(pieces, parts, elastic_ref, acoustic_ref, *refs):
    n = len(pieces)
    outs, held, in_semaphores, out_semaphores = refs[:n], refs[n : 2 * n], refs[-2], refs[-1]
    rows = elastic_ref.shape[2]
    loads, stores = [], []
    for i, (name, field, at, width) in enumerate(pieces):
        source = elastic_ref if name == "el" else acoustic_ref
        for part in range(parts):
            here = pl.ds(part * (rows // parts), rows // parts)
            k = i * parts + part
            loads.append(
                pltpu.make_async_copy(source.at[0, field, here, pl.ds(at, width)], held[i].at[here], in_semaphores.at[k])
            )
            stores.append(pltpu.make_async_copy(held[i].at[here], outs[i].at[here], out_semaphores.at[k]))
    for load in loads:
        load.start()
    for load, store in zip(loads, stores):
        load.wait()
        store.start()
    return stores


def take_first_kernel(field, elastic_ref, out_ref, semaphore):
    copy = pltpu.make_async_copy(elastic_ref.at[0, field], out_ref, semaphore)
    copy.start()
    copy.wait()


def take_first(elastic, field):
    rows, depth = elastic.shape[2:]
    return pl.pallas_call(
        functools.partial(take_first_kernel, field),
        in_specs=[pl.BlockSpec(memory_space=pl.ANY)],
        out_specs=pl.BlockSpec(memory_space=pltpu.VMEM),
        out_shape=pltpu.VMEM((rows, depth), jnp.float32),
        scratch_shapes=[pltpu.SemaphoreType.DMA],
        compiler_params=pltpu.CompilerParams(vmem_limit_bytes=16 * MIB),
        cost_estimate=pl.CostEstimate(flops=0, bytes_accessed=8 * rows * depth, transcendentals=0),
        name="take_first",
    )(in_hbm(elastic))


def take_and_edges_kernel(
    pieces, parts, layers, after_ref, elastic_ref, acoustic_ref, cells_ref, weights_ref, *refs
):
    del after_ref
    n = len(pieces)
    edges_ref, asked_ref, tiles, edge_semaphores = refs[n : n + 4]
    n_el, n_ac = elastic_ref.shape[1], acoustic_ref.shape[1]
    rows, depth = elastic_ref.shape[2:]
    loads = []
    for end, at in enumerate((0, depth - LANES)):
        for k, (source, first, count) in enumerate(((elastic_ref, 0, n_el), (acoustic_ref, n_el, n_ac))):
            loads.append(
                pltpu.make_async_copy(
                    source.at[0, :, :, pl.ds(at, LANES)],
                    tiles.at[end, pl.ds(first, count)],
                    edge_semaphores.at[2 * end + k],
                )
            )
    for load in loads:
        load.start()
    stores = take_kernel(pieces, parts, elastic_ref, acoustic_ref, *refs[:n], *refs[n + 4 :])

    x, z = split(cells_ref[0, 0, 0], depth)
    chunk, at_lane = split(z, LANES)
    words = (chunk * ((n_el + n_ac) * rows) + x) * LANES + at_lane
    asked_ref[...] = jnp.concatenate([words.astype(jnp.float32), weights_ref[0, 0, 0]], axis=1)

    for load in loads:
        load.wait()
    lane = lax.broadcasted_iota(jnp.int32, (rows, LANES), 1)
    columns = jnp.zeros((rows, LANES), jnp.float32)
    for f in range(n_el + n_ac):
        columns = jnp.where(lane == f, tiles[0, f, :, 0:1], columns)
        columns = jnp.where(lane == 8 + f, tiles[1, f, :, LANES - 1 : LANES], columns)
    lines = columns.T
    below = lax.rem(lax.axis_index("layer") + 1, layers)
    for to in range(layers):
        edges_ref[to] = jnp.where(to == below, lines[8:16], lines[0:8])
    for store in stores:
        store.wait()


def take_pieces(elastic, acoustic, pieces, after, cells, weights, layers):
    rows = elastic.shape[2]
    anywhere = pl.BlockSpec(memory_space=pl.ANY)
    vmem = pl.BlockSpec(memory_space=pltpu.VMEM)
    out_shape = [jax.ShapeDtypeStruct((rows, width), jnp.float32) for _, _, _, width in pieces]
    parts = 2
    scratch = [pltpu.VMEM((2, 8, rows, LANES), jnp.float32), pltpu.SemaphoreType.DMA((4,))]
    scratch += [pltpu.VMEM((rows, width), jnp.float32) for _, _, _, width in pieces]
    scratch += [pltpu.SemaphoreType.DMA((len(pieces) * parts,))] * 2
    patches, corners, slots = cells.shape[3:]
    out_shape.append(jax.ShapeDtypeStruct((layers, 8, rows), jnp.float32))
    out_shape.append(jax.ShapeDtypeStruct((patches, 2 * corners, slots), jnp.float32))
    cost = sum(width for _, _, _, width in pieces) * rows
    return pl.pallas_call(
        functools.partial(take_and_edges_kernel, pieces, parts, layers),
        in_specs=[anywhere] * 3 + [vmem] * 2,
        out_specs=[anywhere] * len(pieces) + [vmem] * 2,
        out_shape=out_shape,
        scratch_shapes=scratch,
        compiler_params=pltpu.CompilerParams(vmem_limit_bytes=24 * MIB),
        cost_estimate=pl.CostEstimate(flops=0, bytes_accessed=8 * cost, transcendentals=0),
        name="take_pieces",
    )(after, in_hbm(elastic), in_hbm(acoustic), cells, weights)


def gather_kernel(fields, rows, depth, words_ref, weights_ref, elastic_ref, acoustic_ref, out_ref, mixed):
    n_el = elastic_ref.shape[1]
    chunks = depth // LANES
    for f in range(fields):
        source = elastic_ref.at[0, f] if f < n_el else acoustic_ref.at[0, f - n_el]
        for c in range(chunks):
            mixed[pl.ds((c * fields + f) * rows, rows), :] = source[:, c * LANES : (c + 1) * LANES]
    lane = lax.broadcasted_iota(jnp.int32, (fields, LANES), 1)
    groups = out_ref.shape[1]

    def one_group(step, carry):
        patch, group = split(step, groups)

        def one_slot(r, values):
            slot = group * LANES + r
            total = None
            for s in range(4):
                start, at = split(words_ref[patch, s, slot], LANES)
                picked = mixed[pl.ds(start, fields, stride=rows), :]
                term = jnp.where(lane == at, picked * weights_ref[patch, 4 + s, slot], 0.0)
                total = term if total is None else total + term
            column = jnp.sum(total, axis=1, keepdims=True)
            return jnp.where(lane == r, column, values)

        values = lax.fori_loop(0, LANES, one_slot, jnp.zeros((fields, LANES), jnp.float32), unroll=16)
        out_ref[patch, group] = values
        return carry

    lax.fori_loop(0, out_ref.shape[0] * groups, one_group, 0)


def bf16_pair(value):
    high = value.astype(jnp.bfloat16)
    return high, (value - high.astype(jnp.float32)).astype(jnp.bfloat16)


def three_left(value):
    high, low = bf16_pair(value)
    return jnp.concatenate([high, high, low], axis=1)


def three_right(value):
    high, low = bf16_pair(value)
    return jnp.concatenate([high, low, high], axis=0)


def near_kernel(
    n_el, me_ref, own_ref, far_ref, tail_ref, own_cont_ref, far_cont_ref, elastic_ref, acoustic_ref,
    out_ref, far_operator_ref, operator,
):
    del me_ref

    @pl.when(pl.program_id(0) == 0)
    def _():
        def folded(table, cont):
            return table + jnp.dot(tail_ref[0], cont, precision=HIGHEST, preferred_element_type=jnp.float32)

        operator[...] = three_left(folded(own_ref[...], own_cont_ref[...]))
        far_operator_ref[...] = three_left(folded(far_ref[0], far_cont_ref[...]))

    value = jnp.where(pl.program_id(0) < n_el, elastic_ref[0, 0], acoustic_ref[0, 0])
    out_ref[0] = jnp.dot(operator[...], three_right(value), preferred_element_type=jnp.float32)


def near_derivatives(elastic, acoustic, cont_matrix, me, slabs):
    rows, depth = elastic.shape[2:]
    cont = cont_matrix.shape[0]
    reach = (slabs - 1) * rows
    own, far, tail = operator_tables(rows, slabs, cont)
    own_cont = continuation_on(cont_matrix, rows, slabs, [me])
    far_cont = continuation_on(cont_matrix, rows, slabs, [(me - d) % slabs for d in range(1, slabs)])
    return pl.pallas_call(
        functools.partial(near_kernel, 4),
        grid_spec=pltpu.PrefetchScalarGridSpec(
            num_scalar_prefetch=1,
            grid=(6,),
            in_specs=[
                pl.BlockSpec((rows, rows), lambda f, me: (0, 0)),
                pl.BlockSpec((1, rows, reach), lambda f, me: (me[0], 0, 0)),
                pl.BlockSpec((1, rows, cont), lambda f, me: (me[0], 0, 0)),
                pl.BlockSpec((cont, rows), lambda f, me: (0, 0)),
                pl.BlockSpec((cont, reach), lambda f, me: (0, 0)),
                pl.BlockSpec((1, 1, rows, depth), lambda f, me: (0, jnp.where(f < 3, f, 4), 0, 0)),
                pl.BlockSpec((1, 1, rows, depth), lambda f, me: (0, jnp.maximum(f - 4, 0), 0, 0)),
            ],
            out_specs=[
                pl.BlockSpec((1, rows, depth), lambda f, me: (f, 0, 0)),
                pl.BlockSpec((rows, 3 * reach), lambda f, me: (0, 0)),
            ],
            scratch_shapes=[pltpu.VMEM((rows, 3 * rows), jnp.bfloat16)],
        ),
        out_shape=[
            pltpu.HBM((6, rows, depth), jnp.float32),
            pltpu.VMEM((rows, 3 * reach), jnp.bfloat16),
        ],
        compiler_params=pltpu.CompilerParams(vmem_limit_bytes=24 * MIB),
        cost_estimate=pl.CostEstimate(
            flops=36 * rows * rows * depth, bytes_accessed=60 * rows * depth, transcendentals=0
        ),
        name="near_dx",
    )(
        me.reshape(1), in_hbm(own), in_hbm(far), in_hbm(tail), own_cont, far_cont, in_hbm(elastic), in_hbm(acoustic)
    )


def section_kernel(
    layers, rows, depth, tile,
    cells_ref, counts_ref, interp_ref,
    dx_ref, elastic_ref, acoustic_ref, el_media_ref, ac_media_ref, edges_ref, el_pair_ref, ac_pair_ref,
    new_el_ref, new_ac_ref, open_ref,
    columns,
):
    step = pl.program_id(0)
    here = pl.ds(pl.multiple_of(step * tile, tile), tile)
    lane = lax.broadcasted_iota(jnp.int32, (tile, depth), 1)
    layer = lax.axis_index("layer")
    at_top, at_bottom = layer == 0, layer == layers - 1
    from_above = edges_ref[lax.rem(layer + layers - 1, layers)]
    from_below = edges_ref[lax.rem(layer + 1, layers)]
    ocean_row = from_above[5:6]
    basin_row = from_below[1:2]

    @pl.when(step == 0)
    def _():
        pairs = jnp.concatenate([el_pair_ref[...], ac_pair_ref[...]]).astype(jnp.float32)
        lines = [
            jnp.where(at_top, 0.0, from_above),
            jnp.where(at_bottom, 0.0, from_below),
            pairs,
            jnp.zeros((LANES - 18, rows), jnp.float32),
        ]
        columns[...] = jnp.concatenate(lines).T

    halo = columns[here, :]

    def dz(value, slot):
        above = halo[:, slot : slot + 1]
        below = halo[:, 8 + slot : 9 + slot]
        following = jnp.where(lane == depth - 1, below, pltpu.roll(value, depth - 1, 1))
        previous = jnp.where(lane == 0, above, pltpu.roll(value, 1, 1))
        return (following - previous) * 0.5

    vx, vz, sxx, szz, sxz = [elastic_ref[0, f] for f in range(5)]
    p, ovx, ovz = [acoustic_ref[0, f] for f in range(3)]
    buoyancy = el_media_ref[0, 0]
    lame = el_media_ref[0, 1]
    shear = el_media_ref[0, 2]
    stiffness = lame + 2.0 * shear
    bulk = ac_media_ref[0, 0]
    ocean_buoyancy = ac_media_ref[0, 1]

    dx_vx = dx_ref[0]
    dz_vz = dz(vz, 1)
    new_el_ref[0, 0, here, :] = vx + STEP * (buoyancy * (dx_ref[2] + dz(sxz, 4)))
    new_el_ref[0, 1, here, :] = vz + STEP * (buoyancy * (dx_ref[3] + dz(szz, 3)))
    new_el_ref[0, 2, here, :] = sxx + STEP * (stiffness * dx_vx + lame * dz_vz)
    choose = lax.broadcasted_iota(jnp.int32, (tile, rows), 1).astype(jnp.float32)
    pressure = jnp.sum(jnp.where(halo[:, 16:17] == choose, ocean_row, 0.0), axis=1, keepdims=True)
    velocity = jnp.sum(jnp.where(halo[:, 17:18] == choose, basin_row, 0.0), axis=1, keepdims=True)
    rate_szz = lame * dx_vx + stiffness * dz_vz
    rate_szz = rate_szz + jnp.where((lane == 0) & at_top, PENALTY * (-pressure - szz), 0.0)
    new_el_ref[0, 3, here, :] = szz + STEP * rate_szz
    new_el_ref[0, 4, here, :] = sxz + STEP * (shear * (dz(vx, 0) + dx_ref[1]))
    new_ac_ref[0, 0, here, :] = p - STEP * (bulk * (dx_ref[5] + dz(ovz, 7)))
    new_ac_ref[0, 1, here, :] = ovx - STEP * (ocean_buoyancy * dx_ref[4])
    rate_ovz = -ocean_buoyancy * dz(p, 5)
    rate_ovz = rate_ovz + jnp.where((lane == depth - 1) & at_bottom, PENALTY * (velocity - ovz), 0.0)
    new_ac_ref[0, 2, here, :] = ovz + STEP * rate_ovz
    open_ref[here, :] = jnp.ones((tile, depth), jnp.float32)

    @pl.when(step == pl.num_programs(0) - 1)
    def _():
        place = lax.broadcasted_iota(jnp.int32, (8, LANES), 0) * LANES
        place = place + lax.broadcasted_iota(jnp.int32, (8, LANES), 1)
        n_el = new_el_ref.shape[1]

        def one_patch(q, carry):
            def one_slot(r, inner):
                x, z = split(cells_ref[0, 0, 0, q, r], depth)
                (high, row), (low, at) = split(x, 8), split(z, LANES)
                at_row = pl.ds(pl.multiple_of(high * 8, 8), 8)
                at_lane = pl.ds(pl.multiple_of(low * LANES, LANES), LANES)
                hit = place == row * LANES + at
                group, within = split(r, LANES)
                for f in range(8):
                    target = new_el_ref.at[0, f] if f < n_el else new_ac_ref.at[0, f - n_el]
                    target[at_row, at_lane] = jnp.where(hit, interp_ref[q, group, f, within], target[at_row, at_lane])
                open_ref[at_row, at_lane] = jnp.where(hit, 0.0, open_ref[at_row, at_lane])
                return inner

            return lax.fori_loop(0, counts_ref[0, 0, 0, q], one_slot, carry)

        lax.fori_loop(0, counts_ref.shape[3], one_patch, 0)


def far_kernel(coefficients, turn_ref, d_ref, far_ref, media_ref, open_ref, base_ref, next_ref, out_ref):
    del turn_ref, next_ref
    far = jnp.dot(d_ref[...], three_right(far_ref[...]), preferred_element_type=jnp.float32)
    media = [media_ref[0, i] for i in range(media_ref.shape[1])]
    is_open = open_ref[...] > 0.5
    for i, coefficient in enumerate(coefficients):
        old = base_ref[0, i]
        out_ref[0, i] = jnp.where(is_open, old + (STEP * coefficient(*media)) * far, old)


def add_far(base, operator, far, at, media, first_media, n_media, first_field, coefficients, opened, turn):
    rows, reach = operator.shape[0], far.shape[0]
    width = far.shape[1]
    tile = math.gcd(math.gcd(width, at), 2 * LANES)
    n_out = len(coefficients)
    shift = at // tile
    return pl.pallas_call(
        functools.partial(far_kernel, coefficients),
        grid=(width // tile,),
        in_specs=[
            pl.BlockSpec(memory_space=pl.ANY),
            pl.BlockSpec((rows, 3 * reach), lambda i: (0, 0)),
            pl.BlockSpec((reach, tile), lambda i: (0, i)),
            pl.BlockSpec((1, n_media, rows, tile), lambda i: (0, first_media // n_media, 0, i + shift)),
            pl.BlockSpec((rows, tile), lambda i: (0, i + shift)),
            pl.BlockSpec((1, n_out, rows, tile), lambda i: (0, first_field // n_out, 0, i + shift)),
        ],
        out_specs=[
            pl.BlockSpec(memory_space=pl.ANY),
            pl.BlockSpec((1, n_out, rows, tile), lambda i: (0, first_field // n_out, 0, i + shift)),
        ],
        out_shape=[
            jax.ShapeDtypeStruct(turn.shape, turn.dtype),
            jax.ShapeDtypeStruct(base.shape, base.dtype),
        ],
        input_output_aliases={0: 0, 5: 1},
        compiler_params=pltpu.CompilerParams(vmem_limit_bytes=16 * MIB),
        cost_estimate=pl.CostEstimate(
            flops=6 * rows * reach * width,
            bytes_accessed=4 * rows * width * (3 + n_media + n_out),
            transcendentals=0,
        ),
        name="add_far",
    )(turn, operator, far, in_hbm(media), opened, base)


def prepare_kernel(coefficient, field, at, base_ref, media_ref, open_ref, same_ref, old_ref, scale_ref, semaphore):
    del same_ref
    load = pltpu.make_async_copy(base_ref.at[0, field, :, pl.ds(at, old_ref.shape[1])], old_ref, semaphore)
    load.start()
    scale_ref[...] = jnp.where(open_ref[...] > 0.5, STEP * coefficient(media_ref[0, 0]), 0.0)
    load.wait()


def prepare_last(base, media, first_media, field, coefficient, opened, at, width):
    rows = opened.shape[0]
    anywhere = pl.BlockSpec(memory_space=pl.ANY)
    vmem = pl.BlockSpec(memory_space=pltpu.VMEM)
    return pl.pallas_call(
        functools.partial(prepare_kernel, coefficient, field, at),
        grid=(1,),
        in_specs=[
            anywhere,
            pl.BlockSpec((1, 1, rows, width), lambda i: (0, first_media, 0, at // width)),
            pl.BlockSpec((rows, width), lambda i: (0, at // width)),
        ],
        out_specs=[anywhere, vmem, vmem],
        out_shape=[
            jax.ShapeDtypeStruct(base.shape, base.dtype),
            pltpu.VMEM((rows, width), jnp.float32),
            pltpu.VMEM((rows, width), jnp.float32),
        ],
        scratch_shapes=[pltpu.SemaphoreType.DMA],
        input_output_aliases={0: 0},
        compiler_params=pltpu.CompilerParams(vmem_limit_bytes=16 * MIB),
        cost_estimate=pl.CostEstimate(flops=rows * width, bytes_accessed=20 * rows * width, transcendentals=0),
        name="prepare_last",
    )(base, in_hbm(media), opened)


def finish_kernel(field, at, parts, d_ref, far_ref, old_ref, scale_ref, base_ref, out_ref, held, semaphores):
    del base_ref
    rows, width = old_ref.shape[0] // parts, old_ref.shape[1]
    far_field = three_right(far_ref[...])
    stores = []
    for part in range(parts):
        here = pl.ds(part * rows, rows)
        far = jnp.dot(d_ref[here, :], far_field, preferred_element_type=jnp.float32)
        held[here, :] = old_ref[here, :] + scale_ref[here, :] * far
        stores.append(
            pltpu.make_async_copy(
                held.at[here], out_ref.at[0, field, here, pl.ds(at, width)], semaphores.at[part]
            )
        )
        stores[-1].start()
    for store in stores:
        store.wait()


def finish_last(base, operator, far, old, scale, field, at):
    rows, width = old.shape
    parts = 4
    anywhere = pl.BlockSpec(memory_space=pl.ANY)
    vmem = pl.BlockSpec(memory_space=pltpu.VMEM)
    return pl.pallas_call(
        functools.partial(finish_kernel, field, at, parts),
        in_specs=[vmem] * 4 + [anywhere],
        out_specs=anywhere,
        out_shape=jax.ShapeDtypeStruct(base.shape, base.dtype),
        scratch_shapes=[pltpu.VMEM((rows, width), jnp.float32), pltpu.SemaphoreType.DMA((parts,))],
        input_output_aliases={4: 0},
        compiler_params=pltpu.CompilerParams(vmem_limit_bytes=16 * MIB),
        cost_estimate=pl.CostEstimate(
            flops=2 * rows * operator.shape[1] * width, bytes_accessed=4 * rows * width, transcendentals=0
        ),
        name="finish_last",
    )(operator, far, old, scale, base)


def per_device(
    elastic,
    acoustic,
    el_media,
    ac_media,
    cont_matrix,
    fringe_cells,
    donor_cells,
    donor_weights,
    donor_counts,
    el_pair,
    ac_pair,
):
    rows, depth = elastic.shape[2], elastic.shape[3]
    slabs = lax.axis_size("line")
    layers = lax.axis_size("layer")
    patches = lax.axis_size("patch")
    slots = fringe_cells.shape[-1]
    groups = slots // LANES
    me = lax.axis_index("line")
    layer = lax.axis_index("layer")
    tile = min(64, rows)

    def other_slabs(value):
        parts = [
            lax.ppermute(value, "line", [(i, (i + distance) % slabs) for i in range(slabs)])
            for distance in range(1, slabs)
        ]
        return parts[0] if slabs == 2 else jnp.concatenate(parts, axis=0)

    half, quarter = depth // 2, depth // 4
    pieces = [
        ("el", 0, 0, depth, "el", 0, 3, 2, (lambda b, l, m: l + 2.0 * m, lambda b, l, m: l)),
        ("ac", 0, 0, depth, "ac", 1, 1, 1, (lambda b: -b,)),
        ("ac", 1, 0, depth, "ac", 0, 1, 0, (lambda k: -k,)),
        ("el", 1, 0, depth, "el", 2, 1, 4, (lambda m: m,)),
        ("el", 2, 0, depth, "el", 0, 1, 0, (lambda b: b,)),
        ("el", 4, 0, half, "el", 0, 1, 1, (lambda b: b,)),
        ("el", 4, half, quarter, "el", 0, 1, 1, (lambda b: b,)),
        ("el", 4, half + quarter, quarter, "el", 0, 1, 1, (lambda b: b,)),
    ]
    travelling = [piece[:4] for piece in pieces]
    first = take_first(elastic, travelling[0][1])
    *others, edges, asked = take_pieces(
        elastic, acoustic, travelling[1:], first, donor_cells, donor_weights, layers
    )
    far = [other_slabs(value) for value in [first, *others]]

    asked = lax.all_to_all(asked, "patch", split_axis=0, concat_axis=0, tiled=True)
    asked_words = asked[:, :4].astype(jnp.int32)

    smem = pl.BlockSpec(memory_space=pltpu.SMEM)
    vmem = pl.BlockSpec(memory_space=pltpu.VMEM)
    local = pl.pallas_call(
        functools.partial(gather_kernel, 8, rows, depth),
        in_specs=[smem, smem, vmem, vmem],
        out_specs=vmem,
        out_shape=jax.ShapeDtypeStruct((patches, groups, 8, LANES), jnp.float32),
        scratch_shapes=[pltpu.VMEM((8 * rows * (depth // LANES) + rows, LANES), jnp.float32)],
        compiler_params=pltpu.CompilerParams(vmem_limit_bytes=24 * MIB),
        cost_estimate=pl.CostEstimate(flops=10**9, bytes_accessed=32 * rows * depth, transcendentals=0),
        name="donor_gather",
    )(asked_words, asked, in_hbm(elastic), in_hbm(acoustic))
    interp = lax.all_to_all(local, "patch", split_axis=0, concat_axis=0, tiled=True)
    edges = lax.all_to_all(edges, "layer", split_axis=0, concat_axis=0, tiled=True)

    near, far_operator = near_derivatives(elastic, acoustic, cont_matrix, me, slabs)
    new_el, new_ac, opened = pl.pallas_call(
        functools.partial(section_kernel, layers, rows, depth, tile),
        grid=(rows // tile,),
        in_specs=[
            smem,
            smem,
            smem,
            pl.BlockSpec((6, tile, depth), lambda i: (0, i, 0)),
            pl.BlockSpec((1, 5, tile, depth), lambda i: (0, 0, i, 0)),
            pl.BlockSpec((1, 3, tile, depth), lambda i: (0, 0, i, 0)),
            pl.BlockSpec((1, 3, tile, depth), lambda i: (0, 0, i, 0)),
            pl.BlockSpec((1, 2, tile, depth), lambda i: (0, 0, i, 0)),
            vmem,
            vmem,
            vmem,
        ],
        out_specs=[vmem, vmem, vmem],
        out_shape=[
            jax.ShapeDtypeStruct(elastic.shape, jnp.float32),
            jax.ShapeDtypeStruct(acoustic.shape, jnp.float32),
            pltpu.VMEM((rows, depth), jnp.float32),
        ],
        scratch_shapes=[pltpu.VMEM((rows, LANES), jnp.float32)],
        compiler_params=pltpu.CompilerParams(vmem_limit_bytes=32 * MIB),
        cost_estimate=pl.CostEstimate(
            flops=100 * rows * depth, bytes_accessed=112 * rows * depth, transcendentals=0
        ),
        name="near_section",
    )(
        fringe_cells,
        donor_counts,
        interp,
        near,
        in_hbm(elastic),
        in_hbm(acoustic),
        in_hbm(el_media),
        in_hbm(ac_media),
        edges,
        el_pair,
        ac_pair,
    )

    turn = jnp.zeros((8, LANES), jnp.float32)
    section = {"el": new_el, "ac": new_ac}
    media = {"el": el_media, "ac": ac_media}
    *middle, closing = pieces
    _, _, last_at, last_width, last_target, last_media, _, last_field, (last_coefficient,) = closing
    for i, (_, _, at, _, target, first_media, n_media, first_field, coefficients) in enumerate(middle):
        if i == len(middle) - 1:
            section[last_target], old, scale = prepare_last(
                section[last_target], media[last_target], last_media, last_field, last_coefficient,
                opened, last_at, last_width,
            )
        turn, section[target] = add_far(
            section[target], far_operator, far[i], at,
            media[target], first_media, n_media, first_field, coefficients, opened, turn,
        )
    section[last_target] = finish_last(
        section[last_target], far_operator, far[-1], old, scale, last_field, last_at
    )
    return section["el"], section["ac"]


def solution(mesh):
    placed = (
        P("patch", None, "line", "layer"),
        P("patch", None, "line", "layer"),
        P("patch", None, "line", "layer"),
        P("patch", None, "line", "layer"),
        P(),
        P("patch", "line", "layer", None, None),
        P("patch", "line", "layer", None, None, None),
        P("patch", "line", "layer", None, None, None),
        P("patch", "line", "layer", None),
        P("patch", "line"),
        P("patch", "line"),
    )
    return jax.shard_map(
        per_device,
        mesh=mesh,
        in_specs=placed,
        out_specs=(P("patch", None, "line", "layer"), P("patch", None, "line", "layer")),
        check_vma=False,
    )
```

```python
import functools
import math

import jax
import jax.numpy as jnp
import numpy as np
from jax import lax
from jax.experimental import pallas as pl
from jax.experimental.pallas import tpu as pltpu
from jax.sharding import PartitionSpec as P

STEP = 0.25
PENALTY = 2.0
LANES = 128
MIB = 1024 * 1024
HIGHEST = lax.Precision.HIGHEST


def in_hbm(array):
    return pltpu.with_memory_space_constraint(array, pltpu.HBM)


def derivative_row(period):
    n = np.arange(1, period)
    sign = np.where(n % 2 == 0, 1.0, -1.0)
    row = np.zeros(period)
    row[1:] = (math.pi / period) * sign / np.tan(math.pi * n / period)
    return row


def operator_tables(rows, slabs, cont):
    points = rows * slabs
    period = points + cont
    row = derivative_row(period)
    j = np.arange(rows)
    own = row[(j[:, None] - j[None, :]) % period]
    far, tail = [], []
    for me in range(slabs):
        mine = me * rows + j[:, None]
        others = np.concatenate([(me - d) % slabs * rows + j for d in range(1, slabs)])
        far.append(row[(mine - others[None, :]) % period])
        tail.append(row[(mine - points - np.arange(cont)[None, :]) % period])
    return tuple(jnp.asarray(np.asarray(table, np.float32)) for table in (own, far, tail))


def continuation_on(cont_matrix, rows, slabs, sources):
    match = cont_matrix.shape[1] // 2
    on_last = jnp.pad(cont_matrix[:, :match], ((0, 0), (rows - match, 0)))
    on_first = jnp.pad(cont_matrix[:, match:], ((0, 0), (0, rows - match)))
    return jnp.concatenate(
        [
            jnp.where(source == slabs - 1, on_last, 0.0) + jnp.where(source == 0, on_first, 0.0)
            for source in sources
        ],
        axis=1,
    )


def split(value, size):
    if size & (size - 1) == 0:
        return lax.shift_right_logical(value, size.bit_length() - 1), value & (size - 1)
    return lax.div(value, size), lax.rem(value, size)


def take_kernel(pieces, parts, elastic_ref, acoustic_ref, *refs):
    n = len(pieces)
    outs, held, in_semaphores, out_semaphores = refs[:n], refs[n : 2 * n], refs[-2], refs[-1]
    rows = elastic_ref.shape[2]
    loads, stores = [], []
    for i, (name, field, at, width) in enumerate(pieces):
        source = elastic_ref if name == "el" else acoustic_ref
        for part in range(parts):
            here = pl.ds(part * (rows // parts), rows // parts)
            k = i * parts + part
            loads.append(
                pltpu.make_async_copy(source.at[0, field, here, pl.ds(at, width)], held[i].at[here], in_semaphores.at[k])
            )
            stores.append(pltpu.make_async_copy(held[i].at[here], outs[i].at[here], out_semaphores.at[k]))
    for load in loads:
        load.start()
    for load, store in zip(loads, stores):
        load.wait()
        store.start()
    return stores


def take_first_kernel(field, elastic_ref, out_ref, semaphore):
    copy = pltpu.make_async_copy(elastic_ref.at[0, field], out_ref, semaphore)
    copy.start()
    copy.wait()


def take_first(elastic, field):
    rows, depth = elastic.shape[2:]
    return pl.pallas_call(
        functools.partial(take_first_kernel, field),
        in_specs=[pl.BlockSpec(memory_space=pl.ANY)],
        out_specs=pl.BlockSpec(memory_space=pltpu.VMEM),
        out_shape=pltpu.VMEM((rows, depth), jnp.float32),
        scratch_shapes=[pltpu.SemaphoreType.DMA],
        compiler_params=pltpu.CompilerParams(vmem_limit_bytes=16 * MIB),
        cost_estimate=pl.CostEstimate(flops=0, bytes_accessed=8 * rows * depth, transcendentals=0),
        name="take_first",
    )(in_hbm(elastic))


def take_and_edges_kernel(
    pieces, parts, layers, after_ref, elastic_ref, acoustic_ref, cells_ref, weights_ref, *refs
):
    del after_ref
    n = len(pieces)
    edges_ref, asked_ref, tiles, edge_semaphores = refs[n : n + 4]
    n_el, n_ac = elastic_ref.shape[1], acoustic_ref.shape[1]
    rows, depth = elastic_ref.shape[2:]
    loads = []
    for end, at in enumerate((0, depth - LANES)):
        for k, (source, first, count) in enumerate(((elastic_ref, 0, n_el), (acoustic_ref, n_el, n_ac))):
            loads.append(
                pltpu.make_async_copy(
                    source.at[0, :, :, pl.ds(at, LANES)],
                    tiles.at[end, pl.ds(first, count)],
                    edge_semaphores.at[2 * end + k],
                )
            )
    for load in loads:
        load.start()
    stores = take_kernel(pieces, parts, elastic_ref, acoustic_ref, *refs[:n], *refs[n + 4 :])

    x, z = split(cells_ref[0, 0, 0], depth)
    chunk, at_lane = split(z, LANES)
    words = (chunk * ((n_el + n_ac) * rows) + x) * LANES + at_lane
    asked_ref[...] = jnp.concatenate([words.astype(jnp.float32), weights_ref[0, 0, 0]], axis=1)

    for load in loads:
        load.wait()
    lane = lax.broadcasted_iota(jnp.int32, (rows, LANES), 1)
    columns = jnp.zeros((rows, LANES), jnp.float32)
    for f in range(n_el + n_ac):
        columns = jnp.where(lane == f, tiles[0, f, :, 0:1], columns)
        columns = jnp.where(lane == 8 + f, tiles[1, f, :, LANES - 1 : LANES], columns)
    lines = columns.T
    below = lax.rem(lax.axis_index("layer") + 1, layers)
    for to in range(layers):
        edges_ref[to] = jnp.where(to == below, lines[8:16], lines[0:8])
    for store in stores:
        store.wait()


def take_pieces(elastic, acoustic, pieces, after, cells, weights, layers):
    rows = elastic.shape[2]
    anywhere = pl.BlockSpec(memory_space=pl.ANY)
    vmem = pl.BlockSpec(memory_space=pltpu.VMEM)
    out_shape = [jax.ShapeDtypeStruct((rows, width), jnp.float32) for _, _, _, width in pieces]
    parts = 2
    scratch = [pltpu.VMEM((2, 8, rows, LANES), jnp.float32), pltpu.SemaphoreType.DMA((4,))]
    scratch += [pltpu.VMEM((rows, width), jnp.float32) for _, _, _, width in pieces]
    scratch += [pltpu.SemaphoreType.DMA((len(pieces) * parts,))] * 2
    patches, corners, slots = cells.shape[3:]
    out_shape.append(jax.ShapeDtypeStruct((layers, 8, rows), jnp.float32))
    out_shape.append(jax.ShapeDtypeStruct((patches, 2 * corners, slots), jnp.float32))
    cost = sum(width for _, _, _, width in pieces) * rows
    return pl.pallas_call(
        functools.partial(take_and_edges_kernel, pieces, parts, layers),
        in_specs=[anywhere] * 3 + [vmem] * 2,
        out_specs=[anywhere] * len(pieces) + [vmem] * 2,
        out_shape=out_shape,
        scratch_shapes=scratch,
        compiler_params=pltpu.CompilerParams(vmem_limit_bytes=24 * MIB),
        cost_estimate=pl.CostEstimate(flops=0, bytes_accessed=8 * cost, transcendentals=0),
        name="take_pieces",
    )(after, in_hbm(elastic), in_hbm(acoustic), cells, weights)


def gather_kernel(fields, rows, depth, words_ref, weights_ref, elastic_ref, acoustic_ref, out_ref, mixed):
    n_el = elastic_ref.shape[1]
    chunks = depth // LANES
    for f in range(fields):
        source = elastic_ref.at[0, f] if f < n_el else acoustic_ref.at[0, f - n_el]
        for c in range(chunks):
            mixed[pl.ds((c * fields + f) * rows, rows), :] = source[:, c * LANES : (c + 1) * LANES]
    lane = lax.broadcasted_iota(jnp.int32, (fields, LANES), 1)
    groups = out_ref.shape[1]

    def one_group(step, carry):
        patch, group = split(step, groups)

        def one_slot(r, values):
            slot = group * LANES + r
            total = None
            for s in range(4):
                start, at = split(words_ref[patch, s, slot], LANES)
                picked = mixed[pl.ds(start, fields, stride=rows), :]
                term = jnp.where(lane == at, picked * weights_ref[patch, 4 + s, slot], 0.0)
                total = term if total is None else total + term
            column = jnp.sum(total, axis=1, keepdims=True)
            return jnp.where(lane == r, column, values)

        values = lax.fori_loop(0, LANES, one_slot, jnp.zeros((fields, LANES), jnp.float32), unroll=16)
        out_ref[patch, group] = values
        return carry

    lax.fori_loop(0, out_ref.shape[0] * groups, one_group, 0)


def bf16_pair(value):
    high = value.astype(jnp.bfloat16)
    return high, (value - high.astype(jnp.float32)).astype(jnp.bfloat16)


def three_left(value):
    high, low = bf16_pair(value)
    return jnp.concatenate([high, high, low], axis=1)


def three_right(value):
    high, low = bf16_pair(value)
    return jnp.concatenate([high, low, high], axis=0)


def near_kernel(
    n_el, me_ref, own_ref, far_ref, tail_ref, own_cont_ref, far_cont_ref, elastic_ref, acoustic_ref,
    out_ref, far_operator_ref, operator,
):
    del me_ref

    @pl.when(pl.program_id(0) == 0)
    def _():
        def folded(table, cont):
            return table + jnp.dot(tail_ref[0], cont, precision=HIGHEST, preferred_element_type=jnp.float32)

        operator[...] = three_left(folded(own_ref[...], own_cont_ref[...]))
        far_operator_ref[...] = three_left(folded(far_ref[0], far_cont_ref[...]))

    value = jnp.where(pl.program_id(0) < n_el, elastic_ref[0, 0], acoustic_ref[0, 0])
    out_ref[0] = jnp.dot(operator[...], three_right(value), preferred_element_type=jnp.float32)


def near_derivatives(elastic, acoustic, cont_matrix, me, slabs):
    rows, depth = elastic.shape[2:]
    cont = cont_matrix.shape[0]
    reach = (slabs - 1) * rows
    own, far, tail = operator_tables(rows, slabs, cont)
    own_cont = continuation_on(cont_matrix, rows, slabs, [me])
    far_cont = continuation_on(cont_matrix, rows, slabs, [(me - d) % slabs for d in range(1, slabs)])
    return pl.pallas_call(
        functools.partial(near_kernel, 4),
        grid_spec=pltpu.PrefetchScalarGridSpec(
            num_scalar_prefetch=1,
            grid=(6,),
            in_specs=[
                pl.BlockSpec((rows, rows), lambda f, me: (0, 0)),
                pl.BlockSpec((1, rows, reach), lambda f, me: (me[0], 0, 0)),
                pl.BlockSpec((1, rows, cont), lambda f, me: (me[0], 0, 0)),
                pl.BlockSpec((cont, rows), lambda f, me: (0, 0)),
                pl.BlockSpec((cont, reach), lambda f, me: (0, 0)),
                pl.BlockSpec((1, 1, rows, depth), lambda f, me: (0, jnp.where(f < 3, f, 4), 0, 0)),
                pl.BlockSpec((1, 1, rows, depth), lambda f, me: (0, jnp.maximum(f - 4, 0), 0, 0)),
            ],
            out_specs=[
                pl.BlockSpec((1, rows, depth), lambda f, me: (f, 0, 0)),
                pl.BlockSpec((rows, 3 * reach), lambda f, me: (0, 0)),
            ],
            scratch_shapes=[pltpu.VMEM((rows, 3 * rows), jnp.bfloat16)],
        ),
        out_shape=[
            pltpu.HBM((6, rows, depth), jnp.float32),
            pltpu.VMEM((rows, 3 * reach), jnp.bfloat16),
        ],
        compiler_params=pltpu.CompilerParams(vmem_limit_bytes=24 * MIB),
        cost_estimate=pl.CostEstimate(
            flops=36 * rows * rows * depth, bytes_accessed=60 * rows * depth, transcendentals=0
        ),
        name="near_dx",
    )(
        me.reshape(1), in_hbm(own), in_hbm(far), in_hbm(tail), own_cont, far_cont, in_hbm(elastic), in_hbm(acoustic)
    )


def section_kernel(
    layers, rows, depth, tile,
    cells_ref, counts_ref, interp_ref,
    dx_ref, elastic_ref, acoustic_ref, el_media_ref, ac_media_ref, edges_ref, el_pair_ref, ac_pair_ref,
    new_el_ref, new_ac_ref, open_ref,
    columns,
):
    step = pl.program_id(0)
    here = pl.ds(pl.multiple_of(step * tile, tile), tile)
    lane = lax.broadcasted_iota(jnp.int32, (tile, depth), 1)
    layer = lax.axis_index("layer")
    at_top, at_bottom = layer == 0, layer == layers - 1
    from_above = edges_ref[lax.rem(layer + layers - 1, layers)]
    from_below = edges_ref[lax.rem(layer + 1, layers)]
    ocean_row = from_above[5:6]
    basin_row = from_below[1:2]

    @pl.when(step == 0)
    def _():
        pairs = jnp.concatenate([el_pair_ref[...], ac_pair_ref[...]]).astype(jnp.float32)
        lines = [
            jnp.where(at_top, 0.0, from_above),
            jnp.where(at_bottom, 0.0, from_below),
            pairs,
            jnp.zeros((LANES - 18, rows), jnp.float32),
        ]
        columns[...] = jnp.concatenate(lines).T

    halo = columns[here, :]

    def dz(value, slot):
        above = halo[:, slot : slot + 1]
        below = halo[:, 8 + slot : 9 + slot]
        following = jnp.where(lane == depth - 1, below, pltpu.roll(value, depth - 1, 1))
        previous = jnp.where(lane == 0, above, pltpu.roll(value, 1, 1))
        return (following - previous) * 0.5

    vx, vz, sxx, szz, sxz = [elastic_ref[0, f] for f in range(5)]
    p, ovx, ovz = [acoustic_ref[0, f] for f in range(3)]
    buoyancy = el_media_ref[0, 0]
    lame = el_media_ref[0, 1]
    shear = el_media_ref[0, 2]
    stiffness = lame + 2.0 * shear
    bulk = ac_media_ref[0, 0]
    ocean_buoyancy = ac_media_ref[0, 1]

    dx_vx = dx_ref[0]
    dz_vz = dz(vz, 1)
    new_el_ref[0, 0, here, :] = vx + STEP * (buoyancy * (dx_ref[2] + dz(sxz, 4)))
    new_el_ref[0, 1, here, :] = vz + STEP * (buoyancy * (dx_ref[3] + dz(szz, 3)))
    new_el_ref[0, 2, here, :] = sxx + STEP * (stiffness * dx_vx + lame * dz_vz)
    choose = lax.broadcasted_iota(jnp.int32, (tile, rows), 1).astype(jnp.float32)
    pressure = jnp.sum(jnp.where(halo[:, 16:17] == choose, ocean_row, 0.0), axis=1, keepdims=True)
    velocity = jnp.sum(jnp.where(halo[:, 17:18] == choose, basin_row, 0.0), axis=1, keepdims=True)
    rate_szz = lame * dx_vx + stiffness * dz_vz
    rate_szz = rate_szz + jnp.where((lane == 0) & at_top, PENALTY * (-pressure - szz), 0.0)
    new_el_ref[0, 3, here, :] = szz + STEP * rate_szz
    new_el_ref[0, 4, here, :] = sxz + STEP * (shear * (dz(vx, 0) + dx_ref[1]))
    new_ac_ref[0, 0, here, :] = p - STEP * (bulk * (dx_ref[5] + dz(ovz, 7)))
    new_ac_ref[0, 1, here, :] = ovx - STEP * (ocean_buoyancy * dx_ref[4])
    rate_ovz = -ocean_buoyancy * dz(p, 5)
    rate_ovz = rate_ovz + jnp.where((lane == depth - 1) & at_bottom, PENALTY * (velocity - ovz), 0.0)
    new_ac_ref[0, 2, here, :] = ovz + STEP * rate_ovz
    open_ref[here, :] = jnp.ones((tile, depth), jnp.float32)

    @pl.when(step == pl.num_programs(0) - 1)
    def _():
        place = lax.broadcasted_iota(jnp.int32, (8, LANES), 0) * LANES
        place = place + lax.broadcasted_iota(jnp.int32, (8, LANES), 1)
        n_el = new_el_ref.shape[1]

        def one_patch(q, carry):
            def one_slot(r, inner):
                x, z = split(cells_ref[0, 0, 0, q, r], depth)
                (high, row), (low, at) = split(x, 8), split(z, LANES)
                at_row = pl.ds(pl.multiple_of(high * 8, 8), 8)
                at_lane = pl.ds(pl.multiple_of(low * LANES, LANES), LANES)
                hit = place == row * LANES + at
                group, within = split(r, LANES)
                for f in range(8):
                    target = new_el_ref.at[0, f] if f < n_el else new_ac_ref.at[0, f - n_el]
                    target[at_row, at_lane] = jnp.where(hit, interp_ref[q, group, f, within], target[at_row, at_lane])
                open_ref[at_row, at_lane] = jnp.where(hit, 0.0, open_ref[at_row, at_lane])
                return inner

            return lax.fori_loop(0, counts_ref[0, 0, 0, q], one_slot, carry)

        lax.fori_loop(0, counts_ref.shape[3], one_patch, 0)


def far_kernel(coefficients, turn_ref, d_ref, far_ref, media_ref, open_ref, base_ref, next_ref, out_ref):
    del turn_ref, next_ref
    far = jnp.dot(d_ref[...], three_right(far_ref[...]), preferred_element_type=jnp.float32)
    media = [media_ref[0, i] for i in range(media_ref.shape[1])]
    is_open = open_ref[...] > 0.5
    for i, coefficient in enumerate(coefficients):
        old = base_ref[0, i]
        out_ref[0, i] = jnp.where(is_open, old + (STEP * coefficient(*media)) * far, old)


def add_far(base, operator, far, at, media, first_media, n_media, first_field, coefficients, opened, turn):
    rows, reach = operator.shape[0], far.shape[0]
    width = far.shape[1]
    tile = math.gcd(math.gcd(width, at), 2 * LANES)
    n_out = len(coefficients)
    shift = at // tile
    return pl.pallas_call(
        functools.partial(far_kernel, coefficients),
        grid=(width // tile,),
        in_specs=[
            pl.BlockSpec(memory_space=pl.ANY),
            pl.BlockSpec((rows, 3 * reach), lambda i: (0, 0)),
            pl.BlockSpec((reach, tile), lambda i: (0, i)),
            pl.BlockSpec((1, n_media, rows, tile), lambda i: (0, first_media // n_media, 0, i + shift)),
            pl.BlockSpec((rows, tile), lambda i: (0, i + shift)),
            pl.BlockSpec((1, n_out, rows, tile), lambda i: (0, first_field // n_out, 0, i + shift)),
        ],
        out_specs=[
            pl.BlockSpec(memory_space=pl.ANY),
            pl.BlockSpec((1, n_out, rows, tile), lambda i: (0, first_field // n_out, 0, i + shift)),
        ],
        out_shape=[
            jax.ShapeDtypeStruct(turn.shape, turn.dtype),
            jax.ShapeDtypeStruct(base.shape, base.dtype),
        ],
        input_output_aliases={0: 0, 5: 1},
        compiler_params=pltpu.CompilerParams(vmem_limit_bytes=16 * MIB),
        cost_estimate=pl.CostEstimate(
            flops=6 * rows * reach * width,
            bytes_accessed=4 * rows * width * (3 + n_media + n_out),
            transcendentals=0,
        ),
        name="add_far",
    )(turn, operator, far, in_hbm(media), opened, base)


def prepare_kernel(coefficient, field, at, base_ref, media_ref, open_ref, same_ref, old_ref, scale_ref, semaphore):
    del same_ref
    load = pltpu.make_async_copy(base_ref.at[0, field, :, pl.ds(at, old_ref.shape[1])], old_ref, semaphore)
    load.start()
    scale_ref[...] = jnp.where(open_ref[...] > 0.5, STEP * coefficient(media_ref[0, 0]), 0.0)
    load.wait()


def prepare_last(base, media, first_media, field, coefficient, opened, at, width):
    rows = opened.shape[0]
    anywhere = pl.BlockSpec(memory_space=pl.ANY)
    vmem = pl.BlockSpec(memory_space=pltpu.VMEM)
    return pl.pallas_call(
        functools.partial(prepare_kernel, coefficient, field, at),
        grid=(1,),
        in_specs=[
            anywhere,
            pl.BlockSpec((1, 1, rows, width), lambda i: (0, first_media, 0, at // width)),
            pl.BlockSpec((rows, width), lambda i: (0, at // width)),
        ],
        out_specs=[anywhere, vmem, vmem],
        out_shape=[
            jax.ShapeDtypeStruct(base.shape, base.dtype),
            pltpu.VMEM((rows, width), jnp.float32),
            pltpu.VMEM((rows, width), jnp.float32),
        ],
        scratch_shapes=[pltpu.SemaphoreType.DMA],
        input_output_aliases={0: 0},
        compiler_params=pltpu.CompilerParams(vmem_limit_bytes=16 * MIB),
        cost_estimate=pl.CostEstimate(flops=rows * width, bytes_accessed=20 * rows * width, transcendentals=0),
        name="prepare_last",
    )(base, in_hbm(media), opened)


def finish_kernel(field, at, parts, d_ref, far_ref, old_ref, scale_ref, base_ref, out_ref, held, semaphores):
    del base_ref
    rows, width = old_ref.shape[0] // parts, old_ref.shape[1]
    far_field = three_right(far_ref[...])
    stores = []
    for part in range(parts):
        here = pl.ds(part * rows, rows)
        far = jnp.dot(d_ref[here, :], far_field, preferred_element_type=jnp.float32)
        held[here, :] = old_ref[here, :] + scale_ref[here, :] * far
        stores.append(
            pltpu.make_async_copy(
                held.at[here], out_ref.at[0, field, here, pl.ds(at, width)], semaphores.at[part]
            )
        )
        stores[-1].start()
    for store in stores:
        store.wait()


def finish_last(base, operator, far, old, scale, field, at):
    rows, width = old.shape
    parts = 4
    anywhere = pl.BlockSpec(memory_space=pl.ANY)
    vmem = pl.BlockSpec(memory_space=pltpu.VMEM)
    return pl.pallas_call(
        functools.partial(finish_kernel, field, at, parts),
        in_specs=[vmem] * 4 + [anywhere],
        out_specs=anywhere,
        out_shape=jax.ShapeDtypeStruct(base.shape, base.dtype),
        scratch_shapes=[pltpu.VMEM((rows, width), jnp.float32), pltpu.SemaphoreType.DMA((parts,))],
        input_output_aliases={4: 0},
        compiler_params=pltpu.CompilerParams(vmem_limit_bytes=16 * MIB),
        cost_estimate=pl.CostEstimate(
            flops=2 * rows * operator.shape[1] * width, bytes_accessed=4 * rows * width, transcendentals=0
        ),
        name="finish_last",
    )(operator, far, old, scale, base)


def per_device(
    elastic,
    acoustic,
    el_media,
    ac_media,
    cont_matrix,
    fringe_cells,
    donor_cells,
    donor_weights,
    donor_counts,
    el_pair,
    ac_pair,
):
    rows, depth = elastic.shape[2], elastic.shape[3]
    slabs = lax.axis_size("line")
    layers = lax.axis_size("layer")
    patches = lax.axis_size("patch")
    slots = fringe_cells.shape[-1]
    groups = slots // LANES
    me = lax.axis_index("line")
    layer = lax.axis_index("layer")
    tile = min(64, rows)

    def other_slabs(value):
        parts = [
            lax.ppermute(value, "line", [(i, (i + distance) % slabs) for i in range(slabs)])
            for distance in range(1, slabs)
        ]
        return parts[0] if slabs == 2 else jnp.concatenate(parts, axis=0)

    half, quarter = depth // 2, depth // 4
    pieces = [
        ("el", 0, 0, depth, "el", 0, 3, 2, (lambda b, l, m: l + 2.0 * m, lambda b, l, m: l)),
        ("ac", 0, 0, depth, "ac", 1, 1, 1, (lambda b: -b,)),
        ("ac", 1, 0, depth, "ac", 0, 1, 0, (lambda k: -k,)),
        ("el", 1, 0, depth, "el", 2, 1, 4, (lambda m: m,)),
        ("el", 2, 0, depth, "el", 0, 1, 0, (lambda b: b,)),
        ("el", 4, 0, half, "el", 0, 1, 1, (lambda b: b,)),
        ("el", 4, half, quarter, "el", 0, 1, 1, (lambda b: b,)),
        ("el", 4, half + quarter, quarter, "el", 0, 1, 1, (lambda b: b,)),
    ]
    travelling = [piece[:4] for piece in pieces]
    first = take_first(elastic, travelling[0][1])
    *others, edges, asked = take_pieces(
        elastic, acoustic, travelling[1:], first, donor_cells, donor_weights, layers
    )
    far = [other_slabs(value) for value in [first, *others[2:]]]
    ocean_pair = lax.all_gather(jnp.concatenate(others[:2], axis=1), "line")
    behind = [(me - distance) % slabs for distance in range(1, slabs)]
    ocean_far = [lax.dynamic_index_in_dim(ocean_pair, source, 0, keepdims=False) for source in behind]
    ocean_far = ocean_far[0] if slabs == 2 else jnp.concatenate(ocean_far, axis=0)
    far[1:1] = [ocean_far[:, :depth], ocean_far[:, depth:]]

    asked = lax.all_to_all(asked, "patch", split_axis=0, concat_axis=0, tiled=True)
    asked_words = asked[:, :4].astype(jnp.int32)

    smem = pl.BlockSpec(memory_space=pltpu.SMEM)
    vmem = pl.BlockSpec(memory_space=pltpu.VMEM)
    local = pl.pallas_call(
        functools.partial(gather_kernel, 8, rows, depth),
        in_specs=[smem, smem, vmem, vmem],
        out_specs=vmem,
        out_shape=jax.ShapeDtypeStruct((patches, groups, 8, LANES), jnp.float32),
        scratch_shapes=[pltpu.VMEM((8 * rows * (depth // LANES) + rows, LANES), jnp.float32)],
        compiler_params=pltpu.CompilerParams(vmem_limit_bytes=24 * MIB),
        cost_estimate=pl.CostEstimate(flops=10**9, bytes_accessed=32 * rows * depth, transcendentals=0),
        name="donor_gather",
    )(asked_words, asked, in_hbm(elastic), in_hbm(acoustic))
    interp = lax.all_to_all(local, "patch", split_axis=0, concat_axis=0, tiled=True)
    edges = lax.all_to_all(edges, "layer", split_axis=0, concat_axis=0, tiled=True)

    near, far_operator = near_derivatives(elastic, acoustic, cont_matrix, me, slabs)
    new_el, new_ac, opened = pl.pallas_call(
        functools.partial(section_kernel, layers, rows, depth, tile),
        grid=(rows // tile,),
        in_specs=[
            smem,
            smem,
            smem,
            pl.BlockSpec((6, tile, depth), lambda i: (0, i, 0)),
            pl.BlockSpec((1, 5, tile, depth), lambda i: (0, 0, i, 0)),
            pl.BlockSpec((1, 3, tile, depth), lambda i: (0, 0, i, 0)),
            pl.BlockSpec((1, 3, tile, depth), lambda i: (0, 0, i, 0)),
            pl.BlockSpec((1, 2, tile, depth), lambda i: (0, 0, i, 0)),
            vmem,
            vmem,
            vmem,
        ],
        out_specs=[vmem, vmem, vmem],
        out_shape=[
            jax.ShapeDtypeStruct(elastic.shape, jnp.float32),
            jax.ShapeDtypeStruct(acoustic.shape, jnp.float32),
            pltpu.VMEM((rows, depth), jnp.float32),
        ],
        scratch_shapes=[pltpu.VMEM((rows, LANES), jnp.float32)],
        compiler_params=pltpu.CompilerParams(vmem_limit_bytes=32 * MIB),
        cost_estimate=pl.CostEstimate(
            flops=100 * rows * depth, bytes_accessed=112 * rows * depth, transcendentals=0
        ),
        name="near_section",
    )(
        fringe_cells,
        donor_counts,
        interp,
        near,
        in_hbm(elastic),
        in_hbm(acoustic),
        in_hbm(el_media),
        in_hbm(ac_media),
        edges,
        el_pair,
        ac_pair,
    )

    turn = jnp.zeros((8, LANES), jnp.float32)
    section = {"el": new_el, "ac": new_ac}
    media = {"el": el_media, "ac": ac_media}
    *middle, closing = pieces
    _, _, last_at, last_width, last_target, last_media, _, last_field, (last_coefficient,) = closing
    for i, (_, _, at, _, target, first_media, n_media, first_field, coefficients) in enumerate(middle):
        if i == len(middle) - 1:
            section[last_target], old, scale = prepare_last(
                section[last_target], media[last_target], last_media, last_field, last_coefficient,
                opened, last_at, last_width,
            )
        turn, section[target] = add_far(
            section[target], far_operator, far[i], at,
            media[target], first_media, n_media, first_field, coefficients, opened, turn,
        )
    section[last_target] = finish_last(
        section[last_target], far_operator, far[-1], old, scale, last_field, last_at
    )
    return section["el"], section["ac"]


def solution(mesh):
    placed = (
        P("patch", None, "line", "layer"),
        P("patch", None, "line", "layer"),
        P("patch", None, "line", "layer"),
        P("patch", None, "line", "layer"),
        P(),
        P("patch", "line", "layer", None, None),
        P("patch", "line", "layer", None, None, None),
        P("patch", "line", "layer", None, None, None),
        P("patch", "line", "layer", None),
        P("patch", "line"),
        P("patch", "line"),
    )
    return jax.shard_map(
        per_device,
        mesh=mesh,
        in_specs=placed,
        out_specs=(P("patch", None, "line", "layer"), P("patch", None, "line", "layer")),
        check_vma=False,
    )
```

```python
import functools
import math

import jax
import jax.numpy as jnp
import numpy as np
from jax import lax
from jax.experimental import pallas as pl
from jax.experimental.pallas import tpu as pltpu
from jax.sharding import PartitionSpec as P

STEP = 0.25
PENALTY = 2.0
LANES = 128
MIB = 1024 * 1024
HIGHEST = lax.Precision.HIGHEST


def in_hbm(array):
    return pltpu.with_memory_space_constraint(array, pltpu.HBM)


def derivative_row(period):
    n = np.arange(1, period)
    sign = np.where(n % 2 == 0, 1.0, -1.0)
    row = np.zeros(period)
    row[1:] = (math.pi / period) * sign / np.tan(math.pi * n / period)
    return row


def operator_tables(rows, slabs, cont):
    points = rows * slabs
    period = points + cont
    row = derivative_row(period)
    j = np.arange(rows)
    own = row[(j[:, None] - j[None, :]) % period]
    far, tail = [], []
    for me in range(slabs):
        mine = me * rows + j[:, None]
        others = np.concatenate([(me - d) % slabs * rows + j for d in range(1, slabs)])
        far.append(row[(mine - others[None, :]) % period])
        tail.append(row[(mine - points - np.arange(cont)[None, :]) % period])
    return tuple(jnp.asarray(np.asarray(table, np.float32)) for table in (own, far, tail))


def continuation_on(cont_matrix, rows, slabs, sources):
    match = cont_matrix.shape[1] // 2
    on_last = jnp.pad(cont_matrix[:, :match], ((0, 0), (rows - match, 0)))
    on_first = jnp.pad(cont_matrix[:, match:], ((0, 0), (0, rows - match)))
    return jnp.concatenate(
        [
            jnp.where(source == slabs - 1, on_last, 0.0) + jnp.where(source == 0, on_first, 0.0)
            for source in sources
        ],
        axis=1,
    )


def split(value, size):
    if size & (size - 1) == 0:
        return lax.shift_right_logical(value, size.bit_length() - 1), value & (size - 1)
    return lax.div(value, size), lax.rem(value, size)


def take_kernel(pieces, parts, elastic_ref, acoustic_ref, *refs):
    n = len(pieces)
    outs, held, in_semaphores, out_semaphores = refs[:n], refs[n : 2 * n], refs[-2], refs[-1]
    rows = elastic_ref.shape[2]
    loads, stores = [], []
    for i, (name, field, at, width) in enumerate(pieces):
        source = elastic_ref if name == "el" else acoustic_ref
        for part in range(parts):
            here = pl.ds(part * (rows // parts), rows // parts)
            k = i * parts + part
            loads.append(
                pltpu.make_async_copy(source.at[0, field, here, pl.ds(at, width)], held[i].at[here], in_semaphores.at[k])
            )
            stores.append(pltpu.make_async_copy(held[i].at[here], outs[i].at[here], out_semaphores.at[k]))
    for load in loads:
        load.start()
    for load, store in zip(loads, stores):
        load.wait()
        store.start()
    return stores


def take_first_kernel(field, parts, elastic_ref, out_ref, semaphores):
    rows = out_ref.shape[0] // parts
    copies = []
    for part in range(parts):
        here = pl.ds(part * rows, rows)
        copies.append(pltpu.make_async_copy(elastic_ref.at[0, field, here], out_ref.at[here], semaphores.at[part]))
        copies[-1].start()
    for copy in copies:
        copy.wait()


def take_first(elastic, field):
    rows, depth = elastic.shape[2:]
    parts = 4
    return pl.pallas_call(
        functools.partial(take_first_kernel, field, parts),
        in_specs=[pl.BlockSpec(memory_space=pl.ANY)],
        out_specs=pl.BlockSpec(memory_space=pltpu.VMEM),
        out_shape=pltpu.VMEM((rows, depth), jnp.float32),
        scratch_shapes=[pltpu.SemaphoreType.DMA((parts,))],
        compiler_params=pltpu.CompilerParams(vmem_limit_bytes=16 * MIB),
        cost_estimate=pl.CostEstimate(flops=0, bytes_accessed=8 * rows * depth, transcendentals=0),
        name="take_first",
    )(in_hbm(elastic))


def take_and_edges_kernel(
    pieces, parts, layers, after_ref, elastic_ref, acoustic_ref, cells_ref, weights_ref, *refs
):
    del after_ref
    n = len(pieces)
    edges_ref, asked_ref, tiles, edge_semaphores = refs[n : n + 4]
    n_el, n_ac = elastic_ref.shape[1], acoustic_ref.shape[1]
    rows, depth = elastic_ref.shape[2:]
    loads = []
    for end, at in enumerate((0, depth - LANES)):
        for k, (source, first, count) in enumerate(((elastic_ref, 0, n_el), (acoustic_ref, n_el, n_ac))):
            loads.append(
                pltpu.make_async_copy(
                    source.at[0, :, :, pl.ds(at, LANES)],
                    tiles.at[end, pl.ds(first, count)],
                    edge_semaphores.at[2 * end + k],
                )
            )
    for load in loads:
        load.start()
    stores = take_kernel(pieces, parts, elastic_ref, acoustic_ref, *refs[:n], *refs[n + 4 :])

    x, z = split(cells_ref[0, 0, 0], depth)
    chunk, at_lane = split(z, LANES)
    words = (chunk * ((n_el + n_ac) * rows) + x) * LANES + at_lane
    asked_ref[...] = jnp.concatenate([words.astype(jnp.float32), weights_ref[0, 0, 0]], axis=1)

    for load in loads:
        load.wait()
    lane = lax.broadcasted_iota(jnp.int32, (rows, LANES), 1)
    columns = jnp.zeros((rows, LANES), jnp.float32)
    for f in range(n_el + n_ac):
        columns = jnp.where(lane == f, tiles[0, f, :, 0:1], columns)
        columns = jnp.where(lane == 8 + f, tiles[1, f, :, LANES - 1 : LANES], columns)
    lines = columns.T
    below = lax.rem(lax.axis_index("layer") + 1, layers)
    for to in range(layers):
        edges_ref[to] = jnp.where(to == below, lines[8:16], lines[0:8])
    for store in stores:
        store.wait()


def take_pieces(elastic, acoustic, pieces, after, cells, weights, layers):
    rows = elastic.shape[2]
    anywhere = pl.BlockSpec(memory_space=pl.ANY)
    vmem = pl.BlockSpec(memory_space=pltpu.VMEM)
    out_shape = [jax.ShapeDtypeStruct((rows, width), jnp.float32) for _, _, _, width in pieces]
    parts = 2
    scratch = [pltpu.VMEM((2, 8, rows, LANES), jnp.float32), pltpu.SemaphoreType.DMA((4,))]
    scratch += [pltpu.VMEM((rows, width), jnp.float32) for _, _, _, width in pieces]
    scratch += [pltpu.SemaphoreType.DMA((len(pieces) * parts,))] * 2
    patches, corners, slots = cells.shape[3:]
    out_shape.append(jax.ShapeDtypeStruct((layers, 8, rows), jnp.float32))
    out_shape.append(jax.ShapeDtypeStruct((patches, 2 * corners, slots), jnp.float32))
    cost = sum(width for _, _, _, width in pieces) * rows
    return pl.pallas_call(
        functools.partial(take_and_edges_kernel, pieces, parts, layers),
        in_specs=[anywhere] * 3 + [vmem] * 2,
        out_specs=[anywhere] * len(pieces) + [vmem] * 2,
        out_shape=out_shape,
        scratch_shapes=scratch,
        compiler_params=pltpu.CompilerParams(vmem_limit_bytes=24 * MIB),
        cost_estimate=pl.CostEstimate(flops=0, bytes_accessed=8 * cost, transcendentals=0),
        name="take_pieces",
    )(after, in_hbm(elastic), in_hbm(acoustic), cells, weights)


def gather_kernel(fields, rows, depth, words_ref, weights_ref, elastic_ref, acoustic_ref, out_ref, mixed):
    n_el = elastic_ref.shape[1]
    chunks = depth // LANES
    for f in range(fields):
        source = elastic_ref.at[0, f] if f < n_el else acoustic_ref.at[0, f - n_el]
        for c in range(chunks):
            mixed[pl.ds((c * fields + f) * rows, rows), :] = source[:, c * LANES : (c + 1) * LANES]
    lane = lax.broadcasted_iota(jnp.int32, (fields, LANES), 1)
    groups = out_ref.shape[1]

    def one_group(step, carry):
        patch, group = split(step, groups)

        def one_slot(r, values):
            slot = group * LANES + r
            total = None
            for s in range(4):
                start, at = split(words_ref[patch, s, slot], LANES)
                picked = mixed[pl.ds(start, fields, stride=rows), :]
                term = jnp.where(lane == at, picked * weights_ref[patch, 4 + s, slot], 0.0)
                total = term if total is None else total + term
            column = jnp.sum(total, axis=1, keepdims=True)
            return jnp.where(lane == r, column, values)

        values = lax.fori_loop(0, LANES, one_slot, jnp.zeros((fields, LANES), jnp.float32), unroll=16)
        out_ref[patch, group] = values
        return carry

    lax.fori_loop(0, out_ref.shape[0] * groups, one_group, 0)


def bf16_pair(value):
    high = value.astype(jnp.bfloat16)
    return high, (value - high.astype(jnp.float32)).astype(jnp.bfloat16)


def three_left(value):
    high, low = bf16_pair(value)
    return jnp.concatenate([high, high, low], axis=1)


def three_right(value):
    high, low = bf16_pair(value)
    return jnp.concatenate([high, low, high], axis=0)


def near_kernel(
    n_el, me_ref, own_ref, far_ref, tail_ref, own_cont_ref, far_cont_ref, elastic_ref, acoustic_ref,
    out_ref, far_operator_ref, operator,
):
    del me_ref

    @pl.when(pl.program_id(0) == 0)
    def _():
        def folded(table, cont):
            return table + jnp.dot(tail_ref[0], cont, precision=HIGHEST, preferred_element_type=jnp.float32)

        operator[...] = three_left(folded(own_ref[...], own_cont_ref[...]))
        far_operator_ref[...] = three_left(folded(far_ref[0], far_cont_ref[...]))

    value = jnp.where(pl.program_id(0) < n_el, elastic_ref[0, 0], acoustic_ref[0, 0])
    out_ref[0] = jnp.dot(operator[...], three_right(value), preferred_element_type=jnp.float32)


def near_derivatives(elastic, acoustic, cont_matrix, me, slabs):
    rows, depth = elastic.shape[2:]
    cont = cont_matrix.shape[0]
    reach = (slabs - 1) * rows
    own, far, tail = operator_tables(rows, slabs, cont)
    own_cont = continuation_on(cont_matrix, rows, slabs, [me])
    far_cont = continuation_on(cont_matrix, rows, slabs, [(me - d) % slabs for d in range(1, slabs)])
    return pl.pallas_call(
        functools.partial(near_kernel, 4),
        grid_spec=pltpu.PrefetchScalarGridSpec(
            num_scalar_prefetch=1,
            grid=(6,),
            in_specs=[
                pl.BlockSpec((rows, rows), lambda f, me: (0, 0)),
                pl.BlockSpec((1, rows, reach), lambda f, me: (me[0], 0, 0)),
                pl.BlockSpec((1, rows, cont), lambda f, me: (me[0], 0, 0)),
                pl.BlockSpec((cont, rows), lambda f, me: (0, 0)),
                pl.BlockSpec((cont, reach), lambda f, me: (0, 0)),
                pl.BlockSpec((1, 1, rows, depth), lambda f, me: (0, jnp.where(f < 3, f, 4), 0, 0)),
                pl.BlockSpec((1, 1, rows, depth), lambda f, me: (0, jnp.maximum(f - 4, 0), 0, 0)),
            ],
            out_specs=[
                pl.BlockSpec((1, rows, depth), lambda f, me: (f, 0, 0)),
                pl.BlockSpec((rows, 3 * reach), lambda f, me: (0, 0)),
            ],
            scratch_shapes=[pltpu.VMEM((rows, 3 * rows), jnp.bfloat16)],
        ),
        out_shape=[
            pltpu.HBM((6, rows, depth), jnp.float32),
            pltpu.VMEM((rows, 3 * reach), jnp.bfloat16),
        ],
        compiler_params=pltpu.CompilerParams(vmem_limit_bytes=24 * MIB),
        cost_estimate=pl.CostEstimate(
            flops=36 * rows * rows * depth, bytes_accessed=60 * rows * depth, transcendentals=0
        ),
        name="near_dx",
    )(
        me.reshape(1), in_hbm(own), in_hbm(far), in_hbm(tail), own_cont, far_cont, in_hbm(elastic), in_hbm(acoustic)
    )


def section_kernel(
    layers, rows, depth, tile,
    cells_ref, counts_ref, interp_ref,
    dx_ref, elastic_ref, acoustic_ref, el_media_ref, ac_media_ref, edges_ref, el_pair_ref, ac_pair_ref,
    new_el_ref, new_ac_ref, open_ref,
    columns,
):
    step = pl.program_id(0)
    here = pl.ds(pl.multiple_of(step * tile, tile), tile)
    lane = lax.broadcasted_iota(jnp.int32, (tile, depth), 1)
    layer = lax.axis_index("layer")
    at_top, at_bottom = layer == 0, layer == layers - 1
    from_above = edges_ref[lax.rem(layer + layers - 1, layers)]
    from_below = edges_ref[lax.rem(layer + 1, layers)]
    ocean_row = from_above[5:6]
    basin_row = from_below[1:2]

    @pl.when(step == 0)
    def _():
        pairs = jnp.concatenate([el_pair_ref[...], ac_pair_ref[...]]).astype(jnp.float32)
        lines = [
            jnp.where(at_top, 0.0, from_above),
            jnp.where(at_bottom, 0.0, from_below),
            pairs,
            jnp.zeros((LANES - 18, rows), jnp.float32),
        ]
        columns[...] = jnp.concatenate(lines).T

    halo = columns[here, :]

    def dz(value, slot):
        above = halo[:, slot : slot + 1]
        below = halo[:, 8 + slot : 9 + slot]
        following = jnp.where(lane == depth - 1, below, pltpu.roll(value, depth - 1, 1))
        previous = jnp.where(lane == 0, above, pltpu.roll(value, 1, 1))
        return (following - previous) * 0.5

    vx, vz, sxx, szz, sxz = [elastic_ref[0, f] for f in range(5)]
    p, ovx, ovz = [acoustic_ref[0, f] for f in range(3)]
    buoyancy = el_media_ref[0, 0]
    lame = el_media_ref[0, 1]
    shear = el_media_ref[0, 2]
    stiffness = lame + 2.0 * shear
    bulk = ac_media_ref[0, 0]
    ocean_buoyancy = ac_media_ref[0, 1]

    dx_vx = dx_ref[0]
    dz_vz = dz(vz, 1)
    new_el_ref[0, 0, here, :] = vx + STEP * (buoyancy * (dx_ref[2] + dz(sxz, 4)))
    new_el_ref[0, 1, here, :] = vz + STEP * (buoyancy * (dx_ref[3] + dz(szz, 3)))
    new_el_ref[0, 2, here, :] = sxx + STEP * (stiffness * dx_vx + lame * dz_vz)
    choose = lax.broadcasted_iota(jnp.int32, (tile, rows), 1).astype(jnp.float32)
    pressure = jnp.sum(jnp.where(halo[:, 16:17] == choose, ocean_row, 0.0), axis=1, keepdims=True)
    velocity = jnp.sum(jnp.where(halo[:, 17:18] == choose, basin_row, 0.0), axis=1, keepdims=True)
    rate_szz = lame * dx_vx + stiffness * dz_vz
    rate_szz = rate_szz + jnp.where((lane == 0) & at_top, PENALTY * (-pressure - szz), 0.0)
    new_el_ref[0, 3, here, :] = szz + STEP * rate_szz
    new_el_ref[0, 4, here, :] = sxz + STEP * (shear * (dz(vx, 0) + dx_ref[1]))
    new_ac_ref[0, 0, here, :] = p - STEP * (bulk * (dx_ref[5] + dz(ovz, 7)))
    new_ac_ref[0, 1, here, :] = ovx - STEP * (ocean_buoyancy * dx_ref[4])
    rate_ovz = -ocean_buoyancy * dz(p, 5)
    rate_ovz = rate_ovz + jnp.where((lane == depth - 1) & at_bottom, PENALTY * (velocity - ovz), 0.0)
    new_ac_ref[0, 2, here, :] = ovz + STEP * rate_ovz
    open_ref[here, :] = jnp.ones((tile, depth), jnp.float32)

    @pl.when(step == pl.num_programs(0) - 1)
    def _():
        place = lax.broadcasted_iota(jnp.int32, (8, LANES), 0) * LANES
        place = place + lax.broadcasted_iota(jnp.int32, (8, LANES), 1)
        n_el = new_el_ref.shape[1]

        def one_patch(q, carry):
            def one_slot(r, inner):
                x, z = split(cells_ref[0, 0, 0, q, r], depth)
                (high, row), (low, at) = split(x, 8), split(z, LANES)
                at_row = pl.ds(pl.multiple_of(high * 8, 8), 8)
                at_lane = pl.ds(pl.multiple_of(low * LANES, LANES), LANES)
                hit = place == row * LANES + at
                group, within = split(r, LANES)
                for f in range(8):
                    target = new_el_ref.at[0, f] if f < n_el else new_ac_ref.at[0, f - n_el]
                    target[at_row, at_lane] = jnp.where(hit, interp_ref[q, group, f, within], target[at_row, at_lane])
                open_ref[at_row, at_lane] = jnp.where(hit, 0.0, open_ref[at_row, at_lane])
                return inner

            return lax.fori_loop(0, counts_ref[0, 0, 0, q], one_slot, carry)

        lax.fori_loop(0, counts_ref.shape[3], one_patch, 0)


def far_kernel(coefficients, turn_ref, d_ref, far_ref, media_ref, open_ref, base_ref, next_ref, out_ref):
    del turn_ref, next_ref
    far = jnp.dot(d_ref[...], three_right(far_ref[...]), preferred_element_type=jnp.float32)
    media = [media_ref[0, i] for i in range(media_ref.shape[1])]
    is_open = open_ref[...] > 0.5
    for i, coefficient in enumerate(coefficients):
        old = base_ref[0, i]
        out_ref[0, i] = jnp.where(is_open, old + (STEP * coefficient(*media)) * far, old)


def add_far(base, operator, far, at, media, first_media, n_media, first_field, coefficients, opened, turn):
    rows, reach = operator.shape[0], far.shape[0]
    width = far.shape[1]
    tile = math.gcd(math.gcd(width, at), 2 * LANES)
    n_out = len(coefficients)
    shift = at // tile
    return pl.pallas_call(
        functools.partial(far_kernel, coefficients),
        grid=(width // tile,),
        in_specs=[
            pl.BlockSpec(memory_space=pl.ANY),
            pl.BlockSpec((rows, 3 * reach), lambda i: (0, 0)),
            pl.BlockSpec((reach, tile), lambda i: (0, i)),
            pl.BlockSpec((1, n_media, rows, tile), lambda i: (0, first_media // n_media, 0, i + shift)),
            pl.BlockSpec((rows, tile), lambda i: (0, i + shift)),
            pl.BlockSpec((1, n_out, rows, tile), lambda i: (0, first_field // n_out, 0, i + shift)),
        ],
        out_specs=[
            pl.BlockSpec(memory_space=pl.ANY),
            pl.BlockSpec((1, n_out, rows, tile), lambda i: (0, first_field // n_out, 0, i + shift)),
        ],
        out_shape=[
            jax.ShapeDtypeStruct(turn.shape, turn.dtype),
            jax.ShapeDtypeStruct(base.shape, base.dtype),
        ],
        input_output_aliases={0: 0, 5: 1},
        compiler_params=pltpu.CompilerParams(vmem_limit_bytes=16 * MIB),
        cost_estimate=pl.CostEstimate(
            flops=6 * rows * reach * width,
            bytes_accessed=4 * rows * width * (3 + n_media + n_out),
            transcendentals=0,
        ),
        name="add_far",
    )(turn, operator, far, in_hbm(media), opened, base)


def prepare_kernel(coefficient, field, at, base_ref, media_ref, open_ref, same_ref, old_ref, scale_ref, semaphore):
    del same_ref
    load = pltpu.make_async_copy(base_ref.at[0, field, :, pl.ds(at, old_ref.shape[1])], old_ref, semaphore)
    load.start()
    scale_ref[...] = jnp.where(open_ref[...] > 0.5, STEP * coefficient(media_ref[0, 0]), 0.0)
    load.wait()


def prepare_last(base, media, first_media, field, coefficient, opened, at, width):
    rows = opened.shape[0]
    anywhere = pl.BlockSpec(memory_space=pl.ANY)
    vmem = pl.BlockSpec(memory_space=pltpu.VMEM)
    return pl.pallas_call(
        functools.partial(prepare_kernel, coefficient, field, at),
        grid=(1,),
        in_specs=[
            anywhere,
            pl.BlockSpec((1, 1, rows, width), lambda i: (0, first_media, 0, at // width)),
            pl.BlockSpec((rows, width), lambda i: (0, at // width)),
        ],
        out_specs=[anywhere, vmem, vmem],
        out_shape=[
            jax.ShapeDtypeStruct(base.shape, base.dtype),
            pltpu.VMEM((rows, width), jnp.float32),
            pltpu.VMEM((rows, width), jnp.float32),
        ],
        scratch_shapes=[pltpu.SemaphoreType.DMA],
        input_output_aliases={0: 0},
        compiler_params=pltpu.CompilerParams(vmem_limit_bytes=16 * MIB),
        cost_estimate=pl.CostEstimate(flops=rows * width, bytes_accessed=20 * rows * width, transcendentals=0),
        name="prepare_last",
    )(base, in_hbm(media), opened)


def finish_kernel(field, at, parts, d_ref, far_ref, old_ref, scale_ref, base_ref, out_ref, held, semaphores):
    del base_ref
    rows, width = old_ref.shape[0] // parts, old_ref.shape[1]
    far_field = three_right(far_ref[...])
    stores = []
    for part in range(parts):
        here = pl.ds(part * rows, rows)
        far = jnp.dot(d_ref[here, :], far_field, preferred_element_type=jnp.float32)
        held[here, :] = old_ref[here, :] + scale_ref[here, :] * far
        stores.append(
            pltpu.make_async_copy(
                held.at[here], out_ref.at[0, field, here, pl.ds(at, width)], semaphores.at[part]
            )
        )
        stores[-1].start()
    for store in stores:
        store.wait()


def finish_last(base, operator, far, old, scale, field, at):
    rows, width = old.shape
    parts = 2
    anywhere = pl.BlockSpec(memory_space=pl.ANY)
    vmem = pl.BlockSpec(memory_space=pltpu.VMEM)
    return pl.pallas_call(
        functools.partial(finish_kernel, field, at, parts),
        in_specs=[vmem] * 4 + [anywhere],
        out_specs=anywhere,
        out_shape=jax.ShapeDtypeStruct(base.shape, base.dtype),
        scratch_shapes=[pltpu.VMEM((rows, width), jnp.float32), pltpu.SemaphoreType.DMA((parts,))],
        input_output_aliases={4: 0},
        compiler_params=pltpu.CompilerParams(vmem_limit_bytes=16 * MIB),
        cost_estimate=pl.CostEstimate(
            flops=2 * rows * operator.shape[1] * width, bytes_accessed=4 * rows * width, transcendentals=0
        ),
        name="finish_last",
    )(operator, far, old, scale, base)


def per_device(
    elastic,
    acoustic,
    el_media,
    ac_media,
    cont_matrix,
    fringe_cells,
    donor_cells,
    donor_weights,
    donor_counts,
    el_pair,
    ac_pair,
):
    rows, depth = elastic.shape[2], elastic.shape[3]
    slabs = lax.axis_size("line")
    layers = lax.axis_size("layer")
    patches = lax.axis_size("patch")
    slots = fringe_cells.shape[-1]
    groups = slots // LANES
    me = lax.axis_index("line")
    layer = lax.axis_index("layer")
    tile = min(64, rows)

    def other_slabs(value):
        parts = [
            lax.ppermute(value, "line", [(i, (i + distance) % slabs) for i in range(slabs)])
            for distance in range(1, slabs)
        ]
        return parts[0] if slabs == 2 else jnp.concatenate(parts, axis=0)

    half, quarter = depth // 2, depth // 4
    pieces = [
        ("el", 0, 0, depth, "el", 0, 3, 2, (lambda b, l, m: l + 2.0 * m, lambda b, l, m: l)),
        ("ac", 0, 0, depth, "ac", 1, 1, 1, (lambda b: -b,)),
        ("ac", 1, 0, depth, "ac", 0, 1, 0, (lambda k: -k,)),
        ("el", 1, 0, depth, "el", 2, 1, 4, (lambda m: m,)),
        ("el", 2, 0, depth, "el", 0, 1, 0, (lambda b: b,)),
        ("el", 4, 0, half, "el", 0, 1, 1, (lambda b: b,)),
        ("el", 4, half, quarter, "el", 0, 1, 1, (lambda b: b,)),
        ("el", 4, half + quarter, quarter, "el", 0, 1, 1, (lambda b: b,)),
    ]
    travelling = [piece[:4] for piece in pieces]
    first = take_first(elastic, travelling[0][1])
    *others, edges, asked = take_pieces(
        elastic, acoustic, travelling[1:], first, donor_cells, donor_weights, layers
    )
    far = [other_slabs(value) for value in [first, *others]]

    asked = lax.all_to_all(asked, "patch", split_axis=0, concat_axis=0, tiled=True)
    asked_words = asked[:, :4].astype(jnp.int32)

    smem = pl.BlockSpec(memory_space=pltpu.SMEM)
    vmem = pl.BlockSpec(memory_space=pltpu.VMEM)
    local = pl.pallas_call(
        functools.partial(gather_kernel, 8, rows, depth),
        in_specs=[smem, smem, vmem, vmem],
        out_specs=vmem,
        out_shape=jax.ShapeDtypeStruct((patches, groups, 8, LANES), jnp.float32),
        scratch_shapes=[pltpu.VMEM((8 * rows * (depth // LANES) + rows, LANES), jnp.float32)],
        compiler_params=pltpu.CompilerParams(vmem_limit_bytes=24 * MIB),
        cost_estimate=pl.CostEstimate(flops=10**9, bytes_accessed=32 * rows * depth, transcendentals=0),
        name="donor_gather",
    )(asked_words, asked, in_hbm(elastic), in_hbm(acoustic))
    interp = lax.all_to_all(local, "patch", split_axis=0, concat_axis=0, tiled=True)
    edges = lax.all_to_all(edges, "layer", split_axis=0, concat_axis=0, tiled=True)

    near, far_operator = near_derivatives(elastic, acoustic, cont_matrix, me, slabs)
    new_el, new_ac, opened = pl.pallas_call(
        functools.partial(section_kernel, layers, rows, depth, tile),
        grid=(rows // tile,),
        in_specs=[
            smem,
            smem,
            smem,
            pl.BlockSpec((6, tile, depth), lambda i: (0, i, 0)),
            pl.BlockSpec((1, 5, tile, depth), lambda i: (0, 0, i, 0)),
            pl.BlockSpec((1, 3, tile, depth), lambda i: (0, 0, i, 0)),
            pl.BlockSpec((1, 3, tile, depth), lambda i: (0, 0, i, 0)),
            pl.BlockSpec((1, 2, tile, depth), lambda i: (0, 0, i, 0)),
            vmem,
            vmem,
            vmem,
        ],
        out_specs=[vmem, vmem, vmem],
        out_shape=[
            jax.ShapeDtypeStruct(elastic.shape, jnp.float32),
            jax.ShapeDtypeStruct(acoustic.shape, jnp.float32),
            pltpu.VMEM((rows, depth), jnp.float32),
        ],
        scratch_shapes=[pltpu.VMEM((rows, LANES), jnp.float32)],
        compiler_params=pltpu.CompilerParams(vmem_limit_bytes=32 * MIB),
        cost_estimate=pl.CostEstimate(
            flops=100 * rows * depth, bytes_accessed=112 * rows * depth, transcendentals=0
        ),
        name="near_section",
    )(
        fringe_cells,
        donor_counts,
        interp,
        near,
        in_hbm(elastic),
        in_hbm(acoustic),
        in_hbm(el_media),
        in_hbm(ac_media),
        edges,
        el_pair,
        ac_pair,
    )

    turn = jnp.zeros((8, LANES), jnp.float32)
    section = {"el": new_el, "ac": new_ac}
    media = {"el": el_media, "ac": ac_media}
    *middle, closing = pieces
    _, _, last_at, last_width, last_target, last_media, _, last_field, (last_coefficient,) = closing
    for i, (_, _, at, _, target, first_media, n_media, first_field, coefficients) in enumerate(middle):
        if i == len(middle) - 1:
            section[last_target], old, scale = prepare_last(
                section[last_target], media[last_target], last_media, last_field, last_coefficient,
                opened, last_at, last_width,
            )
        turn, section[target] = add_far(
            section[target], far_operator, far[i], at,
            media[target], first_media, n_media, first_field, coefficients, opened, turn,
        )
    section[last_target] = finish_last(
        section[last_target], far_operator, far[-1], old, scale, last_field, last_at
    )
    return section["el"], section["ac"]


def solution(mesh):
    placed = (
        P("patch", None, "line", "layer"),
        P("patch", None, "line", "layer"),
        P("patch", None, "line", "layer"),
        P("patch", None, "line", "layer"),
        P(),
        P("patch", "line", "layer", None, None),
        P("patch", "line", "layer", None, None, None),
        P("patch", "line", "layer", None, None, None),
        P("patch", "line", "layer", None),
        P("patch", "line"),
        P("patch", "line"),
    )
    return jax.shard_map(
        per_device,
        mesh=mesh,
        in_specs=placed,
        out_specs=(P("patch", None, "line", "layer"), P("patch", None, "line", "layer")),
        check_vma=False,
    )
```

```python
import functools
import math

import jax
import jax.numpy as jnp
import numpy as np
from jax import lax
from jax.experimental import pallas as pl
from jax.experimental.pallas import tpu as pltpu
from jax.sharding import PartitionSpec as P

STEP = 0.25
PENALTY = 2.0
LANES = 128
MIB = 1024 * 1024
HIGHEST = lax.Precision.HIGHEST


def in_hbm(array):
    return pltpu.with_memory_space_constraint(array, pltpu.HBM)


def derivative_row(period):
    n = np.arange(1, period)
    sign = np.where(n % 2 == 0, 1.0, -1.0)
    row = np.zeros(period)
    row[1:] = (math.pi / period) * sign / np.tan(math.pi * n / period)
    return row


def operator_tables(rows, slabs, cont):
    points = rows * slabs
    period = points + cont
    row = derivative_row(period)
    j = np.arange(rows)
    own = row[(j[:, None] - j[None, :]) % period]
    far, tail = [], []
    for me in range(slabs):
        mine = me * rows + j[:, None]
        others = np.concatenate([(me - d) % slabs * rows + j for d in range(1, slabs)])
        far.append(row[(mine - others[None, :]) % period])
        tail.append(row[(mine - points - np.arange(cont)[None, :]) % period])
    return tuple(jnp.asarray(np.asarray(table, np.float32)) for table in (own, far, tail))


def continuation_on(cont_matrix, rows, slabs, sources):
    match = cont_matrix.shape[1] // 2
    on_last = jnp.pad(cont_matrix[:, :match], ((0, 0), (rows - match, 0)))
    on_first = jnp.pad(cont_matrix[:, match:], ((0, 0), (0, rows - match)))
    return jnp.concatenate(
        [
            jnp.where(source == slabs - 1, on_last, 0.0) + jnp.where(source == 0, on_first, 0.0)
            for source in sources
        ],
        axis=1,
    )


def split(value, size):
    if size & (size - 1) == 0:
        return lax.shift_right_logical(value, size.bit_length() - 1), value & (size - 1)
    return lax.div(value, size), lax.rem(value, size)


def take_kernel(pieces, parts, elastic_ref, acoustic_ref, *refs):
    n = len(pieces)
    outs, held, in_semaphores, out_semaphores = refs[:n], refs[n : 2 * n], refs[-2], refs[-1]
    rows = elastic_ref.shape[2]
    loads, stores = [], []
    for i, (name, field, at, width) in enumerate(pieces):
        source = elastic_ref if name == "el" else acoustic_ref
        for part in range(parts):
            here = pl.ds(part * (rows // parts), rows // parts)
            k = i * parts + part
            loads.append(
                pltpu.make_async_copy(source.at[0, field, here, pl.ds(at, width)], held[i].at[here], in_semaphores.at[k])
            )
            stores.append(pltpu.make_async_copy(held[i].at[here], outs[i].at[here], out_semaphores.at[k]))
    for load in loads:
        load.start()
    for load, store in zip(loads, stores):
        load.wait()
        store.start()
    return stores


def take_field_kernel(field, parts, *refs):
    fields_ref, out_ref, semaphores = refs[-3:]
    rows = out_ref.shape[0] // parts
    copies = []
    for part in range(parts):
        here = pl.ds(part * rows, rows)
        copies.append(pltpu.make_async_copy(fields_ref.at[0, field, here], out_ref.at[here], semaphores.at[part]))
        copies[-1].start()
    for copy in copies:
        copy.wait()


def take_field(fields, field, after=None):
    rows, depth = fields.shape[2:]
    parts = 4
    operands = (in_hbm(fields),) if after is None else (after, in_hbm(fields))
    return pl.pallas_call(
        functools.partial(take_field_kernel, field, parts),
        in_specs=[pl.BlockSpec(memory_space=pl.ANY)] * len(operands),
        out_specs=pl.BlockSpec(memory_space=pltpu.VMEM),
        out_shape=pltpu.VMEM((rows, depth), jnp.float32),
        scratch_shapes=[pltpu.SemaphoreType.DMA((parts,))],
        compiler_params=pltpu.CompilerParams(vmem_limit_bytes=16 * MIB),
        cost_estimate=pl.CostEstimate(flops=0, bytes_accessed=8 * rows * depth, transcendentals=0),
        name="take_field",
    )(*operands)


def take_and_edges_kernel(
    pieces, parts, layers, after_ref, elastic_ref, acoustic_ref, cells_ref, weights_ref, *refs
):
    del after_ref
    n = len(pieces)
    edges_ref, asked_ref, tiles, edge_semaphores = refs[n : n + 4]
    n_el, n_ac = elastic_ref.shape[1], acoustic_ref.shape[1]
    rows, depth = elastic_ref.shape[2:]
    loads = []
    for end, at in enumerate((0, depth - LANES)):
        for k, (source, first, count) in enumerate(((elastic_ref, 0, n_el), (acoustic_ref, n_el, n_ac))):
            loads.append(
                pltpu.make_async_copy(
                    source.at[0, :, :, pl.ds(at, LANES)],
                    tiles.at[end, pl.ds(first, count)],
                    edge_semaphores.at[2 * end + k],
                )
            )
    for load in loads:
        load.start()
    stores = take_kernel(pieces, parts, elastic_ref, acoustic_ref, *refs[:n], *refs[n + 4 :])

    x, z = split(cells_ref[0, 0, 0], depth)
    chunk, at_lane = split(z, LANES)
    words = (chunk * ((n_el + n_ac) * rows) + x) * LANES + at_lane
    asked_ref[...] = jnp.concatenate([words.astype(jnp.float32), weights_ref[0, 0, 0]], axis=1)

    for load in loads:
        load.wait()
    lane = lax.broadcasted_iota(jnp.int32, (rows, LANES), 1)
    columns = jnp.zeros((rows, LANES), jnp.float32)
    for f in range(n_el + n_ac):
        columns = jnp.where(lane == f, tiles[0, f, :, 0:1], columns)
        columns = jnp.where(lane == 8 + f, tiles[1, f, :, LANES - 1 : LANES], columns)
    lines = columns.T
    below = lax.rem(lax.axis_index("layer") + 1, layers)
    for to in range(layers):
        edges_ref[to] = jnp.where(to == below, lines[8:16], lines[0:8])
    for store in stores:
        store.wait()


def take_pieces(elastic, acoustic, pieces, after, cells, weights, layers):
    rows = elastic.shape[2]
    anywhere = pl.BlockSpec(memory_space=pl.ANY)
    vmem = pl.BlockSpec(memory_space=pltpu.VMEM)
    out_shape = [jax.ShapeDtypeStruct((rows, width), jnp.float32) for _, _, _, width in pieces]
    parts = 2
    scratch = [pltpu.VMEM((2, 8, rows, LANES), jnp.float32), pltpu.SemaphoreType.DMA((4,))]
    scratch += [pltpu.VMEM((rows, width), jnp.float32) for _, _, _, width in pieces]
    scratch += [pltpu.SemaphoreType.DMA((len(pieces) * parts,))] * 2
    patches, corners, slots = cells.shape[3:]
    out_shape.append(jax.ShapeDtypeStruct((layers, 8, rows), jnp.float32))
    out_shape.append(jax.ShapeDtypeStruct((patches, 2 * corners, slots), jnp.float32))
    cost = sum(width for _, _, _, width in pieces) * rows
    return pl.pallas_call(
        functools.partial(take_and_edges_kernel, pieces, parts, layers),
        in_specs=[anywhere] * 3 + [vmem] * 2,
        out_specs=[anywhere] * len(pieces) + [vmem] * 2,
        out_shape=out_shape,
        scratch_shapes=scratch,
        compiler_params=pltpu.CompilerParams(vmem_limit_bytes=24 * MIB),
        cost_estimate=pl.CostEstimate(flops=0, bytes_accessed=8 * cost, transcendentals=0),
        name="take_pieces",
    )(after, in_hbm(elastic), in_hbm(acoustic), cells, weights)


def gather_kernel(fields, rows, depth, words_ref, weights_ref, elastic_ref, acoustic_ref, out_ref, mixed):
    n_el = elastic_ref.shape[1]
    chunks = depth // LANES
    for f in range(fields):
        source = elastic_ref.at[0, f] if f < n_el else acoustic_ref.at[0, f - n_el]
        for c in range(chunks):
            mixed[pl.ds((c * fields + f) * rows, rows), :] = source[:, c * LANES : (c + 1) * LANES]
    lane = lax.broadcasted_iota(jnp.int32, (fields, LANES), 1)
    groups = out_ref.shape[1]

    def one_group(step, carry):
        patch, group = split(step, groups)

        def one_slot(r, values):
            slot = group * LANES + r
            total = None
            for s in range(4):
                start, at = split(words_ref[patch, s, slot], LANES)
                picked = mixed[pl.ds(start, fields, stride=rows), :]
                term = jnp.where(lane == at, picked * weights_ref[patch, 4 + s, slot], 0.0)
                total = term if total is None else total + term
            column = jnp.sum(total, axis=1, keepdims=True)
            return jnp.where(lane == r, column, values)

        values = lax.fori_loop(0, LANES, one_slot, jnp.zeros((fields, LANES), jnp.float32), unroll=16)
        out_ref[patch, group] = values
        return carry

    lax.fori_loop(0, out_ref.shape[0] * groups, one_group, 0)


def bf16_pair(value):
    high = value.astype(jnp.bfloat16)
    return high, (value - high.astype(jnp.float32)).astype(jnp.bfloat16)


def three_left(value):
    high, low = bf16_pair(value)
    return jnp.concatenate([high, high, low], axis=1)


def three_right(value):
    high, low = bf16_pair(value)
    return jnp.concatenate([high, low, high], axis=0)


def near_kernel(
    n_el, me_ref, own_ref, far_ref, tail_ref, own_cont_ref, far_cont_ref, elastic_ref, acoustic_ref,
    out_ref, far_operator_ref, operator,
):
    del me_ref

    @pl.when(pl.program_id(0) == 0)
    def _():
        def folded(table, cont):
            return table + jnp.dot(tail_ref[0], cont, precision=HIGHEST, preferred_element_type=jnp.float32)

        operator[...] = three_left(folded(own_ref[...], own_cont_ref[...]))
        far_operator_ref[...] = three_left(folded(far_ref[0], far_cont_ref[...]))

    value = jnp.where(pl.program_id(0) < n_el, elastic_ref[0, 0], acoustic_ref[0, 0])
    out_ref[0] = jnp.dot(operator[...], three_right(value), preferred_element_type=jnp.float32)


def near_derivatives(elastic, acoustic, cont_matrix, me, slabs):
    rows, depth = elastic.shape[2:]
    cont = cont_matrix.shape[0]
    reach = (slabs - 1) * rows
    own, far, tail = operator_tables(rows, slabs, cont)
    own_cont = continuation_on(cont_matrix, rows, slabs, [me])
    far_cont = continuation_on(cont_matrix, rows, slabs, [(me - d) % slabs for d in range(1, slabs)])
    return pl.pallas_call(
        functools.partial(near_kernel, 4),
        grid_spec=pltpu.PrefetchScalarGridSpec(
            num_scalar_prefetch=1,
            grid=(6,),
            in_specs=[
                pl.BlockSpec((rows, rows), lambda f, me: (0, 0)),
                pl.BlockSpec((1, rows, reach), lambda f, me: (me[0], 0, 0)),
                pl.BlockSpec((1, rows, cont), lambda f, me: (me[0], 0, 0)),
                pl.BlockSpec((cont, rows), lambda f, me: (0, 0)),
                pl.BlockSpec((cont, reach), lambda f, me: (0, 0)),
                pl.BlockSpec((1, 1, rows, depth), lambda f, me: (0, jnp.where(f < 3, f, 4), 0, 0)),
                pl.BlockSpec((1, 1, rows, depth), lambda f, me: (0, jnp.maximum(f - 4, 0), 0, 0)),
            ],
            out_specs=[
                pl.BlockSpec((1, rows, depth), lambda f, me: (f, 0, 0)),
                pl.BlockSpec((rows, 3 * reach), lambda f, me: (0, 0)),
            ],
            scratch_shapes=[pltpu.VMEM((rows, 3 * rows), jnp.bfloat16)],
        ),
        out_shape=[
            pltpu.HBM((6, rows, depth), jnp.float32),
            pltpu.VMEM((rows, 3 * reach), jnp.bfloat16),
        ],
        compiler_params=pltpu.CompilerParams(vmem_limit_bytes=24 * MIB),
        cost_estimate=pl.CostEstimate(
            flops=36 * rows * rows * depth, bytes_accessed=60 * rows * depth, transcendentals=0
        ),
        name="near_dx",
    )(
        me.reshape(1), in_hbm(own), in_hbm(far), in_hbm(tail), own_cont, far_cont, in_hbm(elastic), in_hbm(acoustic)
    )


def section_kernel(
    layers, rows, depth, tile,
    cells_ref, counts_ref, interp_ref,
    dx_ref, elastic_ref, acoustic_ref, el_media_ref, ac_media_ref, edges_ref, el_pair_ref, ac_pair_ref,
    new_el_ref, new_ac_ref, open_ref,
    columns,
):
    step = pl.program_id(0)
    here = pl.ds(pl.multiple_of(step * tile, tile), tile)
    lane = lax.broadcasted_iota(jnp.int32, (tile, depth), 1)
    layer = lax.axis_index("layer")
    at_top, at_bottom = layer == 0, layer == layers - 1
    from_above = edges_ref[lax.rem(layer + layers - 1, layers)]
    from_below = edges_ref[lax.rem(layer + 1, layers)]
    ocean_row = from_above[5:6]
    basin_row = from_below[1:2]

    @pl.when(step == 0)
    def _():
        pairs = jnp.concatenate([el_pair_ref[...], ac_pair_ref[...]]).astype(jnp.float32)
        lines = [
            jnp.where(at_top, 0.0, from_above),
            jnp.where(at_bottom, 0.0, from_below),
            pairs,
            jnp.zeros((LANES - 18, rows), jnp.float32),
        ]
        columns[...] = jnp.concatenate(lines).T

    halo = columns[here, :]

    def dz(value, slot):
        above = halo[:, slot : slot + 1]
        below = halo[:, 8 + slot : 9 + slot]
        following = jnp.where(lane == depth - 1, below, pltpu.roll(value, depth - 1, 1))
        previous = jnp.where(lane == 0, above, pltpu.roll(value, 1, 1))
        return (following - previous) * 0.5

    vx, vz, sxx, szz, sxz = [elastic_ref[0, f] for f in range(5)]
    p, ovx, ovz = [acoustic_ref[0, f] for f in range(3)]
    buoyancy = el_media_ref[0, 0]
    lame = el_media_ref[0, 1]
    shear = el_media_ref[0, 2]
    stiffness = lame + 2.0 * shear
    bulk = ac_media_ref[0, 0]
    ocean_buoyancy = ac_media_ref[0, 1]

    dx_vx = dx_ref[0]
    dz_vz = dz(vz, 1)
    new_el_ref[0, 0, here, :] = vx + STEP * (buoyancy * (dx_ref[2] + dz(sxz, 4)))
    new_el_ref[0, 1, here, :] = vz + STEP * (buoyancy * (dx_ref[3] + dz(szz, 3)))
    new_el_ref[0, 2, here, :] = sxx + STEP * (stiffness * dx_vx + lame * dz_vz)
    choose = lax.broadcasted_iota(jnp.int32, (tile, rows), 1).astype(jnp.float32)
    pressure = jnp.sum(jnp.where(halo[:, 16:17] == choose, ocean_row, 0.0), axis=1, keepdims=True)
    velocity = jnp.sum(jnp.where(halo[:, 17:18] == choose, basin_row, 0.0), axis=1, keepdims=True)
    rate_szz = lame * dx_vx + stiffness * dz_vz
    rate_szz = rate_szz + jnp.where((lane == 0) & at_top, PENALTY * (-pressure - szz), 0.0)
    new_el_ref[0, 3, here, :] = szz + STEP * rate_szz
    new_el_ref[0, 4, here, :] = sxz + STEP * (shear * (dz(vx, 0) + dx_ref[1]))
    new_ac_ref[0, 0, here, :] = p - STEP * (bulk * (dx_ref[5] + dz(ovz, 7)))
    new_ac_ref[0, 1, here, :] = ovx - STEP * (ocean_buoyancy * dx_ref[4])
    rate_ovz = -ocean_buoyancy * dz(p, 5)
    rate_ovz = rate_ovz + jnp.where((lane == depth - 1) & at_bottom, PENALTY * (velocity - ovz), 0.0)
    new_ac_ref[0, 2, here, :] = ovz + STEP * rate_ovz
    open_ref[here, :] = jnp.ones((tile, depth), jnp.float32)

    @pl.when(step == pl.num_programs(0) - 1)
    def _():
        place = lax.broadcasted_iota(jnp.int32, (8, LANES), 0) * LANES
        place = place + lax.broadcasted_iota(jnp.int32, (8, LANES), 1)
        n_el = new_el_ref.shape[1]

        def one_patch(q, carry):
            def one_slot(r, inner):
                x, z = split(cells_ref[0, 0, 0, q, r], depth)
                (high, row), (low, at) = split(x, 8), split(z, LANES)
                at_row = pl.ds(pl.multiple_of(high * 8, 8), 8)
                at_lane = pl.ds(pl.multiple_of(low * LANES, LANES), LANES)
                hit = place == row * LANES + at
                group, within = split(r, LANES)
                for f in range(8):
                    target = new_el_ref.at[0, f] if f < n_el else new_ac_ref.at[0, f - n_el]
                    target[at_row, at_lane] = jnp.where(hit, interp_ref[q, group, f, within], target[at_row, at_lane])
                open_ref[at_row, at_lane] = jnp.where(hit, 0.0, open_ref[at_row, at_lane])
                return inner

            return lax.fori_loop(0, counts_ref[0, 0, 0, q], one_slot, carry)

        lax.fori_loop(0, counts_ref.shape[3], one_patch, 0)


def far_kernel(coefficients, turn_ref, d_ref, far_ref, media_ref, open_ref, base_ref, next_ref, out_ref):
    del turn_ref, next_ref
    far = jnp.dot(d_ref[...], three_right(far_ref[...]), preferred_element_type=jnp.float32)
    media = [media_ref[0, i] for i in range(media_ref.shape[1])]
    is_open = open_ref[...] > 0.5
    for i, coefficient in enumerate(coefficients):
        old = base_ref[0, i]
        out_ref[0, i] = jnp.where(is_open, old + (STEP * coefficient(*media)) * far, old)


def add_far(base, operator, far, at, media, first_media, n_media, first_field, coefficients, opened, turn):
    rows, reach = operator.shape[0], far.shape[0]
    width = far.shape[1]
    tile = math.gcd(math.gcd(width, at), 2 * LANES)
    n_out = len(coefficients)
    shift = at // tile
    return pl.pallas_call(
        functools.partial(far_kernel, coefficients),
        grid=(width // tile,),
        in_specs=[
            pl.BlockSpec(memory_space=pl.ANY),
            pl.BlockSpec((rows, 3 * reach), lambda i: (0, 0)),
            pl.BlockSpec((reach, tile), lambda i: (0, i)),
            pl.BlockSpec((1, n_media, rows, tile), lambda i: (0, first_media // n_media, 0, i + shift)),
            pl.BlockSpec((rows, tile), lambda i: (0, i + shift)),
            pl.BlockSpec((1, n_out, rows, tile), lambda i: (0, first_field // n_out, 0, i + shift)),
        ],
        out_specs=[
            pl.BlockSpec(memory_space=pl.ANY),
            pl.BlockSpec((1, n_out, rows, tile), lambda i: (0, first_field // n_out, 0, i + shift)),
        ],
        out_shape=[
            jax.ShapeDtypeStruct(turn.shape, turn.dtype),
            jax.ShapeDtypeStruct(base.shape, base.dtype),
        ],
        input_output_aliases={0: 0, 5: 1},
        compiler_params=pltpu.CompilerParams(vmem_limit_bytes=16 * MIB),
        cost_estimate=pl.CostEstimate(
            flops=6 * rows * reach * width,
            bytes_accessed=4 * rows * width * (3 + n_media + n_out),
            transcendentals=0,
        ),
        name="add_far",
    )(turn, operator, far, in_hbm(media), opened, base)


def prepare_kernel(coefficient, field, at, base_ref, media_ref, open_ref, same_ref, old_ref, scale_ref, semaphore):
    del same_ref
    load = pltpu.make_async_copy(base_ref.at[0, field, :, pl.ds(at, old_ref.shape[1])], old_ref, semaphore)
    load.start()
    scale_ref[...] = jnp.where(open_ref[...] > 0.5, STEP * coefficient(media_ref[0, 0]), 0.0)
    load.wait()


def prepare_last(base, media, first_media, field, coefficient, opened, at, width):
    rows = opened.shape[0]
    anywhere = pl.BlockSpec(memory_space=pl.ANY)
    vmem = pl.BlockSpec(memory_space=pltpu.VMEM)
    return pl.pallas_call(
        functools.partial(prepare_kernel, coefficient, field, at),
        grid=(1,),
        in_specs=[
            anywhere,
            pl.BlockSpec((1, 1, rows, width), lambda i: (0, first_media, 0, at // width)),
            pl.BlockSpec((rows, width), lambda i: (0, at // width)),
        ],
        out_specs=[anywhere, vmem, vmem],
        out_shape=[
            jax.ShapeDtypeStruct(base.shape, base.dtype),
            pltpu.VMEM((rows, width), jnp.float32),
            pltpu.VMEM((rows, width), jnp.float32),
        ],
        scratch_shapes=[pltpu.SemaphoreType.DMA],
        input_output_aliases={0: 0},
        compiler_params=pltpu.CompilerParams(vmem_limit_bytes=16 * MIB),
        cost_estimate=pl.CostEstimate(flops=rows * width, bytes_accessed=20 * rows * width, transcendentals=0),
        name="prepare_last",
    )(base, in_hbm(media), opened)


def finish_kernel(field, at, parts, d_ref, far_ref, old_ref, scale_ref, base_ref, out_ref, held, semaphores):
    del base_ref
    rows, width = old_ref.shape[0] // parts, old_ref.shape[1]
    far_field = three_right(far_ref[...])
    stores = []
    for part in range(parts):
        here = pl.ds(part * rows, rows)
        far = jnp.dot(d_ref[here, :], far_field, preferred_element_type=jnp.float32)
        held[here, :] = old_ref[here, :] + scale_ref[here, :] * far
        stores.append(
            pltpu.make_async_copy(
                held.at[here], out_ref.at[0, field, here, pl.ds(at, width)], semaphores.at[part]
            )
        )
        stores[-1].start()
    for store in stores:
        store.wait()


def finish_last(base, operator, far, old, scale, field, at):
    rows, width = old.shape
    parts = 2
    anywhere = pl.BlockSpec(memory_space=pl.ANY)
    vmem = pl.BlockSpec(memory_space=pltpu.VMEM)
    return pl.pallas_call(
        functools.partial(finish_kernel, field, at, parts),
        in_specs=[vmem] * 4 + [anywhere],
        out_specs=anywhere,
        out_shape=jax.ShapeDtypeStruct(base.shape, base.dtype),
        scratch_shapes=[pltpu.VMEM((rows, width), jnp.float32), pltpu.SemaphoreType.DMA((parts,))],
        input_output_aliases={4: 0},
        compiler_params=pltpu.CompilerParams(vmem_limit_bytes=16 * MIB),
        cost_estimate=pl.CostEstimate(
            flops=2 * rows * operator.shape[1] * width, bytes_accessed=4 * rows * width, transcendentals=0
        ),
        name="finish_last",
    )(operator, far, old, scale, base)


def per_device(
    elastic,
    acoustic,
    el_media,
    ac_media,
    cont_matrix,
    fringe_cells,
    donor_cells,
    donor_weights,
    donor_counts,
    el_pair,
    ac_pair,
):
    rows, depth = elastic.shape[2], elastic.shape[3]
    slabs = lax.axis_size("line")
    layers = lax.axis_size("layer")
    patches = lax.axis_size("patch")
    slots = fringe_cells.shape[-1]
    groups = slots // LANES
    me = lax.axis_index("line")
    layer = lax.axis_index("layer")
    tile = min(64, rows)

    def other_slabs(value):
        parts = [
            lax.ppermute(value, "line", [(i, (i + distance) % slabs) for i in range(slabs)])
            for distance in range(1, slabs)
        ]
        return parts[0] if slabs == 2 else jnp.concatenate(parts, axis=0)

    half, quarter = depth // 2, depth // 4
    pieces = [
        ("el", 0, 0, depth, "el", 0, 3, 2, (lambda b, l, m: l + 2.0 * m, lambda b, l, m: l)),
        ("ac", 0, 0, depth, "ac", 1, 1, 1, (lambda b: -b,)),
        ("ac", 1, 0, depth, "ac", 0, 1, 0, (lambda k: -k,)),
        ("el", 1, 0, depth, "el", 2, 1, 4, (lambda m: m,)),
        ("el", 2, 0, depth, "el", 0, 1, 0, (lambda b: b,)),
        ("el", 4, 0, half, "el", 0, 1, 1, (lambda b: b,)),
        ("el", 4, half, quarter, "el", 0, 1, 1, (lambda b: b,)),
        ("el", 4, half + quarter, quarter, "el", 0, 1, 1, (lambda b: b,)),
    ]
    travelling = [piece[:4] for piece in pieces]
    whole = [piece for piece in travelling if piece[3] == depth]
    fields = {"el": elastic, "ac": acoustic}
    taken = [take_field(fields[whole[0][0]], whole[0][1])]
    *others, edges, asked = take_pieces(
        elastic, acoustic, travelling[len(whole) :], taken[0], donor_cells, donor_weights, layers
    )
    for name, field, _, _ in whole[1:]:
        taken.append(take_field(fields[name], field, edges if len(taken) == 1 else taken[-1]))
    far = [other_slabs(value) for value in [*taken, *others]]

    asked = lax.all_to_all(asked, "patch", split_axis=0, concat_axis=0, tiled=True)
    asked_words = asked[:, :4].astype(jnp.int32)

    smem = pl.BlockSpec(memory_space=pltpu.SMEM)
    vmem = pl.BlockSpec(memory_space=pltpu.VMEM)
    local = pl.pallas_call(
        functools.partial(gather_kernel, 8, rows, depth),
        in_specs=[smem, smem, vmem, vmem],
        out_specs=vmem,
        out_shape=jax.ShapeDtypeStruct((patches, groups, 8, LANES), jnp.float32),
        scratch_shapes=[pltpu.VMEM((8 * rows * (depth // LANES) + rows, LANES), jnp.float32)],
        compiler_params=pltpu.CompilerParams(vmem_limit_bytes=24 * MIB),
        cost_estimate=pl.CostEstimate(flops=10**9, bytes_accessed=32 * rows * depth, transcendentals=0),
        name="donor_gather",
    )(asked_words, asked, in_hbm(elastic), in_hbm(acoustic))
    interp = lax.all_to_all(local, "patch", split_axis=0, concat_axis=0, tiled=True)
    edges = lax.all_to_all(edges, "layer", split_axis=0, concat_axis=0, tiled=True)

    near, far_operator = near_derivatives(elastic, acoustic, cont_matrix, me, slabs)
    new_el, new_ac, opened = pl.pallas_call(
        functools.partial(section_kernel, layers, rows, depth, tile),
        grid=(rows // tile,),
        in_specs=[
            smem,
            smem,
            smem,
            pl.BlockSpec((6, tile, depth), lambda i: (0, i, 0)),
            pl.BlockSpec((1, 5, tile, depth), lambda i: (0, 0, i, 0)),
            pl.BlockSpec((1, 3, tile, depth), lambda i: (0, 0, i, 0)),
            pl.BlockSpec((1, 3, tile, depth), lambda i: (0, 0, i, 0)),
            pl.BlockSpec((1, 2, tile, depth), lambda i: (0, 0, i, 0)),
            vmem,
            vmem,
            vmem,
        ],
        out_specs=[vmem, vmem, vmem],
        out_shape=[
            jax.ShapeDtypeStruct(elastic.shape, jnp.float32),
            jax.ShapeDtypeStruct(acoustic.shape, jnp.float32),
            pltpu.VMEM((rows, depth), jnp.float32),
        ],
        scratch_shapes=[pltpu.VMEM((rows, LANES), jnp.float32)],
        compiler_params=pltpu.CompilerParams(vmem_limit_bytes=32 * MIB),
        cost_estimate=pl.CostEstimate(
            flops=100 * rows * depth, bytes_accessed=112 * rows * depth, transcendentals=0
        ),
        name="near_section",
    )(
        fringe_cells,
        donor_counts,
        interp,
        near,
        in_hbm(elastic),
        in_hbm(acoustic),
        in_hbm(el_media),
        in_hbm(ac_media),
        edges,
        el_pair,
        ac_pair,
    )

    turn = jnp.zeros((8, LANES), jnp.float32)
    section = {"el": new_el, "ac": new_ac}
    media = {"el": el_media, "ac": ac_media}
    *middle, closing = pieces
    _, _, last_at, last_width, last_target, last_media, _, last_field, (last_coefficient,) = closing
    for i, (_, _, at, _, target, first_media, n_media, first_field, coefficients) in enumerate(middle):
        if i == len(middle) - 1:
            section[last_target], old, scale = prepare_last(
                section[last_target], media[last_target], last_media, last_field, last_coefficient,
                opened, last_at, last_width,
            )
        turn, section[target] = add_far(
            section[target], far_operator, far[i], at,
            media[target], first_media, n_media, first_field, coefficients, opened, turn,
        )
    section[last_target] = finish_last(
        section[last_target], far_operator, far[-1], old, scale, last_field, last_at
    )
    return section["el"], section["ac"]


def solution(mesh):
    placed = (
        P("patch", None, "line", "layer"),
        P("patch", None, "line", "layer"),
        P("patch", None, "line", "layer"),
        P("patch", None, "line", "layer"),
        P(),
        P("patch", "line", "layer", None, None),
        P("patch", "line", "layer", None, None, None),
        P("patch", "line", "layer", None, None, None),
        P("patch", "line", "layer", None),
        P("patch", "line"),
        P("patch", "line"),
    )
    return jax.shard_map(
        per_device,
        mesh=mesh,
        in_specs=placed,
        out_specs=(P("patch", None, "line", "layer"), P("patch", None, "line", "layer")),
        check_vma=False,
    )
```

```python
import functools
import math

import jax
import jax.numpy as jnp
import numpy as np
from jax import lax
from jax.experimental import pallas as pl
from jax.experimental.pallas import tpu as pltpu
from jax.sharding import PartitionSpec as P

STEP = 0.25
PENALTY = 2.0
LANES = 128
MIB = 1024 * 1024
HIGHEST = lax.Precision.HIGHEST


def in_hbm(array):
    return pltpu.with_memory_space_constraint(array, pltpu.HBM)


def derivative_row(period):
    n = np.arange(1, period)
    sign = np.where(n % 2 == 0, 1.0, -1.0)
    row = np.zeros(period)
    row[1:] = (math.pi / period) * sign / np.tan(math.pi * n / period)
    return row


def operator_tables(rows, slabs, cont):
    points = rows * slabs
    period = points + cont
    row = derivative_row(period)
    j = np.arange(rows)
    own = row[(j[:, None] - j[None, :]) % period]
    far, tail = [], []
    for me in range(slabs):
        mine = me * rows + j[:, None]
        others = np.concatenate([(me - d) % slabs * rows + j for d in range(1, slabs)])
        far.append(row[(mine - others[None, :]) % period])
        tail.append(row[(mine - points - np.arange(cont)[None, :]) % period])
    return tuple(jnp.asarray(np.asarray(table, np.float32)) for table in (own, far, tail))


def continuation_on(cont_matrix, rows, slabs, sources):
    match = cont_matrix.shape[1] // 2
    on_last = jnp.pad(cont_matrix[:, :match], ((0, 0), (rows - match, 0)))
    on_first = jnp.pad(cont_matrix[:, match:], ((0, 0), (0, rows - match)))
    return jnp.concatenate(
        [
            jnp.where(source == slabs - 1, on_last, 0.0) + jnp.where(source == 0, on_first, 0.0)
            for source in sources
        ],
        axis=1,
    )


def split(value, size):
    if size & (size - 1) == 0:
        return lax.shift_right_logical(value, size.bit_length() - 1), value & (size - 1)
    return lax.div(value, size), lax.rem(value, size)


def take_kernel(pieces, parts, elastic_ref, acoustic_ref, *refs):
    n = len(pieces)
    outs, held, in_semaphores, out_semaphores = refs[:n], refs[n : 2 * n], refs[-2], refs[-1]
    loads, stores = [], []
    for i, (name, field, at, width, row, count) in enumerate(pieces):
        source = elastic_ref if name == "el" else acoustic_ref
        for part in range(parts):
            size = count // parts
            here, there = pl.ds(part * size, size), pl.ds(row + part * size, size)
            k = i * parts + part
            loads.append(
                pltpu.make_async_copy(source.at[0, field, there, pl.ds(at, width)], held[i].at[here], in_semaphores.at[k])
            )
            stores.append(pltpu.make_async_copy(held[i].at[here], outs[i].at[here], out_semaphores.at[k]))
    for load in loads:
        load.start()
    for load, store in zip(loads, stores):
        load.wait()
        store.start()
    return stores


def take_first_kernel(field, parts, elastic_ref, out_ref, semaphores):
    rows = out_ref.shape[0] // parts
    copies = []
    for part in range(parts):
        here = pl.ds(part * rows, rows)
        copies.append(pltpu.make_async_copy(elastic_ref.at[0, field, here], out_ref.at[here], semaphores.at[part]))
        copies[-1].start()
    for copy in copies:
        copy.wait()


def take_first(elastic, field):
    rows, depth = elastic.shape[2:]
    parts = 4
    return pl.pallas_call(
        functools.partial(take_first_kernel, field, parts),
        in_specs=[pl.BlockSpec(memory_space=pl.ANY)],
        out_specs=pl.BlockSpec(memory_space=pltpu.VMEM),
        out_shape=pltpu.VMEM((rows, depth), jnp.float32),
        scratch_shapes=[pltpu.SemaphoreType.DMA((parts,))],
        compiler_params=pltpu.CompilerParams(vmem_limit_bytes=16 * MIB),
        cost_estimate=pl.CostEstimate(flops=0, bytes_accessed=8 * rows * depth, transcendentals=0),
        name="take_first",
    )(in_hbm(elastic))


def take_and_edges_kernel(
    pieces, parts, layers, after_ref, elastic_ref, acoustic_ref, cells_ref, weights_ref, *refs
):
    del after_ref
    n = len(pieces)
    edges_ref, asked_ref, tiles, edge_semaphores = refs[n : n + 4]
    n_el, n_ac = elastic_ref.shape[1], acoustic_ref.shape[1]
    rows, depth = elastic_ref.shape[2:]
    loads = []
    for end, at in enumerate((0, depth - LANES)):
        for k, (source, first, count) in enumerate(((elastic_ref, 0, n_el), (acoustic_ref, n_el, n_ac))):
            loads.append(
                pltpu.make_async_copy(
                    source.at[0, :, :, pl.ds(at, LANES)],
                    tiles.at[end, pl.ds(first, count)],
                    edge_semaphores.at[2 * end + k],
                )
            )
    for load in loads:
        load.start()
    stores = take_kernel(pieces, parts, elastic_ref, acoustic_ref, *refs[:n], *refs[n + 4 :])

    x, z = split(cells_ref[0, 0, 0], depth)
    chunk, at_lane = split(z, LANES)
    words = (chunk * ((n_el + n_ac) * rows) + x) * LANES + at_lane
    asked_ref[...] = jnp.concatenate([words.astype(jnp.float32), weights_ref[0, 0, 0]], axis=1)

    for load in loads:
        load.wait()
    lane = lax.broadcasted_iota(jnp.int32, (rows, LANES), 1)
    columns = jnp.zeros((rows, LANES), jnp.float32)
    for f in range(n_el + n_ac):
        columns = jnp.where(lane == f, tiles[0, f, :, 0:1], columns)
        columns = jnp.where(lane == 8 + f, tiles[1, f, :, LANES - 1 : LANES], columns)
    lines = columns.T
    below = lax.rem(lax.axis_index("layer") + 1, layers)
    for to in range(layers):
        edges_ref[to] = jnp.where(to == below, lines[8:16], lines[0:8])
    for store in stores:
        store.wait()


def take_pieces(elastic, acoustic, pieces, after, cells, weights, layers):
    rows = elastic.shape[2]
    anywhere = pl.BlockSpec(memory_space=pl.ANY)
    vmem = pl.BlockSpec(memory_space=pltpu.VMEM)
    out_shape = [jax.ShapeDtypeStruct((count, width), jnp.float32) for _, _, _, width, _, count in pieces]
    parts = 2
    scratch = [pltpu.VMEM((2, 8, rows, LANES), jnp.float32), pltpu.SemaphoreType.DMA((4,))]
    scratch += [pltpu.VMEM((count, width), jnp.float32) for _, _, _, width, _, count in pieces]
    scratch += [pltpu.SemaphoreType.DMA((len(pieces) * parts,))] * 2
    patches, corners, slots = cells.shape[3:]
    out_shape.append(jax.ShapeDtypeStruct((layers, 8, rows), jnp.float32))
    out_shape.append(jax.ShapeDtypeStruct((patches, 2 * corners, slots), jnp.float32))
    cost = sum(width * count for _, _, _, width, _, count in pieces)
    return pl.pallas_call(
        functools.partial(take_and_edges_kernel, pieces, parts, layers),
        in_specs=[anywhere] * 3 + [vmem] * 2,
        out_specs=[anywhere] * len(pieces) + [vmem] * 2,
        out_shape=out_shape,
        scratch_shapes=scratch,
        compiler_params=pltpu.CompilerParams(vmem_limit_bytes=24 * MIB),
        cost_estimate=pl.CostEstimate(flops=0, bytes_accessed=8 * cost, transcendentals=0),
        name="take_pieces",
    )(after, in_hbm(elastic), in_hbm(acoustic), cells, weights)


def gather_kernel(fields, rows, depth, words_ref, weights_ref, elastic_ref, acoustic_ref, out_ref, mixed):
    n_el = elastic_ref.shape[1]
    chunks = depth // LANES
    for f in range(fields):
        source = elastic_ref.at[0, f] if f < n_el else acoustic_ref.at[0, f - n_el]
        for c in range(chunks):
            mixed[pl.ds((c * fields + f) * rows, rows), :] = source[:, c * LANES : (c + 1) * LANES]
    lane = lax.broadcasted_iota(jnp.int32, (fields, LANES), 1)
    groups = out_ref.shape[1]

    def one_group(step, carry):
        patch, group = split(step, groups)

        def one_slot(r, values):
            slot = group * LANES + r
            total = None
            for s in range(4):
                start, at = split(words_ref[patch, s, slot], LANES)
                picked = mixed[pl.ds(start, fields, stride=rows), :]
                term = jnp.where(lane == at, picked * weights_ref[patch, 4 + s, slot], 0.0)
                total = term if total is None else total + term
            column = jnp.sum(total, axis=1, keepdims=True)
            return jnp.where(lane == r, column, values)

        values = lax.fori_loop(0, LANES, one_slot, jnp.zeros((fields, LANES), jnp.float32), unroll=16)
        out_ref[patch, group] = values
        return carry

    lax.fori_loop(0, out_ref.shape[0] * groups, one_group, 0)


def bf16_pair(value):
    high = value.astype(jnp.bfloat16)
    return high, (value - high.astype(jnp.float32)).astype(jnp.bfloat16)


def three_left(value):
    high, low = bf16_pair(value)
    return jnp.concatenate([high, high, low], axis=1)


def three_right(value):
    high, low = bf16_pair(value)
    return jnp.concatenate([high, low, high], axis=0)


def near_kernel(
    n_el, me_ref, own_ref, far_ref, tail_ref, own_cont_ref, far_cont_ref, elastic_ref, acoustic_ref,
    out_ref, far_operator_ref, operator,
):
    del me_ref

    @pl.when(pl.program_id(0) == 0)
    def _():
        def folded(table, cont):
            return table + jnp.dot(tail_ref[0], cont, precision=HIGHEST, preferred_element_type=jnp.float32)

        operator[...] = three_left(folded(own_ref[...], own_cont_ref[...]))
        far_operator_ref[...] = three_left(folded(far_ref[0], far_cont_ref[...]))

    value = jnp.where(pl.program_id(0) < n_el, elastic_ref[0, 0], acoustic_ref[0, 0])
    out_ref[0] = jnp.dot(operator[...], three_right(value), preferred_element_type=jnp.float32)


def near_derivatives(elastic, acoustic, cont_matrix, me, slabs):
    rows, depth = elastic.shape[2:]
    cont = cont_matrix.shape[0]
    reach = (slabs - 1) * rows
    own, far, tail = operator_tables(rows, slabs, cont)
    own_cont = continuation_on(cont_matrix, rows, slabs, [me])
    far_cont = continuation_on(cont_matrix, rows, slabs, [(me - d) % slabs for d in range(1, slabs)])
    return pl.pallas_call(
        functools.partial(near_kernel, 4),
        grid_spec=pltpu.PrefetchScalarGridSpec(
            num_scalar_prefetch=1,
            grid=(6,),
            in_specs=[
                pl.BlockSpec((rows, rows), lambda f, me: (0, 0)),
                pl.BlockSpec((1, rows, reach), lambda f, me: (me[0], 0, 0)),
                pl.BlockSpec((1, rows, cont), lambda f, me: (me[0], 0, 0)),
                pl.BlockSpec((cont, rows), lambda f, me: (0, 0)),
                pl.BlockSpec((cont, reach), lambda f, me: (0, 0)),
                pl.BlockSpec((1, 1, rows, depth), lambda f, me: (0, jnp.where(f < 3, f, 4), 0, 0)),
                pl.BlockSpec((1, 1, rows, depth), lambda f, me: (0, jnp.maximum(f - 4, 0), 0, 0)),
            ],
            out_specs=[
                pl.BlockSpec((1, rows, depth), lambda f, me: (f, 0, 0)),
                pl.BlockSpec((rows, 3 * reach), lambda f, me: (0, 0)),
            ],
            scratch_shapes=[pltpu.VMEM((rows, 3 * rows), jnp.bfloat16)],
        ),
        out_shape=[
            pltpu.HBM((6, rows, depth), jnp.float32),
            pltpu.VMEM((rows, 3 * reach), jnp.bfloat16),
        ],
        compiler_params=pltpu.CompilerParams(vmem_limit_bytes=24 * MIB),
        cost_estimate=pl.CostEstimate(
            flops=36 * rows * rows * depth, bytes_accessed=60 * rows * depth, transcendentals=0
        ),
        name="near_dx",
    )(
        me.reshape(1), in_hbm(own), in_hbm(far), in_hbm(tail), own_cont, far_cont, in_hbm(elastic), in_hbm(acoustic)
    )


def section_kernel(
    layers, rows, depth, tile,
    cells_ref, counts_ref, interp_ref,
    dx_ref, elastic_ref, acoustic_ref, el_media_ref, ac_media_ref, edges_ref, el_pair_ref, ac_pair_ref,
    new_el_ref, new_ac_ref, open_ref,
    columns,
):
    step = pl.program_id(0)
    here = pl.ds(pl.multiple_of(step * tile, tile), tile)
    lane = lax.broadcasted_iota(jnp.int32, (tile, depth), 1)
    layer = lax.axis_index("layer")
    at_top, at_bottom = layer == 0, layer == layers - 1
    from_above = edges_ref[lax.rem(layer + layers - 1, layers)]
    from_below = edges_ref[lax.rem(layer + 1, layers)]
    ocean_row = from_above[5:6]
    basin_row = from_below[1:2]

    @pl.when(step == 0)
    def _():
        pairs = jnp.concatenate([el_pair_ref[...], ac_pair_ref[...]]).astype(jnp.float32)
        lines = [
            jnp.where(at_top, 0.0, from_above),
            jnp.where(at_bottom, 0.0, from_below),
            pairs,
            jnp.zeros((LANES - 18, rows), jnp.float32),
        ]
        columns[...] = jnp.concatenate(lines).T

    halo = columns[here, :]

    def dz(value, slot):
        above = halo[:, slot : slot + 1]
        below = halo[:, 8 + slot : 9 + slot]
        following = jnp.where(lane == depth - 1, below, pltpu.roll(value, depth - 1, 1))
        previous = jnp.where(lane == 0, above, pltpu.roll(value, 1, 1))
        return (following - previous) * 0.5

    vx, vz, sxx, szz, sxz = [elastic_ref[0, f] for f in range(5)]
    p, ovx, ovz = [acoustic_ref[0, f] for f in range(3)]
    buoyancy = el_media_ref[0, 0]
    lame = el_media_ref[0, 1]
    shear = el_media_ref[0, 2]
    stiffness = lame + 2.0 * shear
    bulk = ac_media_ref[0, 0]
    ocean_buoyancy = ac_media_ref[0, 1]

    dx_vx = dx_ref[0]
    dz_vz = dz(vz, 1)
    new_el_ref[0, 0, here, :] = vx + STEP * (buoyancy * (dx_ref[2] + dz(sxz, 4)))
    new_el_ref[0, 1, here, :] = vz + STEP * (buoyancy * (dx_ref[3] + dz(szz, 3)))
    new_el_ref[0, 2, here, :] = sxx + STEP * (stiffness * dx_vx + lame * dz_vz)
    choose = lax.broadcasted_iota(jnp.int32, (tile, rows), 1).astype(jnp.float32)
    pressure = jnp.sum(jnp.where(halo[:, 16:17] == choose, ocean_row, 0.0), axis=1, keepdims=True)
    velocity = jnp.sum(jnp.where(halo[:, 17:18] == choose, basin_row, 0.0), axis=1, keepdims=True)
    rate_szz = lame * dx_vx + stiffness * dz_vz
    rate_szz = rate_szz + jnp.where((lane == 0) & at_top, PENALTY * (-pressure - szz), 0.0)
    new_el_ref[0, 3, here, :] = szz + STEP * rate_szz
    new_el_ref[0, 4, here, :] = sxz + STEP * (shear * (dz(vx, 0) + dx_ref[1]))
    new_ac_ref[0, 0, here, :] = p - STEP * (bulk * (dx_ref[5] + dz(ovz, 7)))
    new_ac_ref[0, 1, here, :] = ovx - STEP * (ocean_buoyancy * dx_ref[4])
    rate_ovz = -ocean_buoyancy * dz(p, 5)
    rate_ovz = rate_ovz + jnp.where((lane == depth - 1) & at_bottom, PENALTY * (velocity - ovz), 0.0)
    new_ac_ref[0, 2, here, :] = ovz + STEP * rate_ovz
    open_ref[here, :] = jnp.ones((tile, depth), jnp.float32)

    @pl.when(step == pl.num_programs(0) - 1)
    def _():
        place = lax.broadcasted_iota(jnp.int32, (8, LANES), 0) * LANES
        place = place + lax.broadcasted_iota(jnp.int32, (8, LANES), 1)
        n_el = new_el_ref.shape[1]

        def one_patch(q, carry):
            def one_slot(r, inner):
                x, z = split(cells_ref[0, 0, 0, q, r], depth)
                (high, row), (low, at) = split(x, 8), split(z, LANES)
                at_row = pl.ds(pl.multiple_of(high * 8, 8), 8)
                at_lane = pl.ds(pl.multiple_of(low * LANES, LANES), LANES)
                hit = place == row * LANES + at
                group, within = split(r, LANES)
                for f in range(8):
                    target = new_el_ref.at[0, f] if f < n_el else new_ac_ref.at[0, f - n_el]
                    target[at_row, at_lane] = jnp.where(hit, interp_ref[q, group, f, within], target[at_row, at_lane])
                open_ref[at_row, at_lane] = jnp.where(hit, 0.0, open_ref[at_row, at_lane])
                return inner

            return lax.fori_loop(0, counts_ref[0, 0, 0, q], one_slot, carry)

        lax.fori_loop(0, counts_ref.shape[3], one_patch, 0)


def far_kernel(coefficients, turn_ref, d_ref, far_ref, media_ref, open_ref, base_ref, next_ref, out_ref):
    del turn_ref, next_ref
    far = jnp.dot(d_ref[...], three_right(far_ref[...]), preferred_element_type=jnp.float32)
    media = [media_ref[0, i] for i in range(media_ref.shape[1])]
    is_open = open_ref[...] > 0.5
    for i, coefficient in enumerate(coefficients):
        old = base_ref[0, i]
        out_ref[0, i] = jnp.where(is_open, old + (STEP * coefficient(*media)) * far, old)


def add_far(base, operator, far, at, media, first_media, n_media, first_field, coefficients, opened, turn):
    rows, reach = operator.shape[0], far.shape[0]
    width = far.shape[1]
    tile = math.gcd(math.gcd(width, at), 2 * LANES)
    n_out = len(coefficients)
    shift = at // tile
    return pl.pallas_call(
        functools.partial(far_kernel, coefficients),
        grid=(width // tile,),
        in_specs=[
            pl.BlockSpec(memory_space=pl.ANY),
            pl.BlockSpec((rows, 3 * reach), lambda i: (0, 0)),
            pl.BlockSpec((reach, tile), lambda i: (0, i)),
            pl.BlockSpec((1, n_media, rows, tile), lambda i: (0, first_media // n_media, 0, i + shift)),
            pl.BlockSpec((rows, tile), lambda i: (0, i + shift)),
            pl.BlockSpec((1, n_out, rows, tile), lambda i: (0, first_field // n_out, 0, i + shift)),
        ],
        out_specs=[
            pl.BlockSpec(memory_space=pl.ANY),
            pl.BlockSpec((1, n_out, rows, tile), lambda i: (0, first_field // n_out, 0, i + shift)),
        ],
        out_shape=[
            jax.ShapeDtypeStruct(turn.shape, turn.dtype),
            jax.ShapeDtypeStruct(base.shape, base.dtype),
        ],
        input_output_aliases={0: 0, 5: 1},
        compiler_params=pltpu.CompilerParams(vmem_limit_bytes=16 * MIB),
        cost_estimate=pl.CostEstimate(
            flops=6 * rows * reach * width,
            bytes_accessed=4 * rows * width * (3 + n_media + n_out),
            transcendentals=0,
        ),
        name="add_far",
    )(turn, operator, far, in_hbm(media), opened, base)


def prepare_kernel(coefficient, field, at, base_ref, media_ref, open_ref, same_ref, old_ref, scale_ref, semaphore):
    del same_ref
    load = pltpu.make_async_copy(base_ref.at[0, field, :, pl.ds(at, old_ref.shape[1])], old_ref, semaphore)
    load.start()
    scale_ref[...] = jnp.where(open_ref[...] > 0.5, STEP * coefficient(media_ref[0, 0]), 0.0)
    load.wait()


def prepare_last(base, media, first_media, field, coefficient, opened, at, width):
    rows = opened.shape[0]
    anywhere = pl.BlockSpec(memory_space=pl.ANY)
    vmem = pl.BlockSpec(memory_space=pltpu.VMEM)
    return pl.pallas_call(
        functools.partial(prepare_kernel, coefficient, field, at),
        grid=(1,),
        in_specs=[
            anywhere,
            pl.BlockSpec((1, 1, rows, width), lambda i: (0, first_media, 0, at // width)),
            pl.BlockSpec((rows, width), lambda i: (0, at // width)),
        ],
        out_specs=[anywhere, vmem, vmem],
        out_shape=[
            jax.ShapeDtypeStruct(base.shape, base.dtype),
            pltpu.VMEM((rows, width), jnp.float32),
            pltpu.VMEM((rows, width), jnp.float32),
        ],
        scratch_shapes=[pltpu.SemaphoreType.DMA],
        input_output_aliases={0: 0},
        compiler_params=pltpu.CompilerParams(vmem_limit_bytes=16 * MIB),
        cost_estimate=pl.CostEstimate(flops=rows * width, bytes_accessed=20 * rows * width, transcendentals=0),
        name="prepare_last",
    )(base, in_hbm(media), opened)


def operator_part(d_ref, here, first, count):
    reach = d_ref.shape[1] // 3
    if count == reach:
        return d_ref[here, :]
    return jnp.concatenate([d_ref[here, pl.ds(k * reach + first, count)] for k in range(3)], axis=1)


def fold_kernel(first, turn_ref, d_ref, far_ref, old_ref, scale_ref, out_ref):
    del turn_ref
    left = operator_part(d_ref, slice(None), first, far_ref.shape[0])
    far = jnp.dot(left, three_right(far_ref[...]), preferred_element_type=jnp.float32)
    out_ref[...] = old_ref[...] + scale_ref[...] * far


def fold_part(operator, far, old, scale, first, turn):
    vmem = pl.BlockSpec(memory_space=pltpu.VMEM)
    return pl.pallas_call(
        functools.partial(fold_kernel, first),
        in_specs=[pl.BlockSpec(memory_space=pl.ANY)] + [vmem] * 4,
        out_specs=vmem,
        out_shape=pltpu.VMEM(old.shape, jnp.float32),
        compiler_params=pltpu.CompilerParams(vmem_limit_bytes=16 * MIB),
        cost_estimate=pl.CostEstimate(
            flops=6 * old.size * far.shape[0], bytes_accessed=16 * old.size, transcendentals=0
        ),
        name="fold_part",
    )(turn, operator, far, old, scale)


def finish_kernel(field, at, first, parts, d_ref, far_ref, old_ref, scale_ref, base_ref, out_ref, held, semaphores):
    del base_ref
    rows, width = old_ref.shape[0] // parts, old_ref.shape[1]
    far_field = three_right(far_ref[...])
    stores = []
    for part in range(parts):
        here = pl.ds(part * rows, rows)
        left = operator_part(d_ref, here, first, far_ref.shape[0])
        far = jnp.dot(left, far_field, preferred_element_type=jnp.float32)
        held[here, :] = old_ref[here, :] + scale_ref[here, :] * far
        stores.append(
            pltpu.make_async_copy(
                held.at[here], out_ref.at[0, field, here, pl.ds(at, width)], semaphores.at[part]
            )
        )
        stores[-1].start()
    for store in stores:
        store.wait()


def finish_last(base, operator, far, old, scale, field, at, first):
    rows, width = old.shape
    parts = 2
    anywhere = pl.BlockSpec(memory_space=pl.ANY)
    vmem = pl.BlockSpec(memory_space=pltpu.VMEM)
    return pl.pallas_call(
        functools.partial(finish_kernel, field, at, first, parts),
        in_specs=[vmem] * 4 + [anywhere],
        out_specs=anywhere,
        out_shape=jax.ShapeDtypeStruct(base.shape, base.dtype),
        scratch_shapes=[pltpu.VMEM((rows, width), jnp.float32), pltpu.SemaphoreType.DMA((parts,))],
        input_output_aliases={4: 0},
        compiler_params=pltpu.CompilerParams(vmem_limit_bytes=16 * MIB),
        cost_estimate=pl.CostEstimate(
            flops=6 * rows * far.shape[0] * width, bytes_accessed=4 * rows * width, transcendentals=0
        ),
        name="finish_last",
    )(operator, far, old, scale, base)


def per_device(
    elastic,
    acoustic,
    el_media,
    ac_media,
    cont_matrix,
    fringe_cells,
    donor_cells,
    donor_weights,
    donor_counts,
    el_pair,
    ac_pair,
):
    rows, depth = elastic.shape[2], elastic.shape[3]
    slabs = lax.axis_size("line")
    layers = lax.axis_size("layer")
    patches = lax.axis_size("patch")
    slots = fringe_cells.shape[-1]
    groups = slots // LANES
    me = lax.axis_index("line")
    layer = lax.axis_index("layer")
    tile = min(64, rows)

    def other_slabs(value):
        parts = [
            lax.ppermute(value, "line", [(i, (i + distance) % slabs) for i in range(slabs)])
            for distance in range(1, slabs)
        ]
        return parts[0] if slabs == 2 else jnp.concatenate(parts, axis=0)

    half, quarter = depth // 2, depth // 4
    pieces = [
        ("el", 0, 0, depth, "el", 0, 3, 2, (lambda b, l, m: l + 2.0 * m, lambda b, l, m: l)),
        ("ac", 0, 0, depth, "ac", 1, 1, 1, (lambda b: -b,)),
        ("ac", 1, 0, depth, "ac", 0, 1, 0, (lambda k: -k,)),
        ("el", 1, 0, depth, "el", 2, 1, 4, (lambda m: m,)),
        ("el", 2, 0, depth, "el", 0, 1, 0, (lambda b: b,)),
        ("el", 4, 0, half, "el", 0, 1, 1, (lambda b: b,)),
        ("el", 4, half, quarter, "el", 0, 1, 1, (lambda b: b,)),
        ("el", 4, half + quarter, quarter, "el", 0, 1, 1, (lambda b: b,)),
    ]
    travelling = [piece[:4] + (0, rows) for piece in pieces]
    late = rows // 4
    if slabs == 2 and late % LANES == 0:
        last = travelling.pop()[:4]
        travelling += [last + (0, rows - late), last + (rows - late, late)]
    first = take_first(elastic, travelling[0][1])
    *others, edges, asked = take_pieces(
        elastic, acoustic, travelling[1:], first, donor_cells, donor_weights, layers
    )
    far = [other_slabs(value) for value in [first, *others]]

    asked = lax.all_to_all(asked, "patch", split_axis=0, concat_axis=0, tiled=True)
    asked_words = asked[:, :4].astype(jnp.int32)

    smem = pl.BlockSpec(memory_space=pltpu.SMEM)
    vmem = pl.BlockSpec(memory_space=pltpu.VMEM)
    local = pl.pallas_call(
        functools.partial(gather_kernel, 8, rows, depth),
        in_specs=[smem, smem, vmem, vmem],
        out_specs=vmem,
        out_shape=jax.ShapeDtypeStruct((patches, groups, 8, LANES), jnp.float32),
        scratch_shapes=[pltpu.VMEM((8 * rows * (depth // LANES) + rows, LANES), jnp.float32)],
        compiler_params=pltpu.CompilerParams(vmem_limit_bytes=24 * MIB),
        cost_estimate=pl.CostEstimate(flops=10**9, bytes_accessed=32 * rows * depth, transcendentals=0),
        name="donor_gather",
    )(asked_words, asked, in_hbm(elastic), in_hbm(acoustic))
    interp = lax.all_to_all(local, "patch", split_axis=0, concat_axis=0, tiled=True)
    edges = lax.all_to_all(edges, "layer", split_axis=0, concat_axis=0, tiled=True)

    near, far_operator = near_derivatives(elastic, acoustic, cont_matrix, me, slabs)
    new_el, new_ac, opened = pl.pallas_call(
        functools.partial(section_kernel, layers, rows, depth, tile),
        grid=(rows // tile,),
        in_specs=[
            smem,
            smem,
            smem,
            pl.BlockSpec((6, tile, depth), lambda i: (0, i, 0)),
            pl.BlockSpec((1, 5, tile, depth), lambda i: (0, 0, i, 0)),
            pl.BlockSpec((1, 3, tile, depth), lambda i: (0, 0, i, 0)),
            pl.BlockSpec((1, 3, tile, depth), lambda i: (0, 0, i, 0)),
            pl.BlockSpec((1, 2, tile, depth), lambda i: (0, 0, i, 0)),
            vmem,
            vmem,
            vmem,
        ],
        out_specs=[vmem, vmem, vmem],
        out_shape=[
            jax.ShapeDtypeStruct(elastic.shape, jnp.float32),
            jax.ShapeDtypeStruct(acoustic.shape, jnp.float32),
            pltpu.VMEM((rows, depth), jnp.float32),
        ],
        scratch_shapes=[pltpu.VMEM((rows, LANES), jnp.float32)],
        compiler_params=pltpu.CompilerParams(vmem_limit_bytes=32 * MIB),
        cost_estimate=pl.CostEstimate(
            flops=100 * rows * depth, bytes_accessed=112 * rows * depth, transcendentals=0
        ),
        name="near_section",
    )(
        fringe_cells,
        donor_counts,
        interp,
        near,
        in_hbm(elastic),
        in_hbm(acoustic),
        in_hbm(el_media),
        in_hbm(ac_media),
        edges,
        el_pair,
        ac_pair,
    )

    turn = jnp.zeros((8, LANES), jnp.float32)
    section = {"el": new_el, "ac": new_ac}
    media = {"el": el_media, "ac": ac_media}
    *middle, closing = pieces
    _, _, last_at, last_width, last_target, last_media, _, last_field, (last_coefficient,) = closing
    for i, (_, _, at, _, target, first_media, n_media, first_field, coefficients) in enumerate(middle):
        if i == len(middle) - 1:
            section[last_target], old, scale = prepare_last(
                section[last_target], media[last_target], last_media, last_field, last_coefficient,
                opened, last_at, last_width,
            )
        turn, section[target] = add_far(
            section[target], far_operator, far[i], at,
            media[target], first_media, n_media, first_field, coefficients, opened, turn,
        )
    *folded, closing_far = far[len(middle) :]
    first_row = 0
    for part in folded:
        old = fold_part(far_operator, part, old, scale, first_row, turn)
        first_row += part.shape[0]
    section[last_target] = finish_last(
        section[last_target], far_operator, closing_far, old, scale, last_field, last_at, first_row
    )
    return section["el"], section["ac"]


def solution(mesh):
    placed = (
        P("patch", None, "line", "layer"),
        P("patch", None, "line", "layer"),
        P("patch", None, "line", "layer"),
        P("patch", None, "line", "layer"),
        P(),
        P("patch", "line", "layer", None, None),
        P("patch", "line", "layer", None, None, None),
        P("patch", "line", "layer", None, None, None),
        P("patch", "line", "layer", None),
        P("patch", "line"),
        P("patch", "line"),
    )
    return jax.shard_map(
        per_device,
        mesh=mesh,
        in_specs=placed,
        out_specs=(P("patch", None, "line", "layer"), P("patch", None, "line", "layer")),
        check_vma=False,
    )
```
